256 devices in a mesh: seq: 32 (over y, x, z_hi), expert: 8 (over z_lo, core).
Axes of the slice: x: 4, y: 4, z: 8 (z_hi: 2, z_lo: 4; z = z_hi * 4 + z_lo), core: 2. Of those that a mesh axis runs over, the one named last changes fastest.
Arguments:
- frames: bfloat16 [8, 4096, 768], P('expert', 'seq'), may hold values from -6 to 6
- cotangent: bfloat16 [8, 4096, 768], P('expert', 'seq'), may hold values from -6 to 6
- routes: int32 [8, 4096, 2], P('expert', 'seq'), may hold values from 0 to 31, all different within a row; in each aligned block of 128 rows (0 to 127, 128 to 255, ..., all dimensions but the last counted through in order) at most 10 rows name the same one
- stream_lengths: int32 [8, 3], P('expert'), may hold values from 1 to 2048, 4096 in all within a row
- conv_weight: float32 [32, 768], replicated, may hold values from -1 to 1
- router_weight: bfloat16 [768, 32], replicated, may hold values from -0.21875 to 0.21875
- gate_weight: bfloat16 [32, 768, 3072], P('seq', None, 'expert'), may hold values from -0.21875 to 0.21875
- up_weight: bfloat16 [32, 768, 3072], P('seq', None, 'expert'), may hold values from -0.21875 to 0.21875
- down_weight: bfloat16 [32, 3072, 768], P('seq', 'expert'), may hold values from -0.109375 to 0.109375
Outputs:
- block_out: bfloat16 [8, 4096, 768], P('expert', 'seq')
- frame_grad: bfloat16 [8, 4096, 768], P('expert', 'seq')
- conv_grads: float32 [32, 768], replicated
- router_grads: float32 [768, 32], replicated
- gate_grads: float32 [32, 768, 3072], P('seq', None, 'expert')
- up_grads: float32 [32, 768, 3072], P('seq', None, 'expert')
- down_grads: float32 [32, 3072, 768], P('seq', 'expert')
The draws below stay inside these ranges and needn't reach their ends.
Inputs may be any that keep to these rules, and one draw needn't show every extreme that they name: The two routes of a frame differ. Among the frames of one device (aligned blocks of 128 frames of a chain), no expert is named by more than 10 routes, a bound that some block reaches. `stream_lengths`: each chain's lengths sum to 4096; the largest is half of 4096.
All inputs are finite; a program needn't handle non-finite values.
Results may differ from the reference program's by a relative error of at most 0.0091.
Values may be sent and summed in bfloat16 or wider, within the bound.
No kernel may reach another device: no remote copies, remote signals or barrier semaphores. Data moves between devices by JAX's collectives and lax.ppermute only.
A program may use at most 128 MiB of HBM per device.

```python
import math
import jax
import jax.numpy as jnp
import numpy as np
from jax import lax

D = 768
F = 3072
KERNEL = 32
NSTREAM = 3
FR_DEV = 128
EXPERTS = 32
CHAINS = 8
FRAMES = 4096
CAP = 10
HBLK = 384
N_SEQ = 32


def block_levels(key, extent, shards, smallest, top_value):
    level, own = 1.0, jax.random.fold_in(key, 6)
    for dim, blocks in shards:
        steps = jnp.exp(jax.random.uniform(jax.random.fold_in(own, dim), (blocks,), jnp.float32, smallest / len(shards), top_value / len(shards)))
        level = level * jnp.repeat(steps, extent[dim] // blocks).reshape([-1 if axis == dim else 1 for axis in range(len(extent))])
    return level


def profile(amount, total, reach, skew):
    loads = [(1 << 20) // math.isqrt(standing ** skew) + 1 for standing in range(2, amount + 1)]
    surplus, holding = total - reach - (amount - 1), [1] * (amount - 1)
    while surplus > 0:
        movable = [i for i in range(amount - 1) if holding[i] < reach]
        whole, left = sum([loads[i] for i in movable]), surplus
        for i in movable:
            more = min(reach - holding[i], max(1, left * loads[i] // whole), surplus)
            holding[i] = holding[i] + more
            surplus = surplus - more
    return np.array([reach] + holding)


def uneven_parts(stream_key, amount, total, bound, skew):
    if amount == 2:
        one = jax.random.randint(stream_key, (), max(1, total - bound), min(bound, total - 1) + 1)
        return jnp.stack([one, total - one])
    tallies = jnp.asarray(profile(amount, total, bound, skew), jnp.int32)
    twos = (amount - 1) // 2
    donor, sink = tallies[1:1 + 2 * twos:2], tallies[2:2 + 2 * twos:2]
    room = jnp.minimum(donor - 1, bound - sink)
    passed = jax.random.randint(jax.random.fold_in(stream_key, 1), (twos,), 0, 1 << 20) % (room + 1)
    tallies = tallies.at[1:1 + 2 * twos:2].set(donor - passed).at[2:2 + 2 * twos:2].set(sink + passed)
    return tallies[jax.random.permutation(jax.random.fold_in(stream_key, 2), amount)]


def routed_block(stream_key, own, number, rows, amount, top, reach, slope):
    order = jax.random.permutation(stream_key, amount)
    crowded, usual = shares(amount, rows * top, reach, slope, True), shares(amount, rows * top, reach, slope, False)
    places = jnp.arange(amount)

    def named(sizes, offset_by):
        used = int((sizes > 0).sum())
        fixed = max(1, used // 4)
        passed = fixed + (places - fixed + offset_by * (used - fixed)) % max(1, amount - fixed)
        return jnp.zeros((amount,), jnp.int32).at[order[jnp.where(places < fixed, places, passed)]].set(jnp.asarray(sizes, jnp.int32))

    sizes = jnp.where(number % 4 == 0, named(crowded, number // 4), named(usual, number - number // 4 - 1))
    mixed = jax.random.permutation(jax.random.fold_in(own, 3), amount)
    giver, receiver = mixed[0:amount // 2 * 2:2], mixed[1:amount // 2 * 2:2]
    room = jnp.minimum(sizes[giver] - 1, reach - sizes[receiver]) // 2
    room = jnp.where((giver == order[0]) | (receiver == order[0]) | (sizes[receiver] == 0), 0, jnp.maximum(room, 0))
    passed = jax.random.randint(jax.random.fold_in(own, 4), (amount // 2,), 0, 1 << 20) % (room + 1)
    sizes = sizes.at[giver].add(-passed).at[receiver].add(passed)
    items = jnp.searchsorted(jnp.cumsum(sizes), jnp.arange(rows * top), side="right").astype(jnp.int32)
    grid = items.reshape(top, rows).T
    grid = grid[jax.random.permutation(jax.random.fold_in(own, 1), rows)]
    offset_by = jax.random.randint(jax.random.fold_in(own, 2), (rows, 1), 0, top)
    return jnp.take_along_axis(grid, (jnp.arange(top)[None, :] + offset_by) % top, axis=1)


def shares(count, total, limit, slope, full):
    weights = [(1 << 20) // math.isqrt(standing ** slope) + 1 for standing in range(1, count + 1)]
    largest = limit if full else min(limit, max(-(-total // count), total * weights[0] // sum(weights)))
    least = 1 if total - largest >= count - 1 else 0
    given, surplus = [largest] + [least] * (count - 1), total - largest - least * (count - 1)
    while surplus > 0:
        candidates = [i for i in range(1, count) if given[i] < largest] or [i for i in range(1, count) if given[i] < limit]
        mass, remaining = sum([weights[i] for i in candidates]), surplus
        for i in candidates:
            extra = min(limit - given[i], max(1, remaining * weights[i] // mass), surplus)
            given[i] = given[i] + extra
            surplus = surplus - extra
    return np.array(given)


def bell_draw(rng, extent, spread, most, pieces=(), kind=jnp.bfloat16):
    values = spread * jax.random.normal(rng, extent, jnp.float32)
    if pieces:
        values = values * block_levels(rng, extent, pieces, -0.22, 0.18)
    return jnp.clip(values, -most, most).astype(kind)


def setup_inputs(seed: int = 0) -> dict:
    key_list = jax.random.split(jax.random.key(seed), 10)
    frames = bell_draw(key_list[0], (CHAINS, FRAMES, D), 1.0, 6.0, ((0, 8), (1, 32)))
    cotangent = bell_draw(key_list[1], (CHAINS, FRAMES, D), 1.0, 6.0, ((0, 8), (1, 32)))
    routes_keys = jax.random.split(jax.random.fold_in(key_list[2], 1), CHAINS * FRAMES // FR_DEV)
    routes_turns = jax.random.permutation(jax.random.fold_in(key_list[2], 3), CHAINS * FRAMES // FR_DEV)
    routes = jax.vmap(lambda own, number: routed_block(jax.random.fold_in(key_list[2], 2), own, number, FR_DEV, EXPERTS, 2, CAP, 2))(routes_keys, routes_turns).reshape((CHAINS, FRAMES, 2))
    stream_lengths = jax.vmap(lambda own: uneven_parts(own, NSTREAM, FRAMES, FRAMES // 2, 2))(jax.random.split(key_list[3], CHAINS)).reshape((CHAINS, NSTREAM)).astype(jnp.int32)
    conv_weight = bell_draw(key_list[4], (KERNEL, D), KERNEL ** -0.5, 1.0, (), jnp.float32)
    router_weight = bell_draw(key_list[5], (D, EXPERTS), D ** -0.5, 0.21875)
    gate_weight = bell_draw(key_list[6], (EXPERTS, D, F), D ** -0.5, 0.21875, ((0, 32), (2, 8)))
    up_weight = bell_draw(key_list[7], (EXPERTS, D, F), D ** -0.5, 0.21875, ((0, 32), (2, 8)))
    down_weight = bell_draw(key_list[8], (EXPERTS, F, D), F ** -0.5, 0.109375, ((0, 32), (1, 8)))
    return {"frames": frames, "cotangent": cotangent, "routes": routes, "stream_lengths": stream_lengths, "conv_weight": conv_weight, "router_weight": router_weight, "gate_weight": gate_weight, "up_weight": up_weight, "down_weight": down_weight}


def reference(frames, cotangent, routes, stream_lengths, conv_weight, router_weight, gate_weight, up_weight, down_weight):
    chain_count = frames.shape[0]
    frame_count = frames.shape[1]
    model_width = frames.shape[2]
    half_kernel = KERNEL // 2
    block_count = F // HBLK
    positions = jnp.arange(frame_count, dtype=jnp.int32)
    bounds = jnp.cumsum(stream_lengths, axis=1).astype(jnp.int32)
    stream_of = jnp.sum((positions[None, :, None] >= bounds[:, None, :]).astype(jnp.int32), axis=2).astype(jnp.int32)
    stream_pad = jnp.pad(stream_of, ((0, 0), (half_kernel, half_kernel)), constant_values=-1)
    inputs = frames.astype(jnp.float32)
    frame_pad = jnp.pad(inputs, ((0, 0), (half_kernel, half_kernel), (0, 0)))
    conv_sum = jnp.zeros(inputs.shape, jnp.float32)
    for offset in range(KERNEL):
        same_fwd = (stream_pad[:, offset:offset + frame_count] == stream_of).astype(jnp.float32)[:, :, None]
        conv_sum = conv_sum + conv_weight[offset] * frame_pad[:, offset:offset + frame_count] * same_fwd
    conv_out = (inputs + conv_sum).astype(jnp.bfloat16)
    flat_conv = conv_out.reshape(-1, model_width)
    scores = jnp.dot(flat_conv, router_weight, preferred_element_type=jnp.float32)
    labels = jnp.arange(EXPERTS, dtype=jnp.int32)
    flat_routes = routes.reshape(-1, 2).astype(jnp.int32)
    route_masks = [(flat_routes[:, route_slot:route_slot + 1] == labels[None, :]).astype(jnp.float32) for route_slot in range(2)]
    gate_values = [jax.nn.sigmoid(jnp.sum(scores * mask_table, axis=1)) for mask_table in route_masks]
    grad_rows = cotangent.reshape(-1, model_width).astype(jnp.float32)
    slot_grads = jnp.stack([(gate_value[:, None] * grad_rows).astype(jnp.bfloat16) for gate_value in gate_values], axis=1).reshape(-1, model_width)
    chosen = flat_routes.reshape(-1)
    member = (chosen[:, None] == labels[None, :]).astype(jnp.int32)
    slot_rank = jnp.sum((jnp.cumsum(member, axis=0) - member) * member, axis=1).astype(jnp.int32)
    most_rows = chain_count * N_SEQ * CAP
    target = (chosen * most_rows + slot_rank).astype(jnp.int32)
    total_slots = chosen.shape[0]
    slot_table = jnp.full((EXPERTS * most_rows,), total_slots, jnp.int32).at[target].set(jnp.arange(total_slots, dtype=jnp.int32)).reshape(EXPERTS, most_rows)
    blank_row = jnp.zeros((1, model_width), jnp.bfloat16)
    slot_inputs = jnp.concatenate([jnp.repeat(flat_conv, 2, axis=0), blank_row], axis=0)
    slot_grads_pad = jnp.concatenate([slot_grads, blank_row], axis=0)

    def expert_pass(packed):
        index, row_ids = packed
        owner_inputs = slot_inputs[row_ids]
        owner_grads = slot_grads_pad[row_ids]
        gate_block = gate_weight[index]
        up_block = up_weight[index]
        down_block = down_weight[index]
        row_total = owner_inputs.shape[0]
        gate_proj = jnp.dot(owner_inputs, gate_block, preferred_element_type=jnp.float32)
        up_proj = jnp.dot(owner_inputs, up_block, preferred_element_type=jnp.float32)
        gate_sigmoid = jax.nn.sigmoid(gate_proj)
        active = gate_proj * gate_sigmoid
        hidden = (active * up_proj).astype(jnp.bfloat16)
        hidden_blocks = hidden.reshape(row_total, block_count, HBLK).astype(jnp.float32)
        down_blocks = down_block.reshape(block_count, HBLK, model_width).astype(jnp.float32)
        partial_value = jnp.einsum("mbh,bhd->bmd", hidden_blocks, down_blocks)
        partial_half = lax.optimization_barrier(partial_value.astype(jnp.bfloat16))
        expert_out = jnp.sum(partial_half.astype(jnp.float32), axis=0).astype(jnp.bfloat16)
        back_hidden = jnp.dot(owner_grads, down_block.T, preferred_element_type=jnp.float32)
        gate_back = (back_hidden * up_proj * (gate_sigmoid * (1.0 + gate_proj * (1.0 - gate_sigmoid)))).astype(jnp.bfloat16)
        up_back = (back_hidden * active).astype(jnp.bfloat16)
        gate_blocks = gate_block.reshape(model_width, block_count, HBLK).astype(jnp.float32)
        up_blocks = up_block.reshape(model_width, block_count, HBLK).astype(jnp.float32)
        partial_back = jnp.einsum("mbh,dbh->bmd", gate_back.reshape(row_total, block_count, HBLK).astype(jnp.float32), gate_blocks)
        partial_back = partial_back + jnp.einsum("mbh,dbh->bmd", up_back.reshape(row_total, block_count, HBLK).astype(jnp.float32), up_blocks)
        back_half = lax.optimization_barrier(partial_back.astype(jnp.bfloat16))
        expert_back = jnp.sum(back_half.astype(jnp.float32), axis=0).astype(jnp.bfloat16)
        grad_gate = jnp.dot(owner_inputs.T, gate_back, preferred_element_type=jnp.float32)
        grad_up = jnp.dot(owner_inputs.T, up_back, preferred_element_type=jnp.float32)
        grad_down = jnp.dot(hidden.T, owner_grads, preferred_element_type=jnp.float32)
        return expert_out, expert_back, grad_gate, grad_up, grad_down

    all_out, all_back, gate_grads, up_grads, down_grads = lax.map(expert_pass, (jnp.arange(EXPERTS, dtype=jnp.int32), slot_table))
    flat_out = all_out.reshape(-1, model_width)[target].reshape(-1, 2, model_width).astype(jnp.float32)
    flat_back = all_back.reshape(-1, model_width)[target].reshape(-1, 2, model_width).astype(jnp.float32)
    conv_rows = flat_conv.astype(jnp.float32)
    block_out = conv_rows + gate_values[0][:, None] * flat_out[:, 0] + gate_values[1][:, None] * flat_out[:, 1]
    logit_grads = [jnp.sum(grad_rows * flat_out[:, route_slot], axis=1) * gate_values[route_slot] * (1.0 - gate_values[route_slot]) for route_slot in range(2)]
    logit_table = logit_grads[0][:, None] * route_masks[0] + logit_grads[1][:, None] * route_masks[1]
    conv_grad = grad_rows + flat_back[:, 0] + flat_back[:, 1] + jnp.dot(logit_table, router_weight.astype(jnp.float32).T, precision=lax.Precision.HIGHEST)
    router_grads = jnp.dot(conv_rows.T, logit_table, precision=lax.Precision.HIGHEST)
    grad_half = conv_grad.astype(jnp.bfloat16).astype(jnp.float32).reshape(chain_count, frame_count, model_width)
    grad_pad = jnp.pad(grad_half, ((0, 0), (half_kernel, half_kernel), (0, 0)))
    back_sum = jnp.zeros(inputs.shape, jnp.float32)
    tap_grads = []
    for offset in range(KERNEL):
        same_fwd = (stream_pad[:, offset:offset + frame_count] == stream_of).astype(jnp.float32)[:, :, None]
        tap_grads.append(jnp.sum(grad_half * frame_pad[:, offset:offset + frame_count] * same_fwd, axis=(0, 1)))
        begin_at = 2 * half_kernel - offset
        same_back = (stream_pad[:, begin_at:begin_at + frame_count] == stream_of).astype(jnp.float32)[:, :, None]
        back_sum = back_sum + conv_weight[offset] * grad_pad[:, begin_at:begin_at + frame_count] * same_back
    frame_grad = (grad_half + back_sum).astype(jnp.bfloat16)
    out_frames = block_out.astype(jnp.bfloat16).reshape(chain_count, frame_count, model_width)
    return (out_frames, frame_grad, jnp.stack(tap_grads), router_grads, gate_grads, up_grads, down_grads)
```

```python
import jax
import jax.numpy as jnp
from jax import lax
from jax.sharding import PartitionSpec as P

BF = jnp.bfloat16
F32 = jnp.float32


def flip(value, axis, bit):
    count = lax.axis_size(axis)
    return lax.ppermute(value, axis, [(i, i ^ bit) for i in range(count)])


def ring_up(value):
    count = lax.axis_size("expert")
    return lax.ppermute(value, "expert", [(i, (i + 2) % count) for i in range(count)])


def halos(block, width):
    count = lax.axis_size("seq")
    forward = [(i, i + 1) for i in range(count - 1)]
    backward = [(i + 1, i) for i in range(count - 1)]
    low = lax.ppermute(block[block.shape[0] - width :], "seq", forward)
    high = lax.ppermute(block[:width], "seq", backward)
    return jnp.concatenate([low, block, high], axis=0)


def dot(a, b, dims=((1,), (0,))):
    return lax.dot_general(a, b, (dims, ((), ())), preferred_element_type=F32)


def expert_chunk(rows, gate_block, up_block, down_block, router_column):
    width = gate_block.shape[0]
    x = rows[:, :width]
    c = rows[:, width:]
    logit = jnp.sum(x.astype(F32) * router_column[None, :], axis=1, keepdims=True)
    gate = jax.nn.sigmoid(logit)
    gate_proj = dot(x, gate_block)
    up_proj = dot(x, up_block)
    base_back = dot(c, down_block, ((1,), (1,)))
    sig = jax.nn.sigmoid(gate_proj)
    active = gate_proj * sig
    hidden = active * up_proj
    hidden_half = hidden.astype(BF)
    logit_grad = jnp.sum(hidden * base_back, axis=1, keepdims=True) * (gate * (1.0 - gate))
    back_hidden = base_back * gate
    gate_back = (back_hidden * up_proj * (sig * (1.0 + gate_proj * (1.0 - sig)))).astype(BF)
    up_back = (back_hidden * active).astype(BF)
    part_out = dot(hidden_half, down_block) * gate
    part_back = (
        dot(gate_back, gate_block, ((1,), (1,)))
        + dot(up_back, up_block, ((1,), (1,)))
        + logit_grad * router_column[None, :]
    )
    parts = jnp.concatenate([part_out.astype(BF), part_back.astype(BF)], axis=1)
    router_part = jnp.sum(logit_grad * x.astype(F32), axis=0)
    hidden_scaled = (hidden * gate).astype(BF)
    return parts, gate_back, up_back, hidden_scaled, router_part


def shards(
    frames,
    cotangent,
    routes,
    stream_lengths,
    conv_weight,
    router_weight,
    gate_weight,
    up_weight,
    down_weight,
):
    row_count = frames.shape[1]
    width = frames.shape[2]
    experts = lax.axis_size("seq")
    capacity = 5 * row_count // (2 * experts)
    slots = experts * capacity
    kernel_size = conv_weight.shape[0]
    half_kernel = kernel_size // 2
    me_seq = lax.axis_index("seq")

    padded = halos(frames[0], half_kernel).astype(F32)
    anchor = me_seq * row_count
    places = anchor - half_kernel + jnp.arange(row_count + 2 * half_kernel, dtype=jnp.int32)
    bounds = jnp.cumsum(stream_lengths[0])
    stream_of = jnp.sum((places[:, None] >= bounds[None, :]).astype(jnp.int32), axis=1)
    centre = stream_of[half_kernel : half_kernel + row_count]
    same_masks = []
    conv_sum = jnp.zeros((row_count, width), F32)
    for offset in range(kernel_size):
        same = (stream_of[offset : offset + row_count] == centre).astype(F32)[:, None]
        same_masks.append(same)
        conv_sum = conv_sum + conv_weight[offset] * padded[offset : offset + row_count] * same
    conv_out = (frames[0].astype(F32) + conv_sum).astype(BF)

    chosen = routes[0]
    labels = jnp.arange(experts, dtype=jnp.int32)
    member = [(chosen[:, k : k + 1] == labels[None, :]) for k in range(2)]
    both = (member[0] | member[1]).astype(BF)
    row_id = jnp.arange(row_count, dtype=jnp.int32)
    earlier = (row_id[:, None] > row_id[None, :]).astype(BF)
    before = dot(earlier, both).astype(jnp.int32)
    slot_id = jnp.arange(slots, dtype=jnp.int32)
    place = jnp.zeros((slots, row_count), jnp.bool_)
    for k in range(2):
        rank = jnp.sum(jnp.where(member[k], before, 0), axis=1)
        place = place | (slot_id[:, None] == (chosen[:, k] * capacity + rank)[None, :])
    place = place.astype(BF)

    sent = dot(place, jnp.concatenate([conv_out, cotangent[0]], axis=1)).astype(BF)
    own = lax.all_to_all(
        sent.reshape(experts, capacity, 2 * width), "seq", split_axis=0, concat_axis=0, tiled=True
    ).reshape(slots, 2 * width)

    gate_block, up_block, down_block = gate_weight[0], up_weight[0], down_weight[0]
    router_column = lax.dynamic_slice_in_dim(router_weight, me_seq, 1, axis=1)[:, 0].astype(F32)

    current = own
    steps = lax.axis_size("expert") // 2
    pairs, results = [], []
    for step in range(steps):
        other = flip(current, "expert", 1)
        pair = jnp.concatenate([current, other], axis=0)
        if step < steps - 1:
            current = ring_up(current)
        pairs.append(pair)
        results.append(expert_chunk(pair, gate_block, up_block, down_block, router_column))

    total = None
    for step in list(range(1, steps)) + [0]:
        parts = results[step][0]
        got = flip(parts[slots:], "expert", 1)
        chip = parts[:slots].astype(F32) + got.astype(F32)
        if total is not None:
            chip = chip + total.astype(F32)
        total = chip.astype(BF)
        if step != 0:
            total = ring_up(total)

    rows_all = jnp.concatenate([p[:, :width] for p in pairs], axis=0)
    grads_all = jnp.concatenate([p[:, width:] for p in pairs], axis=0)
    gate_back, up_back, hidden = [
        jnp.concatenate([r[i] for r in results], axis=0) for i in (1, 2, 3)
    ]
    gate_grads = dot(rows_all, gate_back, ((0,), (0,)))
    up_grads = dot(rows_all, up_back, ((0,), (0,)))
    down_grads = dot(hidden, grads_all, ((0,), (0,)))

    router_part = sum(r[4] for r in results)[None, :]
    for bit in (1, 2, 4):
        router_part = router_part + flip(router_part, "expert", bit)
    for bit in (1, 2, 4, 8, 16):
        got = flip(router_part, "seq", bit)
        upper = (me_seq & bit) != 0
        router_part = jnp.concatenate(
            [jnp.where(upper, got, router_part), jnp.where(upper, router_part, got)], axis=0
        )
    router_total = router_part.T

    back = lax.all_to_all(
        total.reshape(experts, capacity, 2 * width), "seq", split_axis=0, concat_axis=0, tiled=True
    ).reshape(slots, 2 * width)
    summed = dot(place, back, ((0,), (0,)))
    block_out = (conv_out.astype(F32) + summed[:, :width]).astype(BF)
    grad_half = (cotangent[0].astype(F32) + summed[:, width:]).astype(BF)

    centre_grad = grad_half.astype(F32)
    taps = jnp.stack(
        [
            jnp.sum(centre_grad * padded[j : j + row_count] * same_masks[j], axis=0)
            for j in range(kernel_size)
        ]
    )
    half = kernel_size // 2
    core = lax.axis_index("expert") & 1
    mine = lax.dynamic_slice_in_dim(taps, core * half, half, axis=0)
    theirs = lax.dynamic_slice_in_dim(taps, (1 - core) * half, half, axis=0)
    mine = mine + flip(theirs, "expert", 1)
    for axis, bit in (("expert", 2), ("expert", 4), ("seq", 2), ("seq", 4), ("seq", 8), ("seq", 16), ("seq", 1)):
        mine = mine + flip(mine, axis, bit)
    got = flip(mine, "expert", 1)
    conv_grads = jnp.concatenate(
        [jnp.where(core == 0, mine, got), jnp.where(core == 0, got, mine)], axis=0
    )

    grad_pad = halos(grad_half, half_kernel).astype(F32)
    back_sum = jnp.zeros((row_count, width), F32)
    for offset in range(kernel_size):
        begin = 2 * half_kernel - offset
        same = (stream_of[begin : begin + row_count] == centre).astype(F32)[:, None]
        back_sum = back_sum + conv_weight[offset] * grad_pad[begin : begin + row_count] * same
    frame_grad = (centre_grad + back_sum).astype(BF)
    return (
        block_out[None],
        frame_grad[None],
        conv_grads,
        router_total,
        gate_grads[None],
        up_grads[None],
        down_grads[None],
    )


def solution(mesh):
    in_specs = (
        P("expert", "seq", None),
        P("expert", "seq", None),
        P("expert", "seq", None),
        P("expert", None),
        P(),
        P(),
        P("seq", None, "expert"),
        P("seq", None, "expert"),
        P("seq", "expert", None),
    )
    out_specs = (
        P("expert", "seq", None),
        P("expert", "seq", None),
        P(),
        P(),
        P("seq", None, "expert"),
        P("seq", None, "expert"),
        P("seq", "expert", None),
    )
    return jax.shard_map(shards, mesh=mesh, in_specs=in_specs, out_specs=out_specs, check_vma=False)
```

```python
import jax
import jax.numpy as jnp
from jax import lax
from jax.experimental import pallas as pl
from jax.experimental.pallas import tpu as pltpu
from jax.sharding import PartitionSpec as P

BF = jnp.bfloat16
F32 = jnp.float32
LANES = 128


def flip(value, axis, bit):
    count = lax.axis_size(axis)
    return lax.ppermute(value, axis, [(i, i ^ bit) for i in range(count)])


def ring_up(value):
    count = lax.axis_size("expert")
    return lax.ppermute(value, "expert", [(i, (i + 2) % count) for i in range(count)])


def halos(block, width):
    count = lax.axis_size("seq")
    forward = [(i, i + 1) for i in range(count - 1)]
    backward = [(i + 1, i) for i in range(count - 1)]
    low = lax.ppermute(block[block.shape[0] - width :], "seq", forward)
    high = lax.ppermute(block[:width], "seq", backward)
    return low, high


def dot(a, b, dims=((1,), (0,))):
    return lax.dot_general(a, b, (dims, ((), ())), preferred_element_type=F32)


NT = ((1,), (1,))
TN = ((0,), (0,))


def call(body, outs, scratch, flops, moved, smem=0):
    in_vmem = pl.BlockSpec(memory_space=pltpu.VMEM)

    def run(*args):
        specs = [pl.BlockSpec(memory_space=pltpu.SMEM)] * smem + [in_vmem] * (len(args) - smem)
        return pl.pallas_call(
            body,
            out_shape=[jax.ShapeDtypeStruct(*o) for o in outs],
            in_specs=specs,
            out_specs=[in_vmem] * len(outs),
            scratch_shapes=scratch,
            compiler_params=pltpu.CompilerParams(vmem_limit_bytes=48 * 1024 * 1024),
            cost_estimate=pl.CostEstimate(flops=flops, bytes_accessed=moved, transcendentals=0),
        )(*args)

    return run


def expert_body(
    own, other, gate_w, up_w, down_w, wide, column,
    out_own, back_own, out_other, back_other, gate_back, up_back, hidden, router_part,
    gp_ref, up_ref, bb_ref, lg_ref,
):
    slots = own.shape[0] // 2
    hid = gate_w.shape[1]
    repeat = hid // LANES
    for k, src in enumerate((own, other)):
        at = pl.ds(k * slots, slots)
        x = src[:slots]
        gp_ref[at] = dot(x, gate_w[...])
        up_ref[at] = dot(x, up_w[...])
        bb_ref[at] = dot(src[slots:], down_w[...], NT)
        lg_ref[at] = dot(x, wide[...])
    tile = 32

    def step(i, carry):
        at = pl.ds(pl.multiple_of(i * tile, tile), tile)
        gate = jax.nn.sigmoid(lg_ref[at])
        gate_all = jnp.concatenate([gate] * repeat, axis=1)
        gp, up, bb = gp_ref[at], up_ref[at], bb_ref[at]
        sig = jax.nn.sigmoid(gp)
        active = gp * sig
        hid_v = active * up
        terms = hid_v * bb
        row = sum(terms[:, j * LANES : (j + 1) * LANES] for j in range(repeat))
        total = jnp.sum(row, axis=1, keepdims=True)
        lg_ref[at] = total * (gate * (1.0 - gate))
        bh = bb * gate_all
        hidden[at] = (hid_v * gate_all).astype(BF)
        gate_back[at] = (bh * up * (sig * (1.0 + gp * (1.0 - sig)))).astype(BF)
        up_back[at] = (bh * active).astype(BF)
        return carry

    lax.fori_loop(0, 2 * slots // tile, step, 0)
    width = own.shape[1]
    for k, (src, out, back) in enumerate(((own, out_own, back_own), (other, out_other, back_other))):
        at = pl.ds(k * slots, slots)
        out[...] = dot(hidden[at], down_w[...]).astype(BF)
        lg_all = jnp.concatenate([lg_ref[at]] * (width // LANES), axis=1)
        both = dot(gate_back[at], gate_w[...], NT) + dot(up_back[at], up_w[...], NT)
        back[...] = (both + lg_all * column[...]).astype(BF)
    acc = jnp.zeros((8, width), F32)

    def add(i, acc):
        for k, src in enumerate((own, other)):
            at = pl.ds(pl.multiple_of(i * 16, 16), 16)
            here = pl.ds(pl.multiple_of(k * slots + i * 16, 16), 16)
            lg_all = jnp.concatenate([lg_ref[here]] * (width // LANES), axis=1)
            prod = src[at].astype(F32) * lg_all
            acc = acc + prod[:8] + prod[8:]
        return acc

    acc = lax.fori_loop(0, slots // 16, add, acc)
    router_part[...] = jnp.sum(acc, axis=0, keepdims=True)


def grads_body(*refs):
    pairs = refs[:8]
    triples = refs[8:20]
    gate_out, up_out, down_out = refs[20:]
    slots = pairs[0].shape[0] // 2
    for n in range(4):
        gate_back, up_back, hidden = triples[3 * n : 3 * n + 3]
        for k in range(2):
            src = pairs[2 * n + k]
            at = pl.ds(k * slots, slots)
            x = src[:slots]
            c = src[slots:]
            first = n == 0 and k == 0
            a = dot(x, gate_back[at], TN)
            b = dot(x, up_back[at], TN)
            d = dot(hidden[at], c, TN)
            gate_out[...] = a if first else gate_out[...] + a
            up_out[...] = b if first else up_out[...] + b
            down_out[...] = d if first else down_out[...] + d


def stream_ids(bounds, anchor, half, ids_ref):
    place = anchor[0] - half + lax.broadcasted_iota(jnp.int32, ids_ref.shape, 0)
    total = jnp.zeros(ids_ref.shape, jnp.int32)
    edge = jnp.int32(0)
    for s in range(bounds.shape[0]):
        edge = edge + bounds[s]
        total = total + (place >= edge).astype(jnp.int32)
    ids_ref[...] = total


def same_rows(ids_ref, begin, rows, half, copies):
    same = ids_ref[pl.ds(begin, rows)] == ids_ref[pl.ds(half, rows)]
    return jnp.concatenate([same] * copies, axis=1)


def conv_sum(pad_ref, ids_ref, weight, begin0, rows, half, lanes, order):
    taps = weight.shape[0]
    total = jnp.zeros((rows, lanes.size), F32)
    for i in range(taps):
        begin = begin0 + i
        tap = weight[pl.ds(order(i), 1), lanes]
        same = same_rows(ids_ref, begin, rows, half, lanes.size // LANES)
        total = total + tap * jnp.where(same, pad_ref[pl.ds(begin, rows), lanes], 0.0)
    return total


SPAN = 256


def conv_body(bounds, anchor, low, mid, high, cot, weight, place, conv_out, packed, pad_ref, ids_ref, both_ref):
    rows, width = mid.shape
    half = low.shape[0]
    pad_ref[:half] = low[...].astype(F32)
    pad_ref[half : half + rows] = mid[...].astype(F32)
    pad_ref[half + rows :] = high[...].astype(F32)
    stream_ids(bounds, anchor, half, ids_ref)
    for b in range(width // SPAN):
        lanes = pl.ds(b * SPAN, SPAN)
        total = conv_sum(pad_ref, ids_ref, weight, 0, rows, half, lanes, lambda i: i)
        value = (pad_ref[pl.ds(half, rows), lanes] + total).astype(BF)
        conv_out[:, lanes] = value
        both_ref[:rows, lanes] = value
    both_ref[rows:] = cot[...]
    packed[...] = dot(place[...], both_ref[...]).astype(BF)


def combine_body(bounds, anchor, low, mid, high, cot, place, arrived, grad_half, taps, pad_ref, ids_ref, cg_ref):
    rows, width = mid.shape
    half = low.shape[0]
    pad_ref[:half] = low[...].astype(F32)
    pad_ref[half : half + rows] = mid[...].astype(F32)
    pad_ref[half + rows :] = high[...].astype(F32)
    stream_ids(bounds, anchor, half, ids_ref)
    summed = dot(place[...], arrived[...], TN)
    part = width // 2
    for h in range(2):
        lanes = pl.ds(h * part, part)
        value = (cot[:, lanes].astype(F32) + summed[h * rows : (h + 1) * rows]).astype(BF)
        grad_half[:, lanes] = value
        cg_ref[:, lanes] = value.astype(F32)
    for b in range(width // SPAN):
        lanes = pl.ds(b * SPAN, SPAN)
        centre = cg_ref[:, lanes]
        for j in range(taps.shape[0]):
            same = same_rows(ids_ref, j, rows, half, SPAN // LANES)
            prod = centre * jnp.where(same, pad_ref[pl.ds(j, rows), lanes], 0.0)
            taps[pl.ds(j, 1), lanes] = jnp.sum(prod, axis=0, keepdims=True)


def back_body(bounds, anchor, low, mid, high, weight, frame_grad, pad_ref, ids_ref):
    rows, width = mid.shape
    half = low.shape[0]
    pad_ref[:half] = low[...].astype(F32)
    pad_ref[half : half + rows] = mid[...].astype(F32)
    pad_ref[half + rows :] = high[...].astype(F32)
    stream_ids(bounds, anchor, half, ids_ref)
    taps = weight.shape[0]
    for b in range(width // SPAN):
        lanes = pl.ds(b * SPAN, SPAN)
        total = conv_sum(pad_ref, ids_ref, weight, 1, rows, half, lanes, lambda i: taps - 1 - i)
        frame_grad[:, lanes] = (pad_ref[pl.ds(half, rows), lanes] + total).astype(BF)


def shards(
    frames,
    cotangent,
    routes,
    stream_lengths,
    conv_weight,
    router_weight,
    gate_weight,
    up_weight,
    down_weight,
):
    row_count = frames.shape[1]
    width = frames.shape[2]
    part = width // 2
    experts = lax.axis_size("seq")
    capacity = 5 * row_count // (2 * experts)
    slots = experts * capacity
    kernel_size = conv_weight.shape[0]
    half = kernel_size // 2
    me_seq = lax.axis_index("seq")
    cot = cotangent[0]
    mid = frames[0]
    low, high = halos(mid, half)
    bounds = stream_lengths[0]
    anchor = (me_seq * row_count)[None].astype(jnp.int32)

    chosen = routes[0]
    labels = jnp.arange(experts, dtype=jnp.int32)
    member = [(chosen[:, k : k + 1] == labels[None, :]) for k in range(2)]
    both = (member[0] | member[1]).astype(BF)
    row_id = jnp.arange(row_count, dtype=jnp.int32)
    earlier = (row_id[:, None] > row_id[None, :]).astype(BF)
    before = dot(earlier, both).astype(jnp.int32)
    slot_of = [
        chosen[:, k] * capacity + jnp.sum(jnp.where(member[k], before, 0), axis=1) for k in range(2)
    ]
    block = -(-2 * capacity // 8) * 8
    packed_id = jnp.arange(experts * block, dtype=jnp.int32)
    inner = packed_id % block
    key = jnp.where(
        inner < 2 * capacity,
        (inner // capacity) * slots + (packed_id // block) * capacity + inner % capacity,
        -1,
    )
    column_key = [jnp.concatenate([s, s + slots]) for s in slot_of]
    place = (
        (key[:, None] == column_key[0][None, :]) | (key[:, None] == column_key[1][None, :])
    ).astype(BF)
    dense = (jnp.arange(2 * slots, dtype=jnp.int32)[:, None] == key[None, :]).astype(BF)

    pad_rows = row_count + 2 * half
    pad_scratch = [pltpu.VMEM((pad_rows, width), F32), pltpu.VMEM((pad_rows, LANES), jnp.int32)]
    conv_cost = (6 * kernel_size * row_count * width, 4 << 20)
    conv_out, packed = call(
        conv_body,
        [((row_count, width), BF), ((experts * block, width), BF)],
        pad_scratch + [pltpu.VMEM((2 * row_count, width), BF)],
        *conv_cost,
        smem=2,
    )(bounds, anchor, low, mid, high, cot, conv_weight, place)

    def over_seq(value):
        cols = value.shape[1]
        return lax.all_to_all(
            value.reshape(experts, block, cols), "seq", split_axis=0, concat_axis=0, tiled=True
        ).reshape(experts * block, cols)

    current = dot(dense, over_seq(packed)).astype(BF)

    gate_block, up_block, down_block = gate_weight[0], up_weight[0], down_weight[0]
    column = lax.dynamic_slice_in_dim(router_weight, me_seq, 1, axis=1)
    wide = jnp.broadcast_to(column, (width, LANES))
    column_row = column.astype(F32).T
    hid = gate_block.shape[1]
    expert = call(
        expert_body,
        [((slots, width), BF)] * 4 + [((2 * slots, hid), BF)] * 3 + [((1, width), F32)],
        [pltpu.VMEM((2 * slots, hid), F32)] * 3 + [pltpu.VMEM((2 * slots, LANES), F32)],
        12 * 2 * slots * width * hid,
        12 << 20,
    )

    steps = lax.axis_size("expert") // 2
    pairs, results = [], []
    for step in range(steps):
        other = flip(current, "expert", 1)
        here = current
        if step < steps - 1:
            current = ring_up(current)
        pairs += [here, other]
        results.append(expert(here, other, gate_block, up_block, down_block, wide, column_row))

    def chip_sum(step, which, total):
        own, away = results[step][which], results[step][which + 2]
        value = own.astype(F32) + flip(away, "expert", 1).astype(F32)
        if total is not None:
            value = value + total.astype(F32)
        return value.astype(BF)

    total_back = None
    for step in range(1, steps):
        total_back = chip_sum(step, 1, total_back)
        if step == steps - 1:
            first_out, total_back = lax.optimization_barrier((results[1][0], total_back))
            results[1] = [first_out] + list(results[1][1:])
        total_back = ring_up(total_back)
    total_back = chip_sum(0, 1, total_back)
    total_out = None
    for step in range(1, steps):
        total_out = ring_up(chip_sum(step, 0, total_out))
    total_out = chip_sum(0, 0, total_out)

    gate_grads, up_grads, down_grads = call(
        grads_body,
        [((width, hid), F32), ((width, hid), F32), ((hid, width), F32)],
        [],
        6 * 8 * slots * width * hid,
        16 << 20,
    )(*pairs, *[r[i] for r in results for i in (4, 5, 6)])

    router_part = sum(r[7] for r in results)
    for bit in (1, 2, 4):
        router_part = router_part + flip(router_part, "expert", bit)
    for bit in (1, 2, 4, 8, 16):
        got = flip(router_part, "seq", bit)
        upper = (me_seq & bit) != 0
        router_part = jnp.concatenate(
            [jnp.where(upper, got, router_part), jnp.where(upper, router_part, got)], axis=0
        )
    router_total = router_part.T

    def pack_back(total):
        halves = jnp.concatenate([total[:, :part], total[:, part:]], axis=0)
        return over_seq(dot(dense, halves, TN).astype(BF))

    arrived = pack_back(total_back)
    grad_half, taps = call(
        combine_body,
        [((row_count, width), BF), ((kernel_size, width), F32)],
        pad_scratch + [pltpu.VMEM((row_count, width), F32)],
        *conv_cost,
        smem=2,
    )(bounds, anchor, low, mid, high, cot, place, arrived)

    grad_low, grad_high = halos(grad_half, half)
    (frame_grad,) = call(
        back_body, [((row_count, width), BF)], pad_scratch, *conv_cost, smem=2
    )(bounds, anchor, grad_low, grad_half, grad_high, conv_weight)

    split = kernel_size // 2
    core = lax.axis_index("expert") & 1
    mine = lax.dynamic_slice_in_dim(taps, core * split, split, axis=0)
    theirs = lax.dynamic_slice_in_dim(taps, (1 - core) * split, split, axis=0)
    mine = mine + flip(theirs, "expert", 1)
    for axis, bit in (("expert", 2), ("expert", 4), ("seq", 2), ("seq", 4), ("seq", 8), ("seq", 16), ("seq", 1)):
        mine = mine + flip(mine, axis, bit)
    got = flip(mine, "expert", 1)
    conv_grads = jnp.concatenate(
        [jnp.where(core == 0, mine, got), jnp.where(core == 0, got, mine)], axis=0
    )

    summed = dot(place, pack_back(total_out), TN)
    out_sum = jnp.concatenate([summed[:row_count], summed[row_count:]], axis=1)
    block_out = (conv_out.astype(F32) + out_sum).astype(BF)
    return (
        block_out[None],
        frame_grad[None],
        conv_grads,
        router_total,
        gate_grads[None],
        up_grads[None],
        down_grads[None],
    )


def solution(mesh):
    in_specs = (
        P("expert", "seq", None),
        P("expert", "seq", None),
        P("expert", "seq", None),
        P("expert", None),
        P(),
        P(),
        P("seq", None, "expert"),
        P("seq", None, "expert"),
        P("seq", "expert", None),
    )
    out_specs = (
        P("expert", "seq", None),
        P("expert", "seq", None),
        P(),
        P(),
        P("seq", None, "expert"),
        P("seq", None, "expert"),
        P("seq", "expert", None),
    )
    return jax.shard_map(shards, mesh=mesh, in_specs=in_specs, out_specs=out_specs, check_vma=False)
```

```python
import jax
import jax.numpy as jnp
from jax import lax
from jax.experimental import pallas as pl
from jax.experimental.pallas import tpu as pltpu
from jax.sharding import PartitionSpec as P

BF = jnp.bfloat16
F32 = jnp.float32
LANES = 128


def flip(value, axis, bit):
    count = lax.axis_size(axis)
    return lax.ppermute(value, axis, [(i, i ^ bit) for i in range(count)])


def ring_up(value):
    count = lax.axis_size("expert")
    return lax.ppermute(value, "expert", [(i, (i + 2) % count) for i in range(count)])


def halos(block, width):
    count = lax.axis_size("seq")
    forward = [(i, i + 1) for i in range(count - 1)]
    backward = [(i + 1, i) for i in range(count - 1)]
    low = lax.ppermute(block[block.shape[0] - width :], "seq", forward)
    high = lax.ppermute(block[:width], "seq", backward)
    return low, high


def dot(a, b, dims=((1,), (0,))):
    return lax.dot_general(a, b, (dims, ((), ())), preferred_element_type=F32)


NT = ((1,), (1,))
TN = ((0,), (0,))


def call(body, outs, scratch, flops, moved, smem=0):
    in_vmem = pl.BlockSpec(memory_space=pltpu.VMEM)

    def run(*args):
        specs = [pl.BlockSpec(memory_space=pltpu.SMEM)] * smem + [in_vmem] * (len(args) - smem)
        return pl.pallas_call(
            body,
            out_shape=[jax.ShapeDtypeStruct(*o) for o in outs],
            in_specs=specs,
            out_specs=[in_vmem] * len(outs),
            scratch_shapes=scratch,
            compiler_params=pltpu.CompilerParams(vmem_limit_bytes=24 * 1024 * 1024),
            cost_estimate=pl.CostEstimate(flops=flops, bytes_accessed=moved, transcendentals=0),
        )(*args)

    return run


def expert_body(
    own, other, gate_w, up_w, down_w, wide, column,
    out_own, back_own, out_other, back_other, gate_back, up_back, hidden, router_part,
    gp_ref, up_ref, bb_ref, lg_ref,
):
    slots = own.shape[0] // 2
    hid = gate_w.shape[1]
    repeat = hid // LANES
    for k, src in enumerate((own, other)):
        at = pl.ds(k * slots, slots)
        x = src[:slots]
        gp_ref[at] = dot(x, gate_w[...])
        up_ref[at] = dot(x, up_w[...])
        bb_ref[at] = dot(src[slots:], down_w[...], NT)
        lg_ref[at] = dot(x, wide[...])
    tile = 32

    def step(i, carry):
        at = pl.ds(pl.multiple_of(i * tile, tile), tile)
        gate = jax.nn.sigmoid(lg_ref[at])
        gate_all = jnp.concatenate([gate] * repeat, axis=1)
        gp, up, bb = gp_ref[at], up_ref[at], bb_ref[at]
        sig = jax.nn.sigmoid(gp)
        active = gp * sig
        hid_v = active * up
        terms = hid_v * bb
        row = sum(terms[:, j * LANES : (j + 1) * LANES] for j in range(repeat))
        total = jnp.sum(row, axis=1, keepdims=True)
        lg_ref[at] = total * (gate * (1.0 - gate))
        bh = bb * gate_all
        hidden[at] = (hid_v * gate_all).astype(BF)
        gate_back[at] = (bh * up * (sig * (1.0 + gp * (1.0 - sig)))).astype(BF)
        up_back[at] = (bh * active).astype(BF)
        return carry

    lax.fori_loop(0, 2 * slots // tile, step, 0)
    width = own.shape[1]
    for k, (src, out, back) in enumerate(((own, out_own, back_own), (other, out_other, back_other))):
        at = pl.ds(k * slots, slots)
        out[...] = dot(hidden[at], down_w[...]).astype(BF)
        lg_all = jnp.concatenate([lg_ref[at]] * (width // LANES), axis=1)
        both = dot(gate_back[at], gate_w[...], NT) + dot(up_back[at], up_w[...], NT)
        back[...] = (both + lg_all * column[...]).astype(BF)
    acc = jnp.zeros((8, width), F32)

    def add(i, acc):
        for k, src in enumerate((own, other)):
            at = pl.ds(pl.multiple_of(i * 16, 16), 16)
            here = pl.ds(pl.multiple_of(k * slots + i * 16, 16), 16)
            lg_all = jnp.concatenate([lg_ref[here]] * (width // LANES), axis=1)
            prod = src[at].astype(F32) * lg_all
            acc = acc + prod[:8] + prod[8:]
        return acc

    acc = lax.fori_loop(0, slots // 16, add, acc)
    router_part[...] = jnp.sum(acc, axis=0, keepdims=True)


def grads_body(*refs):
    pairs = refs[:8]
    triples = refs[8:20]
    gate_out, up_out, down_out = refs[20:]
    slots = pairs[0].shape[0] // 2
    for n in range(4):
        gate_back, up_back, hidden = triples[3 * n : 3 * n + 3]
        for k in range(2):
            src = pairs[2 * n + k]
            at = pl.ds(k * slots, slots)
            x = src[:slots]
            c = src[slots:]
            first = n == 0 and k == 0
            a = dot(x, gate_back[at], TN)
            b = dot(x, up_back[at], TN)
            d = dot(hidden[at], c, TN)
            gate_out[...] = a if first else gate_out[...] + a
            up_out[...] = b if first else up_out[...] + b
            down_out[...] = d if first else down_out[...] + d


def stream_ids(bounds, anchor, half, ids_ref):
    place = anchor[0] - half + lax.broadcasted_iota(jnp.int32, ids_ref.shape, 0)
    total = jnp.zeros(ids_ref.shape, jnp.int32)
    edge = jnp.int32(0)
    for s in range(bounds.shape[0]):
        edge = edge + bounds[s]
        total = total + (place >= edge).astype(jnp.int32)
    ids_ref[...] = total


def same_rows(ids_ref, begin, rows, half, copies):
    same = ids_ref[pl.ds(begin, rows)] == ids_ref[pl.ds(half, rows)]
    return jnp.concatenate([same] * copies, axis=1)


def conv_sum(pad_ref, ids_ref, weight, begin0, rows, half, lanes, order):
    taps = weight.shape[0]
    total = jnp.zeros((rows, lanes.size), F32)
    for i in range(taps):
        begin = begin0 + i
        tap = weight[pl.ds(order(i), 1), lanes]
        same = same_rows(ids_ref, begin, rows, half, lanes.size // LANES)
        total = total + tap * jnp.where(same, pad_ref[pl.ds(begin, rows), lanes], 0.0)
    return total


SPAN = 256


def conv_body(bounds, anchor, low, mid, high, cot, weight, place, conv_out, packed, pad_ref, ids_ref, both_ref):
    rows, width = mid.shape
    half = low.shape[0]
    pad_ref[:half] = low[...].astype(F32)
    pad_ref[half : half + rows] = mid[...].astype(F32)
    pad_ref[half + rows :] = high[...].astype(F32)
    stream_ids(bounds, anchor, half, ids_ref)
    for b in range(width // SPAN):
        lanes = pl.ds(b * SPAN, SPAN)
        total = conv_sum(pad_ref, ids_ref, weight, 0, rows, half, lanes, lambda i: i)
        value = (pad_ref[pl.ds(half, rows), lanes] + total).astype(BF)
        conv_out[:, lanes] = value
        both_ref[:rows, lanes] = value
    both_ref[rows:] = cot[...]
    packed[...] = dot(place[...], both_ref[...]).astype(BF)


def combine_body(cot, place, arrived, grad_half):
    rows, width = cot.shape
    summed = dot(place[...], arrived[...], TN)
    part = width // 2
    for h in range(2):
        lanes = pl.ds(h * part, part)
        grad_half[:, lanes] = (cot[:, lanes].astype(F32) + summed[h * rows : (h + 1) * rows]).astype(BF)


def taps_body(bounds, anchor, low, mid, high, grad_half, taps, pad_ref, ids_ref):
    rows, width = mid.shape
    half = low.shape[0]
    pad_ref[:half] = low[...].astype(F32)
    pad_ref[half : half + rows] = mid[...].astype(F32)
    pad_ref[half + rows :] = high[...].astype(F32)
    stream_ids(bounds, anchor, half, ids_ref)
    for b in range(width // SPAN):
        lanes = pl.ds(b * SPAN, SPAN)
        centre = grad_half[:, lanes].astype(F32)
        for j in range(taps.shape[0]):
            same = same_rows(ids_ref, j, rows, half, SPAN // LANES)
            prod = centre * jnp.where(same, pad_ref[pl.ds(j, rows), lanes], 0.0)
            taps[pl.ds(j, 1), lanes] = jnp.sum(prod, axis=0, keepdims=True)


def back_body(bounds, anchor, low, mid, high, weight, frame_grad, pad_ref, ids_ref):
    rows, width = mid.shape
    half = low.shape[0]
    pad_ref[:half] = low[...].astype(F32)
    pad_ref[half : half + rows] = mid[...].astype(F32)
    pad_ref[half + rows :] = high[...].astype(F32)
    stream_ids(bounds, anchor, half, ids_ref)
    taps = weight.shape[0]
    for b in range(width // SPAN):
        lanes = pl.ds(b * SPAN, SPAN)
        total = conv_sum(pad_ref, ids_ref, weight, 1, rows, half, lanes, lambda i: taps - 1 - i)
        frame_grad[:, lanes] = (pad_ref[pl.ds(half, rows), lanes] + total).astype(BF)


def shards(
    frames,
    cotangent,
    routes,
    stream_lengths,
    conv_weight,
    router_weight,
    gate_weight,
    up_weight,
    down_weight,
):
    row_count = frames.shape[1]
    width = frames.shape[2]
    part = width // 2
    experts = lax.axis_size("seq")
    capacity = 5 * row_count // (2 * experts)
    slots = experts * capacity
    kernel_size = conv_weight.shape[0]
    half = kernel_size // 2
    me_seq = lax.axis_index("seq")
    cot = cotangent[0]
    mid = frames[0]
    low, high = halos(mid, half)
    bounds = stream_lengths[0]
    anchor = (me_seq * row_count)[None].astype(jnp.int32)

    chosen = routes[0]
    labels = jnp.arange(experts, dtype=jnp.int32)
    member = [(chosen[:, k : k + 1] == labels[None, :]) for k in range(2)]
    both = (member[0] | member[1]).astype(BF)
    row_id = jnp.arange(row_count, dtype=jnp.int32)
    earlier = (row_id[:, None] > row_id[None, :]).astype(BF)
    before = dot(earlier, both).astype(jnp.int32)
    slot_of = [
        chosen[:, k] * capacity + jnp.sum(jnp.where(member[k], before, 0), axis=1) for k in range(2)
    ]
    block = -(-2 * capacity // 8) * 8
    packed_id = jnp.arange(experts * block, dtype=jnp.int32)
    inner = packed_id % block
    key = jnp.where(
        inner < 2 * capacity,
        (inner // capacity) * slots + (packed_id // block) * capacity + inner % capacity,
        -1,
    )
    column_key = [jnp.concatenate([s, s + slots]) for s in slot_of]
    place = (
        (key[:, None] == column_key[0][None, :]) | (key[:, None] == column_key[1][None, :])
    ).astype(BF)
    dense = (jnp.arange(2 * slots, dtype=jnp.int32)[:, None] == key[None, :]).astype(BF)

    pad_rows = row_count + 2 * half
    pad_scratch = [pltpu.VMEM((pad_rows, width), F32), pltpu.VMEM((pad_rows, LANES), jnp.int32)]
    conv_cost = (6 * kernel_size * row_count * width, 4 << 20)
    conv_out, packed = call(
        conv_body,
        [((row_count, width), BF), ((experts * block, width), BF)],
        pad_scratch + [pltpu.VMEM((2 * row_count, width), BF)],
        *conv_cost,
        smem=2,
    )(bounds, anchor, low, mid, high, cot, conv_weight, place)

    def over_seq(value):
        cols = value.shape[1]
        return lax.all_to_all(
            value.reshape(experts, block, cols), "seq", split_axis=0, concat_axis=0, tiled=True
        ).reshape(experts * block, cols)

    current = dot(dense, over_seq(packed)).astype(BF)

    gate_block, up_block, down_block = gate_weight[0], up_weight[0], down_weight[0]
    column = lax.dynamic_slice_in_dim(router_weight, me_seq, 1, axis=1)
    wide = jnp.broadcast_to(column, (width, LANES))
    column_row = column.astype(F32).T
    hid = gate_block.shape[1]
    expert = call(
        expert_body,
        [((slots, width), BF)] * 4 + [((2 * slots, hid), BF)] * 3 + [((1, width), F32)],
        [pltpu.VMEM((2 * slots, hid), F32)] * 3 + [pltpu.VMEM((2 * slots, LANES), F32)],
        12 * 2 * slots * width * hid,
        12 << 20,
    )

    steps = lax.axis_size("expert") // 2
    currents, others, results = [current], [], []

    def chip_sum(step, which, total):
        own, away = results[step][which], results[step][which + 2]
        value = own.astype(F32) + flip(away, "expert", 1).astype(F32)
        if total is not None:
            value = value + total.astype(F32)
        return value.astype(BF)

    def run(step):
        others.append(flip(currents[step], "expert", 1))
        results.append(
            list(expert(currents[step], others[step], gate_block, up_block, down_block, wide, column_row))
        )

    upcoming = ring_up(current)
    run(0)
    total_back = None
    for step in range(1, steps):
        tied = [upcoming, results[step - 1][1], results[step - 1][3]]
        if total_back is None:
            upcoming, results[step - 1][1], results[step - 1][3] = lax.optimization_barrier(tied)
        else:
            upcoming, results[step - 1][1], results[step - 1][3], total_back = lax.optimization_barrier(
                tied + [total_back]
            )
        currents.append(upcoming)
        if step < steps - 1:
            upcoming = ring_up(upcoming)
        if step > 1:
            total_back = ring_up(chip_sum(step - 1, 1, total_back))
        run(step)
    total_back, results[1][0] = lax.optimization_barrier(
        (chip_sum(steps - 1, 1, total_back), results[1][0])
    )
    total_back = ring_up(total_back)

    pairs = [rows for pair in zip(currents, others) for rows in pair]
    weight_grads = call(
        grads_body,
        [((width, hid), F32), ((width, hid), F32), ((hid, width), F32)],
        [],
        6 * 8 * slots * width * hid,
        16 << 20,
    )(*pairs, *[r[i] for r in results for i in (4, 5, 6)])
    total_out = ring_up(chip_sum(1, 0, None))
    total_back, *weight_grads = lax.optimization_barrier((total_back, *weight_grads))
    gate_grads, up_grads, down_grads = weight_grads
    total_back = chip_sum(0, 1, total_back)
    for step in range(2, steps):
        total_out = ring_up(chip_sum(step, 0, total_out))
    total_out = chip_sum(0, 0, total_out)

    router_part = sum(r[7] for r in results)
    router_rows = jnp.where(labels[:, None] == me_seq, router_part, 0.0)

    def pack_back(total):
        halves = jnp.concatenate([total[:, :part], total[:, part:]], axis=0)
        return over_seq(dot(dense, halves, TN).astype(BF))

    arrived = pack_back(total_back)
    (grad_half,) = call(
        combine_body, [((row_count, width), BF)], [], 4 * row_count * experts * block * part, 2 << 20
    )(cot, place, arrived)
    grad_low, grad_high = halos(grad_half, half)
    (taps,) = call(
        taps_body, [((kernel_size, width), F32)], pad_scratch, *conv_cost, smem=2
    )(bounds, anchor, low, mid, high, grad_half)
    (frame_grad,) = call(
        back_body, [((row_count, width), BF)], pad_scratch, *conv_cost, smem=2
    )(bounds, anchor, grad_low, grad_half, grad_high, conv_weight)

    first = (lax.axis_index("expert") & 1) == 0
    mine = jnp.where(first, taps, router_rows) + flip(jnp.where(first, router_rows, taps), "expert", 1)
    for axis, bit in (("seq", 2), ("seq", 4), ("seq", 8), ("seq", 16), ("expert", 2), ("expert", 4), ("seq", 1)):
        if axis == "expert" and bit == 2:
            mine, frame_grad = lax.optimization_barrier((mine, frame_grad))
        mine = mine + flip(mine, axis, bit)
    got = flip(mine, "expert", 1)
    conv_grads = jnp.where(first, mine, got)
    router_total = jnp.where(first, got, mine).T

    summed = dot(place, pack_back(total_out), TN)
    out_sum = jnp.concatenate([summed[:row_count], summed[row_count:]], axis=1)
    block_out = (conv_out.astype(F32) + out_sum).astype(BF)
    return (
        block_out[None],
        frame_grad[None],
        conv_grads,
        router_total,
        gate_grads[None],
        up_grads[None],
        down_grads[None],
    )


def solution(mesh):
    in_specs = (
        P("expert", "seq", None),
        P("expert", "seq", None),
        P("expert", "seq", None),
        P("expert", None),
        P(),
        P(),
        P("seq", None, "expert"),
        P("seq", None, "expert"),
        P("seq", "expert", None),
    )
    out_specs = (
        P("expert", "seq", None),
        P("expert", "seq", None),
        P(),
        P(),
        P("seq", None, "expert"),
        P("seq", None, "expert"),
        P("seq", "expert", None),
    )
    return jax.shard_map(shards, mesh=mesh, in_specs=in_specs, out_specs=out_specs, check_vma=False)
```

```python
import jax
import jax.numpy as jnp
from jax import lax
from jax.experimental import pallas as pl
from jax.experimental.pallas import tpu as pltpu
from jax.sharding import PartitionSpec as P

BF = jnp.bfloat16
F32 = jnp.float32
LANES = 128


def flip(value, axis, bit):
    count = lax.axis_size(axis)
    return lax.ppermute(value, axis, [(i, i ^ bit) for i in range(count)])


def ring_up(value):
    count = lax.axis_size("expert")
    return lax.ppermute(value, "expert", [(i, (i + 2) % count) for i in range(count)])


def halos(block, width):
    count = lax.axis_size("seq")
    forward = [(i, i + 1) for i in range(count - 1)]
    backward = [(i + 1, i) for i in range(count - 1)]
    low = lax.ppermute(block[block.shape[0] - width :], "seq", forward)
    high = lax.ppermute(block[:width], "seq", backward)
    return low, high


def dot(a, b, dims=((1,), (0,))):
    return lax.dot_general(a, b, (dims, ((), ())), preferred_element_type=F32)


NT = ((1,), (1,))
TN = ((0,), (0,))


def call(body, outs, scratch, flops, moved, smem=0):
    in_vmem = pl.BlockSpec(memory_space=pltpu.VMEM)

    def run(*args):
        specs = [pl.BlockSpec(memory_space=pltpu.SMEM)] * smem + [in_vmem] * (len(args) - smem)
        return pl.pallas_call(
            body,
            out_shape=[jax.ShapeDtypeStruct(*o) for o in outs],
            in_specs=specs,
            out_specs=[in_vmem] * len(outs),
            scratch_shapes=scratch,
            compiler_params=pltpu.CompilerParams(vmem_limit_bytes=24 * 1024 * 1024),
            cost_estimate=pl.CostEstimate(flops=flops, bytes_accessed=moved, transcendentals=0),
        )(*args)

    return run


def expert_body(
    own, own_c, other, other_c, gate_w, up_w, down_w, wide, column,
    out_own, back_own, out_other, back_other, gate_back, up_back, hidden, router_part,
    gp_ref, up_ref, bb_ref, lg_ref,
):
    slots = own.shape[0]
    hid = gate_w.shape[1]
    repeat = hid // LANES
    for k, (src, cot) in enumerate(((own, own_c), (other, other_c))):
        at = pl.ds(k * slots, slots)
        x = src[...]
        gp_ref[at] = dot(x, gate_w[...])
        up_ref[at] = dot(x, up_w[...])
        bb_ref[at] = dot(cot[...], down_w[...], NT)
        lg_ref[at] = dot(x, wide[...])
    tile = 32

    def step(i, carry):
        at = pl.ds(pl.multiple_of(i * tile, tile), tile)
        gate = jax.nn.sigmoid(lg_ref[at])
        gate_all = jnp.concatenate([gate] * repeat, axis=1)
        gp, up, bb = gp_ref[at], up_ref[at], bb_ref[at]
        sig = jax.nn.sigmoid(gp)
        active = gp * sig
        hid_v = active * up
        terms = hid_v * bb
        row = sum(terms[:, j * LANES : (j + 1) * LANES] for j in range(repeat))
        total = jnp.sum(row, axis=1, keepdims=True)
        lg_ref[at] = total * (gate * (1.0 - gate))
        bh = bb * gate_all
        hidden[at] = (hid_v * gate_all).astype(BF)
        gate_back[at] = (bh * up * (sig * (1.0 + gp * (1.0 - sig)))).astype(BF)
        up_back[at] = (bh * active).astype(BF)
        return carry

    lax.fori_loop(0, 2 * slots // tile, step, 0)
    width = own.shape[1]
    for k, (src, out, back) in enumerate(((own, out_own, back_own), (other, out_other, back_other))):
        at = pl.ds(k * slots, slots)
        out[...] = dot(hidden[at], down_w[...]).astype(BF)
        lg_all = jnp.concatenate([lg_ref[at]] * (width // LANES), axis=1)
        both = dot(gate_back[at], gate_w[...], NT) + dot(up_back[at], up_w[...], NT)
        back[...] = (both + lg_all * column[...]).astype(BF)
    acc = jnp.zeros((8, width), F32)

    def add(i, acc):
        for k, src in enumerate((own, other)):
            at = pl.ds(pl.multiple_of(i * 16, 16), 16)
            here = pl.ds(pl.multiple_of(k * slots + i * 16, 16), 16)
            lg_all = jnp.concatenate([lg_ref[here]] * (width // LANES), axis=1)
            prod = src[at].astype(F32) * lg_all
            acc = acc + prod[:8] + prod[8:]
        return acc

    acc = lax.fori_loop(0, slots // 16, add, acc)
    router_part[...] = jnp.sum(acc, axis=0, keepdims=True)


def grads_body(*refs):
    quads = refs[:16]
    triples = refs[16:28]
    gate_out, up_out, down_out = refs[28:]
    slots = quads[0].shape[0]
    for n in range(4):
        gate_back, up_back, hidden = triples[3 * n : 3 * n + 3]
        for k in range(2):
            x, c = quads[4 * n + 2 * k : 4 * n + 2 * k + 2]
            at = pl.ds(k * slots, slots)
            first = n == 0 and k == 0
            a = dot(x[...], gate_back[at], TN)
            b = dot(x[...], up_back[at], TN)
            d = dot(hidden[at], c[...], TN)
            gate_out[...] = a if first else gate_out[...] + a
            up_out[...] = b if first else up_out[...] + b
            down_out[...] = d if first else down_out[...] + d


def stream_ids(bounds, anchor, half, ids_ref):
    place = anchor[0] - half + lax.broadcasted_iota(jnp.int32, ids_ref.shape, 0)
    total = jnp.zeros(ids_ref.shape, jnp.int32)
    edge = jnp.int32(0)
    for s in range(bounds.shape[0]):
        edge = edge + bounds[s]
        total = total + (place >= edge).astype(jnp.int32)
    ids_ref[...] = total


def same_rows(ids_ref, begin, rows, half, copies):
    same = ids_ref[pl.ds(begin, rows)] == ids_ref[pl.ds(half, rows)]
    return jnp.concatenate([same] * copies, axis=1)


def conv_sum(pad_ref, ids_ref, weight, begin0, rows, half, lanes, order):
    taps = weight.shape[0]
    total = jnp.zeros((rows, lanes.size), F32)
    for i in range(taps):
        begin = begin0 + i
        tap = weight[pl.ds(order(i), 1), lanes]
        same = same_rows(ids_ref, begin, rows, half, lanes.size // LANES)
        total = total + tap * jnp.where(same, pad_ref[pl.ds(begin, rows), lanes], 0.0)
    return total


SPAN = 256


def conv_body(bounds, anchor, low, mid, high, weight, place, conv_out, packed, pad_ref, ids_ref, both_ref):
    rows, width = mid.shape
    part = width // 2
    half = low.shape[0]
    pad_ref[:half] = low[...].astype(F32)
    pad_ref[half : half + rows] = mid[...].astype(F32)
    pad_ref[half + rows :] = high[...].astype(F32)
    stream_ids(bounds, anchor, half, ids_ref)
    for b in range(width // SPAN):
        lanes = pl.ds(b * SPAN, SPAN)
        total = conv_sum(pad_ref, ids_ref, weight, 0, rows, half, lanes, lambda i: i)
        value = (pad_ref[pl.ds(half, rows), lanes] + total).astype(BF)
        conv_out[:, lanes] = value
    both_ref[:rows] = conv_out[:, :part]
    both_ref[rows:] = conv_out[:, part:]
    packed[...] = dot(place[...], both_ref[...]).astype(BF)


def combine_body(cot, place, arrived, grad_half):
    rows, width = cot.shape
    summed = dot(place[...], arrived[...], TN)
    part = width // 2
    for h in range(2):
        lanes = pl.ds(h * part, part)
        grad_half[:, lanes] = (cot[:, lanes].astype(F32) + summed[h * rows : (h + 1) * rows]).astype(BF)


def taps_body(bounds, anchor, low, mid, high, grad_half, taps, pad_ref, ids_ref):
    rows, width = mid.shape
    half = low.shape[0]
    pad_ref[:half] = low[...].astype(F32)
    pad_ref[half : half + rows] = mid[...].astype(F32)
    pad_ref[half + rows :] = high[...].astype(F32)
    stream_ids(bounds, anchor, half, ids_ref)
    for b in range(width // SPAN):
        lanes = pl.ds(b * SPAN, SPAN)
        centre = grad_half[:, lanes].astype(F32)
        for j in range(taps.shape[0]):
            same = same_rows(ids_ref, j, rows, half, SPAN // LANES)
            prod = centre * jnp.where(same, pad_ref[pl.ds(j, rows), lanes], 0.0)
            taps[pl.ds(j, 1), lanes] = jnp.sum(prod, axis=0, keepdims=True)


def back_body(bounds, anchor, low, mid, high, weight, frame_grad, pad_ref, ids_ref):
    rows, width = mid.shape
    half = low.shape[0]
    pad_ref[:half] = low[...].astype(F32)
    pad_ref[half : half + rows] = mid[...].astype(F32)
    pad_ref[half + rows :] = high[...].astype(F32)
    stream_ids(bounds, anchor, half, ids_ref)
    taps = weight.shape[0]
    for b in range(width // SPAN):
        lanes = pl.ds(b * SPAN, SPAN)
        total = conv_sum(pad_ref, ids_ref, weight, 1, rows, half, lanes, lambda i: taps - 1 - i)
        frame_grad[:, lanes] = (pad_ref[pl.ds(half, rows), lanes] + total).astype(BF)


def shards(
    frames,
    cotangent,
    routes,
    stream_lengths,
    conv_weight,
    router_weight,
    gate_weight,
    up_weight,
    down_weight,
):
    row_count = frames.shape[1]
    width = frames.shape[2]
    part = width // 2
    experts = lax.axis_size("seq")
    capacity = 5 * row_count // (2 * experts)
    slots = experts * capacity
    kernel_size = conv_weight.shape[0]
    half = kernel_size // 2
    me_seq = lax.axis_index("seq")
    cot = cotangent[0]
    mid = frames[0]
    low, high = halos(mid, half)
    bounds = stream_lengths[0]
    anchor = (me_seq * row_count)[None].astype(jnp.int32)

    chosen = routes[0]
    labels = jnp.arange(experts, dtype=jnp.int32)
    member = [(chosen[:, k : k + 1] == labels[None, :]) for k in range(2)]
    both = (member[0] | member[1]).astype(BF)
    row_id = jnp.arange(row_count, dtype=jnp.int32)
    earlier = (row_id[:, None] > row_id[None, :]).astype(BF)
    before = dot(earlier, both).astype(jnp.int32)
    slot_of = [
        chosen[:, k] * capacity + jnp.sum(jnp.where(member[k], before, 0), axis=1) for k in range(2)
    ]
    block = -(-2 * capacity // 8) * 8
    packed_id = jnp.arange(experts * block, dtype=jnp.int32)
    inner = packed_id % block
    key = jnp.where(
        inner < 2 * capacity,
        (inner // capacity) * slots + (packed_id // block) * capacity + inner % capacity,
        -1,
    )
    column_key = [jnp.concatenate([s, s + slots]) for s in slot_of]
    place = (
        (key[:, None] == column_key[0][None, :]) | (key[:, None] == column_key[1][None, :])
    ).astype(BF)
    dense = (jnp.arange(2 * slots, dtype=jnp.int32)[:, None] == key[None, :]).astype(BF)

    def over_seq(value):
        cols = value.shape[1]
        return lax.all_to_all(
            value.reshape(experts, block, cols), "seq", split_axis=0, concat_axis=0, tiled=True
        ).reshape(experts * block, cols)

    def halves(value):
        return jnp.concatenate([value[:, :part], value[:, part:]], axis=0)

    def unpack(packed):
        return jnp.concatenate(
            [dot(dense[:slots], packed).astype(BF), dot(dense[slots:], packed).astype(BF)], axis=1
        )

    cot_arrived = over_seq(dot(place, halves(cot)).astype(BF))

    pad_rows = row_count + 2 * half
    pad_scratch = [pltpu.VMEM((pad_rows, width), F32), pltpu.VMEM((pad_rows, LANES), jnp.int32)]
    conv_cost = (6 * kernel_size * row_count * width, 4 << 20)
    conv_out, packed = call(
        conv_body,
        [((row_count, width), BF), ((experts * block, part), BF)],
        pad_scratch + [pltpu.VMEM((2 * row_count, part), BF)],
        *conv_cost,
        smem=2,
    )(bounds, anchor, low, mid, high, conv_weight, place)
    cot_arrived, conv_out = lax.optimization_barrier((cot_arrived, conv_out))
    cot_rows = unpack(cot_arrived)
    rows = unpack(over_seq(packed))

    gate_block, up_block, down_block = gate_weight[0], up_weight[0], down_weight[0]
    column = lax.dynamic_slice_in_dim(router_weight, me_seq, 1, axis=1)
    wide = jnp.broadcast_to(column, (width, LANES))
    column_row = column.astype(F32).T
    hid = gate_block.shape[1]
    expert = call(
        expert_body,
        [((slots, width), BF)] * 4 + [((2 * slots, hid), BF)] * 3 + [((1, width), F32)],
        [pltpu.VMEM((2 * slots, hid), F32)] * 3 + [pltpu.VMEM((2 * slots, LANES), F32)],
        12 * 2 * slots * width * hid,
        12 << 20,
    )

    steps = lax.axis_size("expert") // 2
    results = []

    def chip_sum(step, which, total):
        own, away = results[step][which], results[step][which + 2]
        value = own.astype(F32) + flip(away, "expert", 1).astype(F32)
        if total is not None:
            value = value + total.astype(F32)
        return value.astype(BF)

    cots = [cot_rows, ring_up(cot_rows)]
    cots.append(ring_up(cots[1]))
    rows, cots[2] = lax.optimization_barrier((rows, cots[2]))
    xs = [rows]
    quads = []

    def run(step):
        quad = [xs[step], cots[step], flip(xs[step], "expert", 1), flip(cots[step], "expert", 1)]
        results.append(list(expert(*quad, gate_block, up_block, down_block, wide, column_row)))
        quads.extend(quad)

    total_back = None
    upcoming = ring_up(rows)
    cots.append(ring_up(cots[2]))
    run(0)
    for step in range(1, steps):
        tied = [upcoming, results[step - 1][1], results[step - 1][3]]
        if step == 2:
            tied.append(cots[3])
        if total_back is not None:
            tied.append(total_back)
        tied = list(lax.optimization_barrier(tied))
        upcoming, results[step - 1][1], results[step - 1][3] = tied[:3]
        if step == 2:
            cots[3] = tied[3]
        if total_back is not None:
            total_back = tied[-1]
        xs.append(upcoming)
        if step < steps - 1:
            upcoming = ring_up(upcoming)
        if step > 1:
            total_back = ring_up(chip_sum(step - 1, 1, total_back))
        run(step)
    total_back = ring_up(chip_sum(steps - 1, 1, total_back))

    weight_grads = call(
        grads_body,
        [((width, hid), F32), ((width, hid), F32), ((hid, width), F32)],
        [],
        6 * 8 * slots * width * hid,
        16 << 20,
    )(*quads, *[r[i] for r in results for i in (4, 5, 6)])
    total_back, results[1][0], *weight_grads = lax.optimization_barrier(
        (total_back, results[1][0], *weight_grads)
    )
    gate_grads, up_grads, down_grads = weight_grads
    total_back = chip_sum(0, 1, total_back)
    router_part = sum(r[7] for r in results)
    router_rows = jnp.where(labels[:, None] == me_seq, router_part, 0.0)

    def pack_back(total):
        return over_seq(dot(dense, halves(total), TN).astype(BF))

    arrived = pack_back(total_back)
    total_out = ring_up(chip_sum(1, 0, None))
    total_out = ring_up(chip_sum(2, 0, total_out))
    arrived, total_out = lax.optimization_barrier((arrived, total_out))
    total_out = ring_up(chip_sum(3, 0, total_out))
    (grad_half,) = call(
        combine_body, [((row_count, width), BF)], [], 4 * row_count * experts * block * part, 2 << 20
    )(cot, place, arrived)
    grad_low, grad_high = halos(grad_half, half)
    (taps,) = call(
        taps_body, [((kernel_size, width), F32)], pad_scratch, *conv_cost, smem=2
    )(bounds, anchor, low, mid, high, grad_half)
    taps, grad_low, grad_high, total_out = lax.optimization_barrier(
        (taps, grad_low, grad_high, total_out)
    )
    out_arrived = pack_back(chip_sum(0, 0, total_out))
    (frame_grad,) = call(
        back_body, [((row_count, width), BF)], pad_scratch, *conv_cost, smem=2
    )(bounds, anchor, grad_low, grad_half, grad_high, conv_weight)

    peers = lax.axis_size("expert")
    each = kernel_size // peers
    pieces = jnp.concatenate(
        [taps.reshape(peers, each, width), router_rows.reshape(peers, experts // peers, width)], axis=1
    )
    pieces = lax.all_to_all(pieces, "expert", split_axis=0, concat_axis=0, tiled=True)
    mine = jnp.sum(pieces, axis=0)
    for bit in (2, 4, 8, 16, 1):
        mine = mine + flip(mine, "seq", bit)
    mine, out_arrived, frame_grad = lax.optimization_barrier((mine, out_arrived, frame_grad))
    full = lax.all_to_all(
        jnp.broadcast_to(mine[None], (peers, *mine.shape)), "expert", split_axis=0, concat_axis=0, tiled=True
    )
    conv_grads = full[:, :each].reshape(kernel_size, width)
    router_total = full[:, each:].reshape(experts, width).T

    summed = dot(place, out_arrived, TN)
    out_sum = jnp.concatenate([summed[:row_count], summed[row_count:]], axis=1)
    block_out = (conv_out.astype(F32) + out_sum).astype(BF)
    return (
        block_out[None],
        frame_grad[None],
        conv_grads,
        router_total,
        gate_grads[None],
        up_grads[None],
        down_grads[None],
    )


def solution(mesh):
    in_specs = (
        P("expert", "seq", None),
        P("expert", "seq", None),
        P("expert", "seq", None),
        P("expert", None),
        P(),
        P(),
        P("seq", None, "expert"),
        P("seq", None, "expert"),
        P("seq", "expert", None),
    )
    out_specs = (
        P("expert", "seq", None),
        P("expert", "seq", None),
        P(),
        P(),
        P("seq", None, "expert"),
        P("seq", None, "expert"),
        P("seq", "expert", None),
    )
    return jax.shard_map(shards, mesh=mesh, in_specs=in_specs, out_specs=out_specs, check_vma=False)
```

```python
import jax
import jax.numpy as jnp
from jax import lax
from jax.experimental import pallas as pl
from jax.experimental.pallas import tpu as pltpu
from jax.sharding import PartitionSpec as P

BF = jnp.bfloat16
F32 = jnp.float32
LANES = 128


def flip(value, axis, bit):
    count = lax.axis_size(axis)
    return lax.ppermute(value, axis, [(i, i ^ bit) for i in range(count)])


def ring_up(value):
    count = lax.axis_size("expert")
    return lax.ppermute(value, "expert", [(i, (i + 2) % count) for i in range(count)])


def halos(block, width):
    count = lax.axis_size("seq")
    forward = [(i, i + 1) for i in range(count - 1)]
    backward = [(i + 1, i) for i in range(count - 1)]
    low = lax.ppermute(block[block.shape[0] - width :], "seq", forward)
    high = lax.ppermute(block[:width], "seq", backward)
    return low, high


def dot(a, b, dims=((1,), (0,))):
    return lax.dot_general(a, b, (dims, ((), ())), preferred_element_type=F32)


NT = ((1,), (1,))
TN = ((0,), (0,))


def call(body, outs, scratch, flops, moved, smem=0):
    in_vmem = pl.BlockSpec(memory_space=pltpu.VMEM)

    def run(*args):
        specs = [pl.BlockSpec(memory_space=pltpu.SMEM)] * smem + [in_vmem] * (len(args) - smem)
        return pl.pallas_call(
            body,
            out_shape=[jax.ShapeDtypeStruct(*o) for o in outs],
            in_specs=specs,
            out_specs=[in_vmem] * len(outs),
            scratch_shapes=scratch,
            compiler_params=pltpu.CompilerParams(vmem_limit_bytes=24 * 1024 * 1024),
            cost_estimate=pl.CostEstimate(flops=flops, bytes_accessed=moved, transcendentals=0),
        )(*args)

    return run


def expert_body(
    own, own_c, other, other_c, gate_w, up_w, down_w, wide, column,
    out_own, back_own, out_other, back_other, gate_back, up_back, hidden, router_part,
    gp_ref, up_ref, bb_ref, lg_ref,
):
    slots = own.shape[0]
    hid = gate_w.shape[1]
    repeat = hid // LANES
    for k, (src, cot) in enumerate(((own, own_c), (other, other_c))):
        at = pl.ds(k * slots, slots)
        x = src[...]
        gp_ref[at] = dot(x, gate_w[...])
        up_ref[at] = dot(x, up_w[...])
        bb_ref[at] = dot(cot[...], down_w[...], NT)
        lg_ref[at] = dot(x, wide[...])
    tile = 32

    def step(i, carry):
        at = pl.ds(pl.multiple_of(i * tile, tile), tile)
        gate = jax.nn.sigmoid(lg_ref[at])
        gate_all = jnp.concatenate([gate] * repeat, axis=1)
        gp, up, bb = gp_ref[at], up_ref[at], bb_ref[at]
        sig = jax.nn.sigmoid(gp)
        active = gp * sig
        hid_v = active * up
        terms = hid_v * bb
        row = sum(terms[:, j * LANES : (j + 1) * LANES] for j in range(repeat))
        total = jnp.sum(row, axis=1, keepdims=True)
        lg_ref[at] = total * (gate * (1.0 - gate))
        bh = bb * gate_all
        hidden[at] = (hid_v * gate_all).astype(BF)
        gate_back[at] = (bh * up * (sig * (1.0 + gp * (1.0 - sig)))).astype(BF)
        up_back[at] = (bh * active).astype(BF)
        return carry

    lax.fori_loop(0, 2 * slots // tile, step, 0)
    width = own.shape[1]
    for k, (src, out, back) in enumerate(((own, out_own, back_own), (other, out_other, back_other))):
        at = pl.ds(k * slots, slots)
        out[...] = dot(hidden[at], down_w[...]).astype(BF)
        lg_all = jnp.concatenate([lg_ref[at]] * (width // LANES), axis=1)
        both = dot(gate_back[at], gate_w[...], NT) + dot(up_back[at], up_w[...], NT)
        back[...] = (both + lg_all * column[...]).astype(BF)
    acc = jnp.zeros((8, width), F32)

    def add(i, acc):
        for k, src in enumerate((own, other)):
            at = pl.ds(pl.multiple_of(i * 16, 16), 16)
            here = pl.ds(pl.multiple_of(k * slots + i * 16, 16), 16)
            lg_all = jnp.concatenate([lg_ref[here]] * (width // LANES), axis=1)
            prod = src[at].astype(F32) * lg_all
            acc = acc + prod[:8] + prod[8:]
        return acc

    acc = lax.fori_loop(0, slots // 16, add, acc)
    router_part[...] = jnp.sum(acc, axis=0, keepdims=True)


def grads_body(*refs):
    quads = refs[:16]
    triples = refs[16:28]
    gate_out, up_out, down_out = refs[28:]
    slots = quads[0].shape[0]
    for n in range(4):
        gate_back, up_back, hidden = triples[3 * n : 3 * n + 3]
        for k in range(2):
            x, c = quads[4 * n + 2 * k : 4 * n + 2 * k + 2]
            at = pl.ds(k * slots, slots)
            first = n == 0 and k == 0
            a = dot(x[...], gate_back[at], TN)
            b = dot(x[...], up_back[at], TN)
            d = dot(hidden[at], c[...], TN)
            gate_out[...] = a if first else gate_out[...] + a
            up_out[...] = b if first else up_out[...] + b
            down_out[...] = d if first else down_out[...] + d


def stream_ids(bounds, anchor, half, ids_ref):
    place = anchor[0] - half + lax.broadcasted_iota(jnp.int32, ids_ref.shape, 0)
    total = jnp.zeros(ids_ref.shape, jnp.int32)
    edge = jnp.int32(0)
    for s in range(bounds.shape[0]):
        edge = edge + bounds[s]
        total = total + (place >= edge).astype(jnp.int32)
    ids_ref[...] = total


def same_rows(ids_ref, begin, rows, half, copies):
    same = ids_ref[pl.ds(begin, rows)] == ids_ref[pl.ds(half, rows)]
    return jnp.concatenate([same] * copies, axis=1)


def conv_sum(pad_ref, ids_ref, weight, begin0, rows, half, lanes, order):
    taps = weight.shape[0]
    total = jnp.zeros((rows, lanes.size), F32)
    for i in range(taps):
        begin = begin0 + i
        tap = weight[pl.ds(order(i), 1), lanes]
        same = same_rows(ids_ref, begin, rows, half, lanes.size // LANES)
        total = total + tap * jnp.where(same, pad_ref[pl.ds(begin, rows), lanes], 0.0)
    return total


SPAN = 256


def conv_body(bounds, anchor, low, mid, high, weight, place, conv_out, packed, pad_ref, ids_ref, both_ref):
    rows, width = mid.shape
    part = width // 2
    half = low.shape[0]
    pad_ref[:half] = low[...].astype(F32)
    pad_ref[half : half + rows] = mid[...].astype(F32)
    pad_ref[half + rows :] = high[...].astype(F32)
    stream_ids(bounds, anchor, half, ids_ref)
    for b in range(width // SPAN):
        lanes = pl.ds(b * SPAN, SPAN)
        total = conv_sum(pad_ref, ids_ref, weight, 0, rows, half, lanes, lambda i: i)
        value = (pad_ref[pl.ds(half, rows), lanes] + total).astype(BF)
        conv_out[:, lanes] = value
    both_ref[:rows] = conv_out[:, :part]
    both_ref[rows:] = conv_out[:, part:]
    packed[...] = dot(place[...], both_ref[...]).astype(BF)


def combine_body(cot, place, arrived, grad_half):
    rows, width = cot.shape
    summed = dot(place[...], arrived[...], TN)
    part = width // 2
    for h in range(2):
        lanes = pl.ds(h * part, part)
        grad_half[:, lanes] = (cot[:, lanes].astype(F32) + summed[h * rows : (h + 1) * rows]).astype(BF)


def taps_body(bounds, anchor, low, mid, high, grad_half, taps, pad_ref, ids_ref):
    rows, width = mid.shape
    half = low.shape[0]
    pad_ref[:half] = low[...].astype(F32)
    pad_ref[half : half + rows] = mid[...].astype(F32)
    pad_ref[half + rows :] = high[...].astype(F32)
    stream_ids(bounds, anchor, half, ids_ref)
    for b in range(width // SPAN):
        lanes = pl.ds(b * SPAN, SPAN)
        centre = grad_half[:, lanes].astype(F32)
        for j in range(taps.shape[0]):
            same = same_rows(ids_ref, j, rows, half, SPAN // LANES)
            prod = centre * jnp.where(same, pad_ref[pl.ds(j, rows), lanes], 0.0)
            taps[pl.ds(j, 1), lanes] = jnp.sum(prod, axis=0, keepdims=True)


def back_body(bounds, anchor, low, mid, high, weight, frame_grad, pad_ref, ids_ref):
    rows, width = mid.shape
    half = low.shape[0]
    pad_ref[:half] = low[...].astype(F32)
    pad_ref[half : half + rows] = mid[...].astype(F32)
    pad_ref[half + rows :] = high[...].astype(F32)
    stream_ids(bounds, anchor, half, ids_ref)
    taps = weight.shape[0]
    for b in range(width // SPAN):
        lanes = pl.ds(b * SPAN, SPAN)
        total = conv_sum(pad_ref, ids_ref, weight, 1, rows, half, lanes, lambda i: taps - 1 - i)
        frame_grad[:, lanes] = (pad_ref[pl.ds(half, rows), lanes] + total).astype(BF)


def shards(
    frames,
    cotangent,
    routes,
    stream_lengths,
    conv_weight,
    router_weight,
    gate_weight,
    up_weight,
    down_weight,
):
    row_count = frames.shape[1]
    width = frames.shape[2]
    part = width // 2
    experts = lax.axis_size("seq")
    capacity = 5 * row_count // (2 * experts)
    slots = experts * capacity
    kernel_size = conv_weight.shape[0]
    half = kernel_size // 2
    me_seq = lax.axis_index("seq")
    cot = cotangent[0]
    mid = frames[0]
    low, high = halos(mid, half)
    bounds = stream_lengths[0]
    anchor = (me_seq * row_count)[None].astype(jnp.int32)

    chosen = routes[0]
    labels = jnp.arange(experts, dtype=jnp.int32)
    member = [(chosen[:, k : k + 1] == labels[None, :]) for k in range(2)]
    both = (member[0] | member[1]).astype(BF)
    row_id = jnp.arange(row_count, dtype=jnp.int32)
    earlier = (row_id[:, None] > row_id[None, :]).astype(BF)
    before = dot(earlier, both).astype(jnp.int32)
    slot_of = [
        chosen[:, k] * capacity + jnp.sum(jnp.where(member[k], before, 0), axis=1) for k in range(2)
    ]
    block = -(-2 * capacity // 8) * 8
    packed_id = jnp.arange(experts * block, dtype=jnp.int32)
    inner = packed_id % block
    key = jnp.where(
        inner < 2 * capacity,
        (inner // capacity) * slots + (packed_id // block) * capacity + inner % capacity,
        -1,
    )
    column_key = [jnp.concatenate([s, s + slots]) for s in slot_of]
    place = (
        (key[:, None] == column_key[0][None, :]) | (key[:, None] == column_key[1][None, :])
    ).astype(BF)
    dense = (jnp.arange(2 * slots, dtype=jnp.int32)[:, None] == key[None, :]).astype(BF)

    def over_seq(value):
        cols = value.shape[1]
        return lax.all_to_all(
            value.reshape(experts, block, cols), "seq", split_axis=0, concat_axis=0, tiled=True
        ).reshape(experts * block, cols)

    def halves(value):
        return jnp.concatenate([value[:, :part], value[:, part:]], axis=0)

    def unpack(packed):
        return jnp.concatenate(
            [dot(dense[:slots], packed).astype(BF), dot(dense[slots:], packed).astype(BF)], axis=1
        )

    cot_arrived = over_seq(dot(place, halves(cot)).astype(BF))

    pad_rows = row_count + 2 * half
    pad_scratch = [pltpu.VMEM((pad_rows, width), F32), pltpu.VMEM((pad_rows, LANES), jnp.int32)]
    conv_cost = (6 * kernel_size * row_count * width, 4 << 20)
    conv_out, packed = call(
        conv_body,
        [((row_count, width), BF), ((experts * block, part), BF)],
        pad_scratch + [pltpu.VMEM((2 * row_count, part), BF)],
        *conv_cost,
        smem=2,
    )(bounds, anchor, low, mid, high, conv_weight, place)
    cot_rows, packed = lax.optimization_barrier((unpack(cot_arrived), packed))
    rows = unpack(over_seq(packed))

    gate_block, up_block, down_block = gate_weight[0], up_weight[0], down_weight[0]
    column = lax.dynamic_slice_in_dim(router_weight, me_seq, 1, axis=1)
    wide = jnp.broadcast_to(column, (width, LANES))
    column_row = column.astype(F32).T
    hid = gate_block.shape[1]
    expert = call(
        expert_body,
        [((slots, width), BF)] * 4 + [((2 * slots, hid), BF)] * 3 + [((1, width), F32)],
        [pltpu.VMEM((2 * slots, hid), F32)] * 3 + [pltpu.VMEM((2 * slots, LANES), F32)],
        12 * 2 * slots * width * hid,
        12 << 20,
    )

    steps = lax.axis_size("expert") // 2
    results = []

    def chip_sum(step, which, total):
        own, away = results[step][which], results[step][which + 2]
        value = own.astype(F32) + flip(away, "expert", 1).astype(F32)
        if total is not None:
            value = value + total.astype(F32)
        return value.astype(BF)

    cots = [cot_rows, ring_up(cot_rows)]
    cots.append(ring_up(cots[1]))
    rows, cots[2] = lax.optimization_barrier((rows, cots[2]))
    xs = [rows]
    quads = []

    def run(step):
        quad = [xs[step], cots[step], flip(xs[step], "expert", 1), flip(cots[step], "expert", 1)]
        results.append(list(expert(*quad, gate_block, up_block, down_block, wide, column_row)))
        quads.extend(quad)

    total_back = None
    upcoming = ring_up(rows)
    cots.append(ring_up(cots[2]))
    run(0)
    for step in range(1, steps):
        tied = [upcoming, results[step - 1][1], results[step - 1][3]]
        if step == 2:
            tied.append(cots[3])
        if total_back is not None:
            tied.append(total_back)
        tied = list(lax.optimization_barrier(tied))
        upcoming, results[step - 1][1], results[step - 1][3] = tied[:3]
        if step == 2:
            cots[3] = tied[3]
        if total_back is not None:
            total_back = tied[-1]
        xs.append(upcoming)
        if step < steps - 1:
            upcoming = ring_up(upcoming)
        if step > 1:
            total_back = ring_up(chip_sum(step - 1, 1, total_back))
        run(step)
    total_back = ring_up(chip_sum(steps - 1, 1, total_back))

    weight_grads = call(
        grads_body,
        [((width, hid), F32), ((width, hid), F32), ((hid, width), F32)],
        [],
        6 * 8 * slots * width * hid,
        16 << 20,
    )(*quads, *[r[i] for r in results for i in (4, 5, 6)])
    total_back, results[1][0], *weight_grads = lax.optimization_barrier(
        (total_back, results[1][0], *weight_grads)
    )
    gate_grads, up_grads, down_grads = weight_grads
    total_back = chip_sum(0, 1, total_back)
    router_part = sum(r[7] for r in results)
    router_rows = jnp.where(labels[:, None] == me_seq, router_part, 0.0)

    def pack_back(total):
        return over_seq(dot(dense, halves(total), TN).astype(BF))

    arrived = pack_back(total_back)
    total_out = ring_up(chip_sum(1, 0, None))
    total_out = ring_up(chip_sum(2, 0, total_out))
    arrived, total_out = lax.optimization_barrier((arrived, total_out))
    total_out = ring_up(chip_sum(3, 0, total_out))
    (grad_half,) = call(
        combine_body, [((row_count, width), BF)], [], 4 * row_count * experts * block * part, 2 << 20
    )(cot, place, arrived)
    (taps,) = call(
        taps_body, [((kernel_size, width), F32)], pad_scratch, *conv_cost, smem=2
    )(bounds, anchor, low, mid, high, grad_half)
    taps, grad_half = lax.optimization_barrier((taps, grad_half))
    grad_low, grad_high = halos(grad_half, half)
    peers = lax.axis_size("expert")
    each = kernel_size // peers
    pieces = jnp.concatenate(
        [taps.reshape(peers, each, width), router_rows.reshape(peers, experts // peers, width)], axis=1
    )
    pieces = lax.all_to_all(pieces, "expert", split_axis=0, concat_axis=0, tiled=True)
    pieces, grad_low, grad_high, total_out = lax.optimization_barrier(
        (pieces, grad_low, grad_high, total_out)
    )
    out_arrived = pack_back(chip_sum(0, 0, total_out))
    (frame_grad,) = call(
        back_body, [((row_count, width), BF)], pad_scratch, *conv_cost, smem=2
    )(bounds, anchor, grad_low, grad_half, grad_high, conv_weight)
    mine = jnp.sum(pieces, axis=0)
    for bit in (2, 4, 8, 16, 1):
        mine = mine + flip(mine, "seq", bit)
    mine, out_arrived, frame_grad = lax.optimization_barrier((mine, out_arrived, frame_grad))
    full = lax.all_to_all(
        jnp.broadcast_to(mine[None], (peers, *mine.shape)), "expert", split_axis=0, concat_axis=0, tiled=True
    )
    conv_grads = full[:, :each].reshape(kernel_size, width)
    router_total = full[:, each:].reshape(experts, width).T

    summed = dot(place, out_arrived, TN)
    out_sum = jnp.concatenate([summed[:row_count], summed[row_count:]], axis=1)
    block_out = (conv_out.astype(F32) + out_sum).astype(BF)
    return (
        block_out[None],
        frame_grad[None],
        conv_grads,
        router_total,
        gate_grads[None],
        up_grads[None],
        down_grads[None],
    )


def solution(mesh):
    in_specs = (
        P("expert", "seq", None),
        P("expert", "seq", None),
        P("expert", "seq", None),
        P("expert", None),
        P(),
        P(),
        P("seq", None, "expert"),
        P("seq", None, "expert"),
        P("seq", "expert", None),
    )
    out_specs = (
        P("expert", "seq", None),
        P("expert", "seq", None),
        P(),
        P(),
        P("seq", None, "expert"),
        P("seq", None, "expert"),
        P("seq", "expert", None),
    )
    return jax.shard_map(shards, mesh=mesh, in_specs=in_specs, out_specs=out_specs, check_vma=False)
```

```python
import jax
import jax.numpy as jnp
from jax import lax
from jax.experimental import pallas as pl
from jax.experimental.pallas import tpu as pltpu
from jax.sharding import PartitionSpec as P

BF = jnp.bfloat16
F32 = jnp.float32
LANES = 128


def flip(value, axis, bit):
    count = lax.axis_size(axis)
    return lax.ppermute(value, axis, [(i, i ^ bit) for i in range(count)])


def halos(block, width):
    count = lax.axis_size("seq")
    forward = [(i, i + 1) for i in range(count - 1)]
    backward = [(i + 1, i) for i in range(count - 1)]
    low = lax.ppermute(block[block.shape[0] - width :], "seq", forward)
    high = lax.ppermute(block[:width], "seq", backward)
    return low, high


def dot(a, b, dims=((1,), (0,))):
    return lax.dot_general(a, b, (dims, ((), ())), preferred_element_type=F32)


NT = ((1,), (1,))
TN = ((0,), (0,))


def call(body, outs, scratch, flops, moved, smem=0):
    in_vmem = pl.BlockSpec(memory_space=pltpu.VMEM)

    def run(*args):
        specs = [pl.BlockSpec(memory_space=pltpu.SMEM)] * smem + [in_vmem] * (len(args) - smem)
        return pl.pallas_call(
            body,
            out_shape=[jax.ShapeDtypeStruct(*o) for o in outs],
            in_specs=specs,
            out_specs=[in_vmem] * len(outs),
            scratch_shapes=scratch,
            compiler_params=pltpu.CompilerParams(vmem_limit_bytes=32 * 1024 * 1024),
            cost_estimate=pl.CostEstimate(flops=flops, bytes_accessed=moved, transcendentals=0),
        )(*args)

    return run


def expert_body(
    own, own_c, other, other_c, gate_a, up_a, down_a, gate_b, up_b, down_b, wide, column,
    out_own, back_own, out_other, back_other, gate_back, up_back, hidden, router_part,
    gp_ref, up_ref, bb_ref, lg_ref,
):
    slots, width = own.shape
    hid = gate_a.shape[1]
    repeat = 2 * hid // LANES
    sets = ((gate_a, up_a, down_a, pl.ds(0, hid)), (gate_b, up_b, down_b, pl.ds(hid, hid)))
    for k, (src, cot) in enumerate(((own, own_c), (other, other_c))):
        at = pl.ds(k * slots, slots)
        x = src[...]
        for gate_w, up_w, down_w, cols in sets:
            gp_ref[at, cols] = dot(x, gate_w[...])
            up_ref[at, cols] = dot(x, up_w[...])
            bb_ref[at, cols] = dot(cot[...], down_w[...], NT)
        lg_ref[at] = dot(x, wide[...])
    tile = 16

    def step(i, carry):
        at = pl.ds(pl.multiple_of(i * tile, tile), tile)
        gate = jax.nn.sigmoid(lg_ref[at])
        gate_all = jnp.concatenate([gate] * repeat, axis=1)
        gp, up, bb = gp_ref[at], up_ref[at], bb_ref[at]
        sig = jax.nn.sigmoid(gp)
        active = gp * sig
        hid_v = active * up
        terms = hid_v * bb
        row = sum(terms[:, j * LANES : (j + 1) * LANES] for j in range(repeat))
        total = jnp.sum(row, axis=1, keepdims=True)
        lg_ref[at] = total * (gate * (1.0 - gate))
        bh = bb * gate_all
        hidden[at] = (hid_v * gate_all).astype(BF)
        gate_back[at] = (bh * up * (sig * (1.0 + gp * (1.0 - sig)))).astype(BF)
        up_back[at] = (bh * active).astype(BF)
        return carry

    lax.fori_loop(0, 2 * slots // tile, step, 0)
    for k, (out, back) in enumerate(((out_own, back_own), (out_other, back_other))):
        at = pl.ds(k * slots, slots)
        lg_all = jnp.concatenate([lg_ref[at]] * (width // LANES), axis=1)
        forth = 0.0
        both = lg_all * column[...]
        for gate_w, up_w, down_w, cols in sets:
            forth = forth + dot(hidden[at, cols], down_w[...])
            both = both + dot(gate_back[at, cols], gate_w[...], NT) + dot(up_back[at, cols], up_w[...], NT)
        out[...] = forth.astype(BF)
        back[...] = both.astype(BF)
    acc = jnp.zeros((8, width), F32)

    def add(i, acc):
        for k, src in enumerate((own, other)):
            at = pl.ds(pl.multiple_of(i * 16, 16), 16)
            here = pl.ds(pl.multiple_of(k * slots + i * 16, 16), 16)
            lg_all = jnp.concatenate([lg_ref[here]] * (width // LANES), axis=1)
            prod = src[at].astype(F32) * lg_all
            acc = acc + prod[:8] + prod[8:]
        return acc

    acc = lax.fori_loop(0, slots // 16, add, acc)
    router_part[...] = jnp.sum(acc, axis=0, keepdims=True)


def grads_body(*refs):
    quads, triples, outs = refs[:8], refs[8:14], refs[14:]
    slots = quads[0].shape[0]
    hid = outs[0].shape[1]
    for part in range(2):
        cols = pl.ds(part * hid, hid)
        gate_out, up_out, down_out = outs[3 * part : 3 * part + 3]
        a = b = d = 0.0
        for n in range(2):
            gate_back, up_back, hidden = triples[3 * n : 3 * n + 3]
            for k in range(2):
                x, c = quads[4 * n + 2 * k : 4 * n + 2 * k + 2]
                at = pl.ds(k * slots, slots)
                a = a + dot(x[...], gate_back[at, cols], TN)
                b = b + dot(x[...], up_back[at, cols], TN)
                d = d + dot(hidden[at, cols], c[...], TN)
        gate_out[...] = a.astype(gate_out.dtype)
        up_out[...] = b.astype(up_out.dtype)
        down_out[...] = d.astype(down_out.dtype)


def stream_ids(bounds, anchor, half, ids_ref):
    place = anchor[0] - half + lax.broadcasted_iota(jnp.int32, ids_ref.shape, 0)
    total = jnp.zeros(ids_ref.shape, jnp.int32)
    edge = jnp.int32(0)
    for s in range(bounds.shape[0]):
        edge = edge + bounds[s]
        total = total + (place >= edge).astype(jnp.int32)
    ids_ref[...] = total


def same_rows(ids_ref, begin, rows, half, copies):
    same = ids_ref[pl.ds(begin, rows)] == ids_ref[pl.ds(half, rows)]
    return jnp.concatenate([same] * copies, axis=1)


def conv_sum(pad_ref, ids_ref, weight, begin0, rows, half, lanes, order):
    taps = weight.shape[0]
    total = jnp.zeros((rows, lanes.size), F32)
    for i in range(taps):
        begin = begin0 + i
        tap = weight[pl.ds(order(i), 1), lanes]
        same = same_rows(ids_ref, begin, rows, half, lanes.size // LANES)
        total = total + tap * jnp.where(same, pad_ref[pl.ds(begin, rows), lanes], 0.0)
    return total


SPAN = 256


def conv_body(bounds, anchor, low, mid, high, weight, place, conv_out, packed, pad_ref, ids_ref, both_ref):
    rows, width = mid.shape
    part = width // 2
    half = low.shape[0]
    pad_ref[:half] = low[...].astype(F32)
    pad_ref[half : half + rows] = mid[...].astype(F32)
    pad_ref[half + rows :] = high[...].astype(F32)
    stream_ids(bounds, anchor, half, ids_ref)
    for b in range(width // SPAN):
        lanes = pl.ds(b * SPAN, SPAN)
        total = conv_sum(pad_ref, ids_ref, weight, 0, rows, half, lanes, lambda i: i)
        value = (pad_ref[pl.ds(half, rows), lanes] + total).astype(BF)
        conv_out[:, lanes] = value
    both_ref[:rows] = conv_out[:, :part]
    both_ref[rows:] = conv_out[:, part:]
    packed[...] = dot(place[...], both_ref[...]).astype(BF)


def combine_body(cot, place, arrived, grad_half):
    rows, width = cot.shape
    summed = dot(place[...], arrived[...], TN)
    part = width // 2
    for h in range(2):
        lanes = pl.ds(h * part, part)
        grad_half[:, lanes] = (cot[:, lanes].astype(F32) + summed[h * rows : (h + 1) * rows]).astype(BF)


def taps_body(bounds, anchor, low, mid, high, grad_half, taps, pad_ref, ids_ref):
    rows, width = mid.shape
    half = low.shape[0]
    pad_ref[:half] = low[...].astype(F32)
    pad_ref[half : half + rows] = mid[...].astype(F32)
    pad_ref[half + rows :] = high[...].astype(F32)
    stream_ids(bounds, anchor, half, ids_ref)
    for b in range(width // SPAN):
        lanes = pl.ds(b * SPAN, SPAN)
        centre = grad_half[:, lanes].astype(F32)
        for j in range(taps.shape[0]):
            same = same_rows(ids_ref, j, rows, half, SPAN // LANES)
            prod = centre * jnp.where(same, pad_ref[pl.ds(j, rows), lanes], 0.0)
            taps[pl.ds(j, 1), lanes] = jnp.sum(prod, axis=0, keepdims=True)


def back_body(bounds, anchor, low, mid, high, weight, frame_grad, pad_ref, ids_ref):
    rows, width = mid.shape
    half = low.shape[0]
    pad_ref[:half] = low[...].astype(F32)
    pad_ref[half : half + rows] = mid[...].astype(F32)
    pad_ref[half + rows :] = high[...].astype(F32)
    stream_ids(bounds, anchor, half, ids_ref)
    taps = weight.shape[0]
    for b in range(width // SPAN):
        lanes = pl.ds(b * SPAN, SPAN)
        total = conv_sum(pad_ref, ids_ref, weight, 1, rows, half, lanes, lambda i: taps - 1 - i)
        frame_grad[:, lanes] = (pad_ref[pl.ds(half, rows), lanes] + total).astype(BF)


def shards(
    frames,
    cotangent,
    routes,
    stream_lengths,
    conv_weight,
    router_weight,
    gate_weight,
    up_weight,
    down_weight,
):
    row_count = frames.shape[1]
    width = frames.shape[2]
    part = width // 2
    experts = lax.axis_size("seq")
    capacity = 5 * row_count // (2 * experts)
    slots = experts * capacity
    kernel_size = conv_weight.shape[0]
    half = kernel_size // 2
    me_seq = lax.axis_index("seq")
    cot = cotangent[0]
    mid = frames[0]
    low, high = halos(mid, half)
    bounds = stream_lengths[0]
    anchor = (me_seq * row_count)[None].astype(jnp.int32)

    chosen = routes[0]
    labels = jnp.arange(experts, dtype=jnp.int32)
    member = [(chosen[:, k : k + 1] == labels[None, :]) for k in range(2)]
    both = (member[0] | member[1]).astype(BF)
    row_id = jnp.arange(row_count, dtype=jnp.int32)
    earlier = (row_id[:, None] > row_id[None, :]).astype(BF)
    before = dot(earlier, both).astype(jnp.int32)
    slot_of = [
        chosen[:, k] * capacity + jnp.sum(jnp.where(member[k], before, 0), axis=1) for k in range(2)
    ]
    block = -(-2 * capacity // 8) * 8
    packed_id = jnp.arange(experts * block, dtype=jnp.int32)
    inner = packed_id % block
    key = jnp.where(
        inner < 2 * capacity,
        (inner // capacity) * slots + (packed_id // block) * capacity + inner % capacity,
        -1,
    )
    column_key = [jnp.concatenate([s, s + slots]) for s in slot_of]
    place = (
        (key[:, None] == column_key[0][None, :]) | (key[:, None] == column_key[1][None, :])
    ).astype(BF)
    dense = (jnp.arange(2 * slots, dtype=jnp.int32)[:, None] == key[None, :]).astype(BF)

    def over_seq(value):
        cols = value.shape[1]
        return lax.all_to_all(
            value.reshape(experts, block, cols), "seq", split_axis=0, concat_axis=0, tiled=True
        ).reshape(experts * block, cols)

    def halves(value):
        return jnp.concatenate([value[:, :part], value[:, part:]], axis=0)

    def unpack(packed):
        return jnp.concatenate(
            [dot(dense[:slots], packed).astype(BF), dot(dense[slots:], packed).astype(BF)], axis=1
        )

    cot_arrived = over_seq(dot(place, halves(cot)).astype(BF))

    pad_rows = row_count + 2 * half
    pad_scratch = [pltpu.VMEM((pad_rows, width), F32), pltpu.VMEM((pad_rows, LANES), jnp.int32)]
    conv_cost = (6 * kernel_size * row_count * width, 4 << 20)
    conv_out, packed = call(
        conv_body,
        [((row_count, width), BF), ((experts * block, part), BF)],
        pad_scratch + [pltpu.VMEM((2 * row_count, part), BF)],
        *conv_cost,
        smem=2,
    )(bounds, anchor, low, mid, high, conv_weight, place)
    weights = [gate_weight[0], up_weight[0], down_weight[0]]
    cot_arrived, *swapped = lax.optimization_barrier(
        (cot_arrived, *[flip(w, "expert", 2) for w in weights])
    )
    weights = weights + swapped
    cot_rows = unpack(cot_arrived)
    rows = unpack(over_seq(packed))

    column = lax.dynamic_slice_in_dim(router_weight, me_seq, 1, axis=1)
    wide = jnp.broadcast_to(column, (width, LANES))
    column_row = column.astype(F32).T
    hid = weights[0].shape[1]
    expert = call(
        expert_body,
        [((slots, width), BF)] * 4 + [((2 * slots, 2 * hid), BF)] * 3 + [((1, width), F32)],
        [pltpu.VMEM((2 * slots, 2 * hid), F32)] * 3 + [pltpu.VMEM((2 * slots, LANES), F32)],
        24 * 2 * slots * width * hid,
        16 << 20,
    )

    def run(rows, cots):
        quad = [rows, cots, flip(rows, "expert", 1), flip(cots, "expert", 1)]
        return quad, list(expert(*quad, *weights, wide, column_row))

    def chip_sum(result, which, total=None):
        value = result[which].astype(F32) + flip(result[which + 2], "expert", 1).astype(F32)
        if total is not None:
            value = value + total.astype(F32)
        return value.astype(BF)

    far_cots = flip(cot_rows, "expert", 4)
    rows, far_cots = lax.optimization_barrier((rows, far_cots))
    far_rows = flip(rows, "expert", 4)
    quad, near = run(rows, cot_rows)
    far_rows, near[1], near[3] = lax.optimization_barrier((far_rows, near[1], near[3]))
    far_quad, far = run(far_rows, far_cots)
    total_back = flip(chip_sum(far, 1), "expert", 4)
    weight_grads = call(
        grads_body,
        [(w.shape, d) for d in (F32, BF) for w in weights[:3]],
        [],
        48 * 2 * slots * width * hid // 2,
        20 << 20,
    )(*quad, *far_quad, *near[4:7], *far[4:7])
    total_back, far[0], *weight_grads = lax.optimization_barrier((total_back, far[0], *weight_grads))
    total_back = chip_sum(near, 1, total_back)
    results = [near, far]

    router_part = sum(r[7] for r in results)
    router_rows = jnp.where(labels[:, None] == me_seq, router_part, 0.0)

    def pack_back(total):
        return over_seq(dot(dense, halves(total), TN).astype(BF))

    arrived = pack_back(total_back)
    total_out = flip(chip_sum(far, 0), "expert", 4)
    arrived, total_out = lax.optimization_barrier((arrived, total_out))
    returned = [flip(w, "expert", 2) for w in weight_grads[3:]]
    (grad_half,) = call(
        combine_body, [((row_count, width), BF)], [], 4 * row_count * experts * block * part, 2 << 20
    )(cot, place, arrived)
    (taps,) = call(
        taps_body, [((kernel_size, width), F32)], pad_scratch, *conv_cost, smem=2
    )(bounds, anchor, low, mid, high, grad_half)
    taps, grad_half = lax.optimization_barrier((taps, grad_half))
    grad_low, grad_high = halos(grad_half, half)
    peers = lax.axis_size("expert")
    each = kernel_size // peers
    pieces = jnp.concatenate(
        [taps.reshape(peers, each, width), router_rows.reshape(peers, experts // peers, width)], axis=1
    )
    pieces = lax.all_to_all(pieces, "expert", split_axis=0, concat_axis=0, tiled=True)
    pieces, grad_low, grad_high, returned[0] = lax.optimization_barrier(
        (pieces, grad_low, grad_high, returned[0])
    )
    out_arrived = pack_back(chip_sum(near, 0, total_out))
    (frame_grad,) = call(
        back_body, [((row_count, width), BF)], pad_scratch, *conv_cost, smem=2
    )(bounds, anchor, grad_low, grad_half, grad_high, conv_weight)
    mine = jnp.sum(pieces, axis=0)
    for bit in (2, 4, 8, 16, 1):
        if bit == 8:
            mine, returned[1] = lax.optimization_barrier((mine, returned[1]))
        mine = mine + flip(mine, "seq", bit)
    mine, out_arrived, frame_grad, returned[2] = lax.optimization_barrier(
        (mine, out_arrived, frame_grad, returned[2])
    )
    gate_grads, up_grads, down_grads = [
        own + far_part.astype(F32) for own, far_part in zip(weight_grads, returned)
    ]
    full = lax.all_to_all(
        jnp.broadcast_to(mine[None], (peers, *mine.shape)), "expert", split_axis=0, concat_axis=0, tiled=True
    )
    conv_grads = full[:, :each].reshape(kernel_size, width)
    router_total = full[:, each:].reshape(experts, width).T

    summed = dot(place, out_arrived, TN)
    out_sum = jnp.concatenate([summed[:row_count], summed[row_count:]], axis=1)
    block_out = (conv_out.astype(F32) + out_sum).astype(BF)
    return (
        block_out[None],
        frame_grad[None],
        conv_grads,
        router_total,
        gate_grads[None],
        up_grads[None],
        down_grads[None],
    )


def solution(mesh):
    in_specs = (
        P("expert", "seq", None),
        P("expert", "seq", None),
        P("expert", "seq", None),
        P("expert", None),
        P(),
        P(),
        P("seq", None, "expert"),
        P("seq", None, "expert"),
        P("seq", "expert", None),
    )
    out_specs = (
        P("expert", "seq", None),
        P("expert", "seq", None),
        P(),
        P(),
        P("seq", None, "expert"),
        P("seq", None, "expert"),
        P("seq", "expert", None),
    )
    return jax.shard_map(shards, mesh=mesh, in_specs=in_specs, out_specs=out_specs, check_vma=False)
```

```python
import jax
import jax.numpy as jnp
from jax import lax
from jax.experimental import pallas as pl
from jax.experimental.pallas import tpu as pltpu
from jax.sharding import PartitionSpec as P

BF = jnp.bfloat16
F32 = jnp.float32
LANES = 128


def flip(value, axis, bit):
    count = lax.axis_size(axis)
    return lax.ppermute(value, axis, [(i, i ^ bit) for i in range(count)])


def halos(block, width):
    count = lax.axis_size("seq")
    forward = [(i, i + 1) for i in range(count - 1)]
    backward = [(i + 1, i) for i in range(count - 1)]
    low = lax.ppermute(block[block.shape[0] - width :], "seq", forward)
    high = lax.ppermute(block[:width], "seq", backward)
    return low, high


def dot(a, b, dims=((1,), (0,))):
    return lax.dot_general(a, b, (dims, ((), ())), preferred_element_type=F32)


NT = ((1,), (1,))
TN = ((0,), (0,))


def call(body, outs, scratch, flops, moved, smem=0):
    in_vmem = pl.BlockSpec(memory_space=pltpu.VMEM)

    def run(*args):
        specs = [pl.BlockSpec(memory_space=pltpu.SMEM)] * smem + [in_vmem] * (len(args) - smem)
        return pl.pallas_call(
            body,
            out_shape=[jax.ShapeDtypeStruct(*o) for o in outs],
            in_specs=specs,
            out_specs=[in_vmem] * len(outs),
            scratch_shapes=scratch,
            compiler_params=pltpu.CompilerParams(vmem_limit_bytes=32 * 1024 * 1024),
            cost_estimate=pl.CostEstimate(flops=flops, bytes_accessed=moved, transcendentals=0),
        )(*args)

    return run


def expert_body(
    own, own_c, other, other_c, gate_a, up_a, down_a, gate_b, up_b, down_b, wide, column,
    out_own, back_own, out_other, back_other, gate_back, up_back, hidden, router_part,
    gp_ref, up_ref, bb_ref, lg_ref,
):
    slots, width = own.shape
    hid = gate_a.shape[1]
    repeat = 2 * hid // LANES
    sets = ((gate_a, up_a, down_a, pl.ds(0, hid)), (gate_b, up_b, down_b, pl.ds(hid, hid)))
    for k, (src, cot) in enumerate(((own, own_c), (other, other_c))):
        at = pl.ds(k * slots, slots)
        x = src[...]
        for gate_w, up_w, down_w, cols in sets:
            gp_ref[at, cols] = dot(x, gate_w[...])
            up_ref[at, cols] = dot(x, up_w[...])
            bb_ref[at, cols] = dot(cot[...], down_w[...], NT)
        lg_ref[at] = dot(x, wide[...])
    tile = 16

    def step(i, carry):
        at = pl.ds(pl.multiple_of(i * tile, tile), tile)
        gate = jax.nn.sigmoid(lg_ref[at])
        gate_all = jnp.concatenate([gate] * repeat, axis=1)
        gp, up, bb = gp_ref[at], up_ref[at], bb_ref[at]
        sig = jax.nn.sigmoid(gp)
        active = gp * sig
        hid_v = active * up
        terms = hid_v * bb
        row = sum(terms[:, j * LANES : (j + 1) * LANES] for j in range(repeat))
        total = jnp.sum(row, axis=1, keepdims=True)
        lg_ref[at] = total * (gate * (1.0 - gate))
        bh = bb * gate_all
        hidden[at] = (hid_v * gate_all).astype(BF)
        gate_back[at] = (bh * up * (sig * (1.0 + gp * (1.0 - sig)))).astype(BF)
        up_back[at] = (bh * active).astype(BF)
        return carry

    lax.fori_loop(0, 2 * slots // tile, step, 0)
    for k, (out, back) in enumerate(((out_own, back_own), (out_other, back_other))):
        at = pl.ds(k * slots, slots)
        lg_all = jnp.concatenate([lg_ref[at]] * (width // LANES), axis=1)
        forth = 0.0
        both = lg_all * column[...]
        for gate_w, up_w, down_w, cols in sets:
            forth = forth + dot(hidden[at, cols], down_w[...])
            both = both + dot(gate_back[at, cols], gate_w[...], NT) + dot(up_back[at, cols], up_w[...], NT)
        out[...] = forth.astype(BF)
        back[...] = both.astype(BF)
    acc = jnp.zeros((8, width), F32)

    def add(i, acc):
        for k, src in enumerate((own, other)):
            at = pl.ds(pl.multiple_of(i * 16, 16), 16)
            here = pl.ds(pl.multiple_of(k * slots + i * 16, 16), 16)
            lg_all = jnp.concatenate([lg_ref[here]] * (width // LANES), axis=1)
            prod = src[at].astype(F32) * lg_all
            acc = acc + prod[:8] + prod[8:]
        return acc

    acc = lax.fori_loop(0, slots // 16, add, acc)
    router_part[...] = jnp.sum(acc, axis=0, keepdims=True)


def grads_body(*refs):
    quads, triples, outs = refs[:8], refs[8:14], refs[14:]
    slots = quads[0].shape[0]
    hid = outs[0].shape[1]
    for part in range(2):
        cols = pl.ds(part * hid, hid)
        gate_out, up_out, down_out = outs[3 * part : 3 * part + 3]
        a = b = d = 0.0
        for n in range(2):
            gate_back, up_back, hidden = triples[3 * n : 3 * n + 3]
            for k in range(2):
                x, c = quads[4 * n + 2 * k : 4 * n + 2 * k + 2]
                at = pl.ds(k * slots, slots)
                a = a + dot(x[...], gate_back[at, cols], TN)
                b = b + dot(x[...], up_back[at, cols], TN)
                d = d + dot(hidden[at, cols], c[...], TN)
        gate_out[...] = a.astype(gate_out.dtype)
        up_out[...] = b.astype(up_out.dtype)
        down_out[...] = d.astype(down_out.dtype)


def stream_ids(bounds, anchor, half, ids_ref):
    place = anchor[0] - half + lax.broadcasted_iota(jnp.int32, ids_ref.shape, 0)
    total = jnp.zeros(ids_ref.shape, jnp.int32)
    edge = jnp.int32(0)
    for s in range(bounds.shape[0]):
        edge = edge + bounds[s]
        total = total + (place >= edge).astype(jnp.int32)
    ids_ref[...] = total


def same_rows(ids_ref, begin, rows, half, copies):
    same = ids_ref[pl.ds(begin, rows)] == ids_ref[pl.ds(half, rows)]
    return jnp.concatenate([same] * copies, axis=1)


def conv_sum(pad_ref, ids_ref, weight, begin0, rows, half, lanes, order):
    taps = weight.shape[0]
    total = jnp.zeros((rows, lanes.size), F32)
    for i in range(taps):
        begin = begin0 + i
        tap = weight[pl.ds(order(i), 1), lanes]
        same = same_rows(ids_ref, begin, rows, half, lanes.size // LANES)
        total = total + tap * jnp.where(same, pad_ref[pl.ds(begin, rows), lanes], 0.0)
    return total


SPAN = 256


def conv_body(bounds, anchor, low, mid, high, cot, weight, place, conv_out, packed, pad_ref, ids_ref, both_ref):
    rows, width = mid.shape
    half = low.shape[0]
    pad_ref[:half] = low[...].astype(F32)
    pad_ref[half : half + rows] = mid[...].astype(F32)
    pad_ref[half + rows :] = high[...].astype(F32)
    stream_ids(bounds, anchor, half, ids_ref)
    for b in range(width // SPAN):
        lanes = pl.ds(b * SPAN, SPAN)
        total = conv_sum(pad_ref, ids_ref, weight, 0, rows, half, lanes, lambda i: i)
        value = (pad_ref[pl.ds(half, rows), lanes] + total).astype(BF)
        conv_out[:, lanes] = value
        both_ref[:rows, lanes] = value
    both_ref[rows:] = cot[...]
    packed[...] = dot(place[...], both_ref[...]).astype(BF)


def combine_body(conv_out, cot, place, arrived, block_out, grad_half):
    rows = cot.shape[0]
    summed = dot(place[...], arrived[...], TN)
    block_out[...] = (conv_out[...].astype(F32) + summed[:rows]).astype(BF)
    grad_half[...] = (cot[...].astype(F32) + summed[rows:]).astype(BF)


def taps_body(bounds, anchor, low, mid, high, grad_half, taps, pad_ref, ids_ref):
    rows, width = mid.shape
    half = low.shape[0]
    pad_ref[:half] = low[...].astype(F32)
    pad_ref[half : half + rows] = mid[...].astype(F32)
    pad_ref[half + rows :] = high[...].astype(F32)
    stream_ids(bounds, anchor, half, ids_ref)
    for b in range(width // SPAN):
        lanes = pl.ds(b * SPAN, SPAN)
        centre = grad_half[:, lanes].astype(F32)
        for j in range(taps.shape[0]):
            same = same_rows(ids_ref, j, rows, half, SPAN // LANES)
            prod = centre * jnp.where(same, pad_ref[pl.ds(j, rows), lanes], 0.0)
            taps[pl.ds(j, 1), lanes] = jnp.sum(prod, axis=0, keepdims=True)


def back_body(bounds, anchor, low, mid, high, weight, frame_grad, pad_ref, ids_ref):
    rows, width = mid.shape
    half = low.shape[0]
    pad_ref[:half] = low[...].astype(F32)
    pad_ref[half : half + rows] = mid[...].astype(F32)
    pad_ref[half + rows :] = high[...].astype(F32)
    stream_ids(bounds, anchor, half, ids_ref)
    taps = weight.shape[0]
    for b in range(width // SPAN):
        lanes = pl.ds(b * SPAN, SPAN)
        total = conv_sum(pad_ref, ids_ref, weight, 1, rows, half, lanes, lambda i: taps - 1 - i)
        frame_grad[:, lanes] = (pad_ref[pl.ds(half, rows), lanes] + total).astype(BF)


def shards(
    frames,
    cotangent,
    routes,
    stream_lengths,
    conv_weight,
    router_weight,
    gate_weight,
    up_weight,
    down_weight,
):
    row_count = frames.shape[1]
    width = frames.shape[2]
    experts = lax.axis_size("seq")
    capacity = 5 * row_count // (2 * experts)
    slots = experts * capacity
    kernel_size = conv_weight.shape[0]
    half = kernel_size // 2
    me_seq = lax.axis_index("seq")
    cot = cotangent[0]
    mid = frames[0]
    low, high = halos(mid, half)
    bounds = stream_lengths[0]
    anchor = (me_seq * row_count)[None].astype(jnp.int32)

    chosen = routes[0]
    labels = jnp.arange(experts, dtype=jnp.int32)
    member = [(chosen[:, k : k + 1] == labels[None, :]) for k in range(2)]
    both = (member[0] | member[1]).astype(BF)
    row_id = jnp.arange(row_count, dtype=jnp.int32)
    earlier = (row_id[:, None] > row_id[None, :]).astype(BF)
    before = dot(earlier, both).astype(jnp.int32)
    slot_of = [
        chosen[:, k] * capacity + jnp.sum(jnp.where(member[k], before, 0), axis=1) for k in range(2)
    ]
    block = -(-2 * capacity // 8) * 8
    packed_id = jnp.arange(experts * block, dtype=jnp.int32)
    inner = packed_id % block
    key = jnp.where(
        inner < 2 * capacity,
        (inner // capacity) * slots + (packed_id // block) * capacity + inner % capacity,
        -1,
    )
    column_key = [jnp.concatenate([s, s + slots]) for s in slot_of]
    place = (
        (key[:, None] == column_key[0][None, :]) | (key[:, None] == column_key[1][None, :])
    ).astype(BF)
    dense = (jnp.arange(2 * slots, dtype=jnp.int32)[:, None] == key[None, :]).astype(BF)

    def over_seq(value):
        cols = value.shape[1]
        return lax.all_to_all(
            value.reshape(experts, block, cols), "seq", split_axis=0, concat_axis=0, tiled=True
        ).reshape(experts * block, cols)

    weights = [gate_weight[0], up_weight[0], down_weight[0]]
    swapped = [flip(w, "expert", 2) for w in weights]

    pad_rows = row_count + 2 * half
    pad_scratch = [pltpu.VMEM((pad_rows, width), F32), pltpu.VMEM((pad_rows, LANES), jnp.int32)]
    conv_cost = (6 * kernel_size * row_count * width, 4 << 20)
    conv_out, packed = call(
        conv_body,
        [((row_count, width), BF), ((experts * block, width), BF)],
        pad_scratch + [pltpu.VMEM((2 * row_count, width), BF)],
        *conv_cost,
        smem=2,
    )(bounds, anchor, low, mid, high, cot, conv_weight, place)
    packed, swapped[0] = lax.optimization_barrier((packed, swapped[0]))
    landed, swapped[1], swapped[2] = lax.optimization_barrier((over_seq(packed), swapped[1], swapped[2]))
    weights = weights + swapped
    cot_rows = dot(dense[slots:], landed).astype(BF)
    rows = dot(dense[:slots], landed).astype(BF)

    column = lax.dynamic_slice_in_dim(router_weight, me_seq, 1, axis=1)
    wide = jnp.broadcast_to(column, (width, LANES))
    column_row = column.astype(F32).T
    hid = weights[0].shape[1]
    expert = call(
        expert_body,
        [((slots, width), BF)] * 4 + [((2 * slots, 2 * hid), BF)] * 3 + [((1, width), F32)],
        [pltpu.VMEM((2 * slots, 2 * hid), F32)] * 3 + [pltpu.VMEM((2 * slots, LANES), F32)],
        24 * 2 * slots * width * hid,
        16 << 20,
    )

    def run(rows, cots):
        quad = [rows, cots, flip(rows, "expert", 1), flip(cots, "expert", 1)]
        return quad, list(expert(*quad, *weights, wide, column_row))

    def chip_sum(result, which, total=None):
        value = result[which].astype(F32) + flip(result[which + 2], "expert", 1).astype(F32)
        if total is not None:
            value = value + total.astype(F32)
        return value.astype(BF)

    far_cots = flip(cot_rows, "expert", 4)
    far_rows = flip(rows, "expert", 4)
    quad, near = run(rows, cot_rows)
    far_rows, near[1], near[3] = lax.optimization_barrier((far_rows, near[1], near[3]))
    far_quad, far = run(far_rows, far_cots)
    totals = [chip_sum(far, which) for which in range(2)]
    *totals, far[4], far[5], far[6] = lax.optimization_barrier((*totals, *far[4:7]))
    totals = [flip(total, "expert", 4) for total in totals]
    weight_grads = call(
        grads_body,
        [(w.shape, d) for d in (F32, BF) for w in weights[:3]],
        [],
        48 * 2 * slots * width * hid // 2,
        20 << 20,
    )(*quad, *far_quad, *near[4:7], *far[4:7])
    returned = [flip(w, "expert", 2) for w in weight_grads[3:]]
    *totals, returned[0], returned[1] = lax.optimization_barrier((*totals, returned[0], returned[1]))
    totals = jnp.concatenate([chip_sum(near, which, totals[which]) for which in range(2)], axis=0)
    results = [near, far]

    router_part = sum(r[7] for r in results)
    router_rows = jnp.where(labels[:, None] == me_seq, router_part, 0.0)

    arrived = over_seq(dot(dense, totals, TN).astype(BF))
    block_out, grad_half = call(
        combine_body, [((row_count, width), BF)] * 2, [], 4 * row_count * experts * block * width, 2 << 20
    )(conv_out, cot, place, arrived)
    (taps,) = call(
        taps_body, [((kernel_size, width), F32)], pad_scratch, *conv_cost, smem=2
    )(bounds, anchor, low, mid, high, grad_half)
    taps, grad_half = lax.optimization_barrier((taps, grad_half))
    grad_low, grad_high = halos(grad_half, half)
    peers = lax.axis_size("expert")
    each = kernel_size // peers
    pieces = jnp.concatenate(
        [taps.reshape(peers, each, width), router_rows.reshape(peers, experts // peers, width)], axis=1
    )
    pieces = lax.all_to_all(pieces, "expert", split_axis=0, concat_axis=0, tiled=True)
    pieces, grad_low, grad_high, returned[2] = lax.optimization_barrier(
        (pieces, grad_low, grad_high, returned[2])
    )
    (frame_grad,) = call(
        back_body, [((row_count, width), BF)], pad_scratch, *conv_cost, smem=2
    )(bounds, anchor, grad_low, grad_half, grad_high, conv_weight)
    mine = jnp.sum(pieces, axis=0)
    for bit in (2, 4, 8, 16, 1):
        mine = mine + flip(mine, "seq", bit)
    mine, frame_grad = lax.optimization_barrier((mine, frame_grad))
    gate_grads, up_grads, down_grads = [
        own + far_part.astype(F32) for own, far_part in zip(weight_grads, returned)
    ]
    full = lax.all_to_all(
        jnp.broadcast_to(mine[None], (peers, *mine.shape)), "expert", split_axis=0, concat_axis=0, tiled=True
    )
    conv_grads = full[:, :each].reshape(kernel_size, width)
    router_total = full[:, each:].reshape(experts, width).T

    return (
        block_out[None],
        frame_grad[None],
        conv_grads,
        router_total,
        gate_grads[None],
        up_grads[None],
        down_grads[None],
    )


def solution(mesh):
    in_specs = (
        P("expert", "seq", None),
        P("expert", "seq", None),
        P("expert", "seq", None),
        P("expert", None),
        P(),
        P(),
        P("seq", None, "expert"),
        P("seq", None, "expert"),
        P("seq", "expert", None),
    )
    out_specs = (
        P("expert", "seq", None),
        P("expert", "seq", None),
        P(),
        P(),
        P("seq", None, "expert"),
        P("seq", None, "expert"),
        P("seq", "expert", None),
    )
    return jax.shard_map(shards, mesh=mesh, in_specs=in_specs, out_specs=out_specs, check_vma=False)
```

```python
import functools

import jax
import jax.numpy as jnp
from jax import lax
from jax.experimental import pallas as pl
from jax.experimental.pallas import tpu as pltpu
from jax.sharding import PartitionSpec as P

BF = jnp.bfloat16
F32 = jnp.float32
LANES = 128


def flip(value, axis, bit):
    count = lax.axis_size(axis)
    return lax.ppermute(value, axis, [(i, i ^ bit) for i in range(count)])


def halos(block, width):
    count = lax.axis_size("seq")
    forward = [(i, i + 1) for i in range(count - 1)]
    backward = [(i + 1, i) for i in range(count - 1)]
    low = lax.ppermute(block[block.shape[0] - width :], "seq", forward)
    high = lax.ppermute(block[:width], "seq", backward)
    return low, high


def dot(a, b, dims=((1,), (0,))):
    return lax.dot_general(a, b, (dims, ((), ())), preferred_element_type=F32)


NT = ((1,), (1,))
TN = ((0,), (0,))


def call(body, outs, scratch, flops, moved, smem=0):
    in_vmem = pl.BlockSpec(memory_space=pltpu.VMEM)

    def run(*args):
        specs = [pl.BlockSpec(memory_space=pltpu.SMEM)] * smem + [in_vmem] * (len(args) - smem)
        return pl.pallas_call(
            body,
            out_shape=[jax.ShapeDtypeStruct(*o) for o in outs],
            in_specs=specs,
            out_specs=[in_vmem] * len(outs),
            scratch_shapes=scratch,
            compiler_params=pltpu.CompilerParams(vmem_limit_bytes=32 * 1024 * 1024),
            cost_estimate=pl.CostEstimate(flops=flops, bytes_accessed=moved, transcendentals=0),
        )(*args)

    return run


def expert_body(
    own, own_c, other, other_c, gate_a, up_a, down_a, gate_b, up_b, down_b, wide, column,
    out_own, back_own, out_other, back_other, gate_back, up_back, hidden, router_part,
    gp_ref, up_ref, bb_ref, lg_ref,
):
    slots, width = own.shape
    hid = gate_a.shape[1]
    repeat = 2 * hid // LANES
    sets = ((gate_a, up_a, down_a, pl.ds(0, hid)), (gate_b, up_b, down_b, pl.ds(hid, hid)))
    for k, (src, cot) in enumerate(((own, own_c), (other, other_c))):
        at = pl.ds(k * slots, slots)
        x = src[...]
        for gate_w, up_w, down_w, cols in sets:
            gp_ref[at, cols] = dot(x, gate_w[...])
            up_ref[at, cols] = dot(x, up_w[...])
            bb_ref[at, cols] = dot(cot[...], down_w[...], NT)
        lg_ref[at] = dot(x, wide[...])
    tile = 16

    def step(i, carry):
        at = pl.ds(pl.multiple_of(i * tile, tile), tile)
        gate = jax.nn.sigmoid(lg_ref[at])
        gate_all = jnp.concatenate([gate] * repeat, axis=1)
        gp, up, bb = gp_ref[at], up_ref[at], bb_ref[at]
        sig = jax.nn.sigmoid(gp)
        active = gp * sig
        hid_v = active * up
        terms = hid_v * bb
        row = sum(terms[:, j * LANES : (j + 1) * LANES] for j in range(repeat))
        total = jnp.sum(row, axis=1, keepdims=True)
        lg_ref[at] = total * (gate * (1.0 - gate))
        bh = bb * gate_all
        hidden[at] = (hid_v * gate_all).astype(BF)
        gate_back[at] = (bh * up * (sig * (1.0 + gp * (1.0 - sig)))).astype(BF)
        up_back[at] = (bh * active).astype(BF)
        return carry

    lax.fori_loop(0, 2 * slots // tile, step, 0)
    for k, (out, back) in enumerate(((out_own, back_own), (out_other, back_other))):
        at = pl.ds(k * slots, slots)
        lg_all = jnp.concatenate([lg_ref[at]] * (width // LANES), axis=1)
        forth = 0.0
        both = lg_all * column[...]
        for gate_w, up_w, down_w, cols in sets:
            forth = forth + dot(hidden[at, cols], down_w[...])
            both = both + dot(gate_back[at, cols], gate_w[...], NT) + dot(up_back[at, cols], up_w[...], NT)
        out[...] = forth.astype(BF)
        back[...] = both.astype(BF)
    acc = jnp.zeros((8, width), F32)

    def add(i, acc):
        for k, src in enumerate((own, other)):
            at = pl.ds(pl.multiple_of(i * 16, 16), 16)
            here = pl.ds(pl.multiple_of(k * slots + i * 16, 16), 16)
            lg_all = jnp.concatenate([lg_ref[here]] * (width // LANES), axis=1)
            prod = src[at].astype(F32) * lg_all
            acc = acc + prod[:8] + prod[8:]
        return acc

    acc = lax.fori_loop(0, slots // 16, add, acc)
    router_part[...] = jnp.sum(acc, axis=0, keepdims=True)


def grads_body(part, *refs):
    quads, triples, outs = refs[:8], refs[8:14], refs[14:]
    slots = quads[0].shape[0]
    hid = outs[0].shape[1]
    cols = pl.ds(part * hid, hid)
    gate_out, up_out, down_out = outs
    a = b = d = 0.0
    for n in range(2):
        gate_back, up_back, hidden = triples[3 * n : 3 * n + 3]
        for k in range(2):
            x, c = quads[4 * n + 2 * k : 4 * n + 2 * k + 2]
            at = pl.ds(k * slots, slots)
            a = a + dot(x[...], gate_back[at, cols], TN)
            b = b + dot(x[...], up_back[at, cols], TN)
            d = d + dot(hidden[at, cols], c[...], TN)
    gate_out[...] = a.astype(gate_out.dtype)
    up_out[...] = b.astype(up_out.dtype)
    down_out[...] = d.astype(down_out.dtype)


def stream_ids(bounds, anchor, half, ids_ref):
    place = anchor[0] - half + lax.broadcasted_iota(jnp.int32, ids_ref.shape, 0)
    total = jnp.zeros(ids_ref.shape, jnp.int32)
    edge = jnp.int32(0)
    for s in range(bounds.shape[0]):
        edge = edge + bounds[s]
        total = total + (place >= edge).astype(jnp.int32)
    ids_ref[...] = total


def same_rows(ids_ref, begin, rows, half, copies):
    same = ids_ref[pl.ds(begin, rows)] == ids_ref[pl.ds(half, rows)]
    return jnp.concatenate([same] * copies, axis=1)


def conv_sum(pad_ref, ids_ref, weight, begin0, rows, half, lanes, order):
    taps = weight.shape[0]
    total = jnp.zeros((rows, lanes.size), F32)
    for i in range(taps):
        begin = begin0 + i
        tap = weight[pl.ds(order(i), 1), lanes]
        same = same_rows(ids_ref, begin, rows, half, lanes.size // LANES)
        total = total + tap * jnp.where(same, pad_ref[pl.ds(begin, rows), lanes], 0.0)
    return total


SPAN = 256


def conv_body(bounds, anchor, low, mid, high, cot, weight, place, conv_out, packed, pad_ref, ids_ref, both_ref):
    rows, width = mid.shape
    half = low.shape[0]
    pad_ref[:half] = low[...].astype(F32)
    pad_ref[half : half + rows] = mid[...].astype(F32)
    pad_ref[half + rows :] = high[...].astype(F32)
    stream_ids(bounds, anchor, half, ids_ref)
    for b in range(width // SPAN):
        lanes = pl.ds(b * SPAN, SPAN)
        total = conv_sum(pad_ref, ids_ref, weight, 0, rows, half, lanes, lambda i: i)
        value = (pad_ref[pl.ds(half, rows), lanes] + total).astype(BF)
        conv_out[:, lanes] = value
        both_ref[:rows, lanes] = value
    both_ref[rows:] = cot[...]
    packed[...] = dot(place[...], both_ref[...]).astype(BF)


def combine_body(conv_out, cot, place, arrived, block_out, grad_half):
    rows = cot.shape[0]
    summed = dot(place[...], arrived[...], TN)
    block_out[...] = (conv_out[...].astype(F32) + summed[:rows]).astype(BF)
    grad_half[...] = (cot[...].astype(F32) + summed[rows:]).astype(BF)


def taps_body(bounds, anchor, low, mid, high, grad_half, taps, pad_ref, ids_ref):
    rows, width = mid.shape
    half = low.shape[0]
    pad_ref[:half] = low[...].astype(F32)
    pad_ref[half : half + rows] = mid[...].astype(F32)
    pad_ref[half + rows :] = high[...].astype(F32)
    stream_ids(bounds, anchor, half, ids_ref)
    for b in range(width // SPAN):
        lanes = pl.ds(b * SPAN, SPAN)
        centre = grad_half[:, lanes].astype(F32)
        for j in range(taps.shape[0]):
            same = same_rows(ids_ref, j, rows, half, SPAN // LANES)
            prod = centre * jnp.where(same, pad_ref[pl.ds(j, rows), lanes], 0.0)
            taps[pl.ds(j, 1), lanes] = jnp.sum(prod, axis=0, keepdims=True)


def back_body(bounds, anchor, low, mid, high, weight, frame_grad, pad_ref, ids_ref):
    rows, width = mid.shape
    half = low.shape[0]
    pad_ref[:half] = low[...].astype(F32)
    pad_ref[half : half + rows] = mid[...].astype(F32)
    pad_ref[half + rows :] = high[...].astype(F32)
    stream_ids(bounds, anchor, half, ids_ref)
    taps = weight.shape[0]
    for b in range(width // SPAN):
        lanes = pl.ds(b * SPAN, SPAN)
        total = conv_sum(pad_ref, ids_ref, weight, 1, rows, half, lanes, lambda i: taps - 1 - i)
        frame_grad[:, lanes] = (pad_ref[pl.ds(half, rows), lanes] + total).astype(BF)


def shards(
    frames,
    cotangent,
    routes,
    stream_lengths,
    conv_weight,
    router_weight,
    gate_weight,
    up_weight,
    down_weight,
):
    row_count = frames.shape[1]
    width = frames.shape[2]
    experts = lax.axis_size("seq")
    capacity = 5 * row_count // (2 * experts)
    slots = experts * capacity
    kernel_size = conv_weight.shape[0]
    half = kernel_size // 2
    me_seq = lax.axis_index("seq")
    cot = cotangent[0]
    mid = frames[0]
    low, high = halos(mid, half)
    bounds = stream_lengths[0]
    anchor = (me_seq * row_count)[None].astype(jnp.int32)

    chosen = routes[0]
    labels = jnp.arange(experts, dtype=jnp.int32)
    member = [(chosen[:, k : k + 1] == labels[None, :]) for k in range(2)]
    both = (member[0] | member[1]).astype(BF)
    row_id = jnp.arange(row_count, dtype=jnp.int32)
    earlier = (row_id[:, None] > row_id[None, :]).astype(BF)
    before = dot(earlier, both).astype(jnp.int32)
    slot_of = [
        chosen[:, k] * capacity + jnp.sum(jnp.where(member[k], before, 0), axis=1) for k in range(2)
    ]
    block = -(-2 * capacity // 8) * 8
    packed_id = jnp.arange(experts * block, dtype=jnp.int32)
    inner = packed_id % block
    key = jnp.where(
        inner < 2 * capacity,
        (inner // capacity) * slots + (packed_id // block) * capacity + inner % capacity,
        -1,
    )
    column_key = [jnp.concatenate([s, s + slots]) for s in slot_of]
    place = (
        (key[:, None] == column_key[0][None, :]) | (key[:, None] == column_key[1][None, :])
    ).astype(BF)
    dense = (jnp.arange(2 * slots, dtype=jnp.int32)[:, None] == key[None, :]).astype(BF)

    def over_seq(value):
        cols = value.shape[1]
        return lax.all_to_all(
            value.reshape(experts, block, cols), "seq", split_axis=0, concat_axis=0, tiled=True
        ).reshape(experts * block, cols)

    weights = [gate_weight[0], up_weight[0], down_weight[0]]
    swapped = [flip(weights[0], "expert", 2)]

    pad_rows = row_count + 2 * half
    pad_scratch = [pltpu.VMEM((pad_rows, width), F32), pltpu.VMEM((pad_rows, LANES), jnp.int32)]
    conv_cost = (6 * kernel_size * row_count * width, 4 << 20)
    conv_out, packed = call(
        conv_body,
        [((row_count, width), BF), ((experts * block, width), BF)],
        pad_scratch + [pltpu.VMEM((2 * row_count, width), BF)],
        *conv_cost,
        smem=2,
    )(bounds, anchor, low, mid, high, cot, conv_weight, place)
    packed, swapped[0] = lax.optimization_barrier((packed, swapped[0]))
    landed, *later = lax.optimization_barrier((over_seq(packed), weights[1], weights[2]))
    swapped += [flip(w, "expert", 2) for w in later]
    weights = weights + swapped
    cot_rows = dot(dense[slots:], landed).astype(BF)
    rows = dot(dense[:slots], landed).astype(BF)

    column = lax.dynamic_slice_in_dim(router_weight, me_seq, 1, axis=1)
    wide = jnp.broadcast_to(column, (width, LANES))
    column_row = column.astype(F32).T
    hid = weights[0].shape[1]
    expert = call(
        expert_body,
        [((slots, width), BF)] * 4 + [((2 * slots, 2 * hid), BF)] * 3 + [((1, width), F32)],
        [pltpu.VMEM((2 * slots, 2 * hid), F32)] * 3 + [pltpu.VMEM((2 * slots, LANES), F32)],
        24 * 2 * slots * width * hid,
        16 << 20,
    )

    def run(rows, cots):
        quad = [rows, cots, flip(rows, "expert", 1), flip(cots, "expert", 1)]
        return quad, list(expert(*quad, *weights, wide, column_row))

    def chip_sum(result, which, total=None):
        value = result[which].astype(F32) + flip(result[which + 2], "expert", 1).astype(F32)
        if total is not None:
            value = value + total.astype(F32)
        return value.astype(BF)

    far_rows = flip(rows, "expert", 4)
    far_cots, weights[4] = lax.optimization_barrier((cot_rows, weights[4]))
    far_cots = flip(far_cots, "expert", 4)
    quad, near = run(rows, cot_rows)
    far_rows, near[1], near[3] = lax.optimization_barrier((far_rows, near[1], near[3]))
    far_quad, far = run(far_rows, far_cots)
    totals = [chip_sum(far, which) for which in range(2)]
    *totals, far[4], far[5], far[6] = lax.optimization_barrier((*totals, *far[4:7]))
    totals = [flip(total, "expert", 4) for total in totals]
    saved = [*quad, *far_quad, *near[4:7], *far[4:7]]

    def weight_grads(part, kind):
        return call(
            functools.partial(grads_body, part),
            [(w.shape, kind) for w in weights[:3]],
            [],
            24 * 2 * slots * width * hid // 2,
            14 << 20,
        )(*saved)

    lent = list(weight_grads(1, BF))
    returned = [flip(w, "expert", 2) for w in lent[:2]]
    lent[2], saved[0] = lax.optimization_barrier((lent[2], saved[0]))
    kept = weight_grads(0, F32)
    tied = lax.optimization_barrier((*totals, *returned, *kept))
    totals, returned, kept = list(tied[:2]), list(tied[2:4]), list(tied[4:])
    totals = jnp.concatenate([chip_sum(near, which, totals[which]) for which in range(2)], axis=0)
    results = [near, far]

    router_part = sum(r[7] for r in results)
    router_rows = jnp.where(labels[:, None] == me_seq, router_part, 0.0)

    arrived = over_seq(dot(dense, totals, TN).astype(BF))
    arrived, lent[2] = lax.optimization_barrier((arrived, lent[2]))
    returned.append(flip(lent[2], "expert", 2))
    block_out, grad_half = call(
        combine_body, [((row_count, width), BF)] * 2, [], 4 * row_count * experts * block * width, 2 << 20
    )(conv_out, cot, place, arrived)
    (taps,) = call(
        taps_body, [((kernel_size, width), F32)], pad_scratch, *conv_cost, smem=2
    )(bounds, anchor, low, mid, high, grad_half)
    taps, grad_half = lax.optimization_barrier((taps, grad_half))
    grad_low, grad_high = halos(grad_half, half)
    peers = lax.axis_size("expert")
    each = kernel_size // peers
    pieces = jnp.concatenate(
        [taps.reshape(peers, each, width), router_rows.reshape(peers, experts // peers, width)], axis=1
    )
    pieces = lax.all_to_all(pieces, "expert", split_axis=0, concat_axis=0, tiled=True)
    pieces, grad_low, grad_high = lax.optimization_barrier((pieces, grad_low, grad_high))
    (frame_grad,) = call(
        back_body, [((row_count, width), BF)], pad_scratch, *conv_cost, smem=2
    )(bounds, anchor, grad_low, grad_half, grad_high, conv_weight)
    mine = jnp.sum(pieces, axis=0)
    for bit in (2, 4, 8, 16, 1):
        mine = mine + flip(mine, "seq", bit)
    mine, frame_grad, returned[2] = lax.optimization_barrier((mine, frame_grad, returned[2]))
    gate_grads, up_grads, down_grads = [
        own + far_part.astype(F32) for own, far_part in zip(kept, returned)
    ]
    full = lax.all_to_all(
        jnp.broadcast_to(mine[None], (peers, *mine.shape)), "expert", split_axis=0, concat_axis=0, tiled=True
    )
    conv_grads = full[:, :each].reshape(kernel_size, width)
    router_total = full[:, each:].reshape(experts, width).T

    return (
        block_out[None],
        frame_grad[None],
        conv_grads,
        router_total,
        gate_grads[None],
        up_grads[None],
        down_grads[None],
    )


def solution(mesh):
    in_specs = (
        P("expert", "seq", None),
        P("expert", "seq", None),
        P("expert", "seq", None),
        P("expert", None),
        P(),
        P(),
        P("seq", None, "expert"),
        P("seq", None, "expert"),
        P("seq", "expert", None),
    )
    out_specs = (
        P("expert", "seq", None),
        P("expert", "seq", None),
        P(),
        P(),
        P("seq", None, "expert"),
        P("seq", None, "expert"),
        P("seq", "expert", None),
    )
    return jax.shard_map(shards, mesh=mesh, in_specs=in_specs, out_specs=out_specs, check_vma=False)
```

```python
import functools

import jax
import jax.numpy as jnp
from jax import lax
from jax.experimental import pallas as pl
from jax.experimental.pallas import tpu as pltpu
from jax.sharding import PartitionSpec as P

BF = jnp.bfloat16
F32 = jnp.float32
LANES = 128


def flip(value, axis, bit):
    count = lax.axis_size(axis)
    return lax.ppermute(value, axis, [(i, i ^ bit) for i in range(count)])


def halos(block, width):
    count = lax.axis_size("seq")
    forward = [(i, i + 1) for i in range(count - 1)]
    backward = [(i + 1, i) for i in range(count - 1)]
    low = lax.ppermute(block[block.shape[0] - width :], "seq", forward)
    high = lax.ppermute(block[:width], "seq", backward)
    return low, high


def dot(a, b, dims=((1,), (0,))):
    return lax.dot_general(a, b, (dims, ((), ())), preferred_element_type=F32)


NT = ((1,), (1,))
TN = ((0,), (0,))


def call(body, outs, scratch, flops, moved, smem=0):
    in_vmem = pl.BlockSpec(memory_space=pltpu.VMEM)

    def run(*args):
        specs = [pl.BlockSpec(memory_space=pltpu.SMEM)] * smem + [in_vmem] * (len(args) - smem)
        return pl.pallas_call(
            body,
            out_shape=[jax.ShapeDtypeStruct(*o) for o in outs],
            in_specs=specs,
            out_specs=[in_vmem] * len(outs),
            scratch_shapes=scratch,
            compiler_params=pltpu.CompilerParams(vmem_limit_bytes=32 * 1024 * 1024),
            cost_estimate=pl.CostEstimate(flops=flops, bytes_accessed=moved, transcendentals=0),
        )(*args)

    return run


def expert_body(
    own, own_c, other, other_c, gate_a, up_a, down_a, gate_b, up_b, down_b, wide, column,
    out_own, back_own, out_other, back_other, gate_back, up_back, hidden, router_part,
    gp_ref, up_ref, bb_ref, lg_ref,
):
    slots, width = own.shape
    hid = gate_a.shape[1]
    repeat = 2 * hid // LANES
    sets = ((gate_a, up_a, down_a, pl.ds(0, hid)), (gate_b, up_b, down_b, pl.ds(hid, hid)))
    for k, (src, cot) in enumerate(((own, own_c), (other, other_c))):
        at = pl.ds(k * slots, slots)
        x = src[...]
        for gate_w, up_w, down_w, cols in sets:
            gp_ref[at, cols] = dot(x, gate_w[...])
            up_ref[at, cols] = dot(x, up_w[...])
            bb_ref[at, cols] = dot(cot[...], down_w[...], NT)
        lg_ref[at] = dot(x, wide[...])
    tile = 16

    def step(i, carry):
        at = pl.ds(pl.multiple_of(i * tile, tile), tile)
        gate = jax.nn.sigmoid(lg_ref[at])
        gate_all = jnp.concatenate([gate] * repeat, axis=1)
        gp, up, bb = gp_ref[at], up_ref[at], bb_ref[at]
        sig = jax.nn.sigmoid(gp)
        active = gp * sig
        hid_v = active * up
        terms = hid_v * bb
        row = sum(terms[:, j * LANES : (j + 1) * LANES] for j in range(repeat))
        total = jnp.sum(row, axis=1, keepdims=True)
        lg_ref[at] = total * (gate * (1.0 - gate))
        bh = bb * gate_all
        hidden[at] = (hid_v * gate_all).astype(BF)
        gate_back[at] = (bh * up * (sig * (1.0 + gp * (1.0 - sig)))).astype(BF)
        up_back[at] = (bh * active).astype(BF)
        return carry

    lax.fori_loop(0, 2 * slots // tile, step, 0)
    for k, (out, back) in enumerate(((out_own, back_own), (out_other, back_other))):
        at = pl.ds(k * slots, slots)
        lg_all = jnp.concatenate([lg_ref[at]] * (width // LANES), axis=1)
        forth = 0.0
        both = lg_all * column[...]
        for gate_w, up_w, down_w, cols in sets:
            forth = forth + dot(hidden[at, cols], down_w[...])
            both = both + dot(gate_back[at, cols], gate_w[...], NT) + dot(up_back[at, cols], up_w[...], NT)
        out[...] = forth.astype(BF)
        back[...] = both.astype(BF)
    acc = jnp.zeros((8, width), F32)

    def add(i, acc):
        for k, src in enumerate((own, other)):
            at = pl.ds(pl.multiple_of(i * 16, 16), 16)
            here = pl.ds(pl.multiple_of(k * slots + i * 16, 16), 16)
            lg_all = jnp.concatenate([lg_ref[here]] * (width // LANES), axis=1)
            prod = src[at].astype(F32) * lg_all
            acc = acc + prod[:8] + prod[8:]
        return acc

    acc = lax.fori_loop(0, slots // 16, add, acc)
    router_part[...] = jnp.sum(acc, axis=0, keepdims=True)


def grads_body(part, *refs):
    groups = (len(refs) - 3) // 7
    quads, triples, outs = refs[: 4 * groups], refs[4 * groups : 7 * groups], refs[7 * groups :]
    hid = outs[0].shape[1]
    cols = pl.ds(part * hid, hid)
    gate_out, up_out, down_out = outs
    a = b = d = 0.0
    for n in range(groups):
        gate_back, up_back, hidden = triples[3 * n : 3 * n + 3]
        slots = quads[4 * n].shape[0]
        for k in range(2):
            x, c = quads[4 * n + 2 * k : 4 * n + 2 * k + 2]
            at = pl.ds(k * slots, slots)
            a = a + dot(x[...], gate_back[at, cols], TN)
            b = b + dot(x[...], up_back[at, cols], TN)
            d = d + dot(hidden[at, cols], c[...], TN)
    gate_out[...] = a.astype(gate_out.dtype)
    up_out[...] = b.astype(up_out.dtype)
    down_out[...] = d.astype(down_out.dtype)


def stream_ids(bounds, anchor, half, ids_ref):
    place = anchor[0] - half + lax.broadcasted_iota(jnp.int32, ids_ref.shape, 0)
    total = jnp.zeros(ids_ref.shape, jnp.int32)
    edge = jnp.int32(0)
    for s in range(bounds.shape[0]):
        edge = edge + bounds[s]
        total = total + (place >= edge).astype(jnp.int32)
    ids_ref[...] = total


def same_rows(ids_ref, begin, rows, half, copies):
    same = ids_ref[pl.ds(begin, rows)] == ids_ref[pl.ds(half, rows)]
    return jnp.concatenate([same] * copies, axis=1)


def conv_sum(pad_ref, ids_ref, weight, begin0, rows, half, lanes, order):
    taps = weight.shape[0]
    total = jnp.zeros((rows, lanes.size), F32)
    for i in range(taps):
        begin = begin0 + i
        tap = weight[pl.ds(order(i), 1), lanes]
        same = same_rows(ids_ref, begin, rows, half, lanes.size // LANES)
        total = total + tap * jnp.where(same, pad_ref[pl.ds(begin, rows), lanes], 0.0)
    return total


SPAN = 256


def conv_body(bounds, anchor, low, mid, high, cot, weight, place, conv_out, packed, pad_ref, ids_ref, both_ref):
    rows, width = mid.shape
    half = low.shape[0]
    pad_ref[:half] = low[...].astype(F32)
    pad_ref[half : half + rows] = mid[...].astype(F32)
    pad_ref[half + rows :] = high[...].astype(F32)
    stream_ids(bounds, anchor, half, ids_ref)
    for b in range(width // SPAN):
        lanes = pl.ds(b * SPAN, SPAN)
        total = conv_sum(pad_ref, ids_ref, weight, 0, rows, half, lanes, lambda i: i)
        value = (pad_ref[pl.ds(half, rows), lanes] + total).astype(BF)
        conv_out[:, lanes] = value
        both_ref[:rows, lanes] = value
    both_ref[rows:] = cot[...]
    packed[...] = dot(place[...], both_ref[...]).astype(BF)


def combine_body(conv_out, cot, place, arrived, block_out, grad_half):
    rows = cot.shape[0]
    summed = dot(place[...], arrived[...], TN)
    block_out[...] = (conv_out[...].astype(F32) + summed[:rows]).astype(BF)
    grad_half[...] = (cot[...].astype(F32) + summed[rows:]).astype(BF)


def taps_body(bounds, anchor, low, mid, high, grad_half, taps, pad_ref, ids_ref):
    rows, width = mid.shape
    half = low.shape[0]
    pad_ref[:half] = low[...].astype(F32)
    pad_ref[half : half + rows] = mid[...].astype(F32)
    pad_ref[half + rows :] = high[...].astype(F32)
    stream_ids(bounds, anchor, half, ids_ref)
    for b in range(width // SPAN):
        lanes = pl.ds(b * SPAN, SPAN)
        centre = grad_half[:, lanes].astype(F32)
        for j in range(taps.shape[0]):
            same = same_rows(ids_ref, j, rows, half, SPAN // LANES)
            prod = centre * jnp.where(same, pad_ref[pl.ds(j, rows), lanes], 0.0)
            taps[pl.ds(j, 1), lanes] = jnp.sum(prod, axis=0, keepdims=True)


def back_body(bounds, anchor, low, mid, high, weight, frame_grad, pad_ref, ids_ref):
    rows, width = mid.shape
    half = low.shape[0]
    pad_ref[:half] = low[...].astype(F32)
    pad_ref[half : half + rows] = mid[...].astype(F32)
    pad_ref[half + rows :] = high[...].astype(F32)
    stream_ids(bounds, anchor, half, ids_ref)
    taps = weight.shape[0]
    for b in range(width // SPAN):
        lanes = pl.ds(b * SPAN, SPAN)
        total = conv_sum(pad_ref, ids_ref, weight, 1, rows, half, lanes, lambda i: taps - 1 - i)
        frame_grad[:, lanes] = (pad_ref[pl.ds(half, rows), lanes] + total).astype(BF)


def shards(
    frames,
    cotangent,
    routes,
    stream_lengths,
    conv_weight,
    router_weight,
    gate_weight,
    up_weight,
    down_weight,
):
    row_count = frames.shape[1]
    width = frames.shape[2]
    experts = lax.axis_size("seq")
    capacity = 5 * row_count // (2 * experts)
    slots = experts * capacity
    kernel_size = conv_weight.shape[0]
    half = kernel_size // 2
    me_seq = lax.axis_index("seq")
    cot = cotangent[0]
    mid = frames[0]
    low, high = halos(mid, half)
    bounds = stream_lengths[0]
    anchor = (me_seq * row_count)[None].astype(jnp.int32)

    chosen = routes[0]
    labels = jnp.arange(experts, dtype=jnp.int32)
    member = [(chosen[:, k : k + 1] == labels[None, :]) for k in range(2)]
    both = (member[0] | member[1]).astype(BF)
    row_id = jnp.arange(row_count, dtype=jnp.int32)
    earlier = (row_id[:, None] > row_id[None, :]).astype(BF)
    before = dot(earlier, both).astype(jnp.int32)
    slot_of = [
        chosen[:, k] * capacity + jnp.sum(jnp.where(member[k], before, 0), axis=1) for k in range(2)
    ]
    block = -(-2 * capacity // 8) * 8
    packed_id = jnp.arange(experts * block, dtype=jnp.int32)
    inner = packed_id % block
    key = jnp.where(
        inner < 2 * capacity,
        (inner // capacity) * slots + (packed_id // block) * capacity + inner % capacity,
        -1,
    )
    column_key = [jnp.concatenate([s, s + slots]) for s in slot_of]
    place = (
        (key[:, None] == column_key[0][None, :]) | (key[:, None] == column_key[1][None, :])
    ).astype(BF)
    dense = (jnp.arange(2 * slots, dtype=jnp.int32)[:, None] == key[None, :]).astype(BF)

    def over_seq(value):
        cols = value.shape[1]
        return lax.all_to_all(
            value.reshape(experts, block, cols), "seq", split_axis=0, concat_axis=0, tiled=True
        ).reshape(experts * block, cols)

    weights = [gate_weight[0], up_weight[0], down_weight[0]]
    swapped = [flip(weights[0], "expert", 2)]

    pad_rows = row_count + 2 * half
    pad_scratch = [pltpu.VMEM((pad_rows, width), F32), pltpu.VMEM((pad_rows, LANES), jnp.int32)]
    conv_cost = (6 * kernel_size * row_count * width, 4 << 20)
    conv_out, packed = call(
        conv_body,
        [((row_count, width), BF), ((experts * block, width), BF)],
        pad_scratch + [pltpu.VMEM((2 * row_count, width), BF)],
        *conv_cost,
        smem=2,
    )(bounds, anchor, low, mid, high, cot, conv_weight, place)
    packed, swapped[0] = lax.optimization_barrier((packed, swapped[0]))
    landed, *later = lax.optimization_barrier((over_seq(packed), weights[1], weights[2]))
    swapped += [flip(w, "expert", 2) for w in later]
    weights = weights + swapped
    cot_rows = dot(dense[slots:], landed).astype(BF)
    rows = dot(dense[:slots], landed).astype(BF)

    column = lax.dynamic_slice_in_dim(router_weight, me_seq, 1, axis=1)
    wide = jnp.broadcast_to(column, (width, LANES))
    column_row = column.astype(F32).T
    hid = weights[0].shape[1]
    def run(rows, cots):
        count = rows.shape[0]
        quad = [rows, cots, flip(rows, "expert", 1), flip(cots, "expert", 1)]
        expert = call(
            expert_body,
            [((count, width), BF)] * 4 + [((2 * count, 2 * hid), BF)] * 3 + [((1, width), F32)],
            [pltpu.VMEM((2 * count, 2 * hid), F32)] * 3 + [pltpu.VMEM((2 * count, LANES), F32)],
            24 * 2 * count * width * hid,
            12 << 20,
        )
        return quad, list(expert(*quad, *weights, wide, column_row))

    def chip_sum(result, which, total=None):
        value = result[which].astype(F32) + flip(result[which + 2], "expert", 1).astype(F32)
        if total is not None:
            value = value + total.astype(F32)
        return value.astype(BF)

    def exchange(values):
        return [flip(value, "expert", 4) for value in values]

    middle = slots // 2
    first = exchange([rows[:middle], cot_rows[:middle]])
    *second, weights[4] = lax.optimization_barrier((rows[middle:], cot_rows[middle:], weights[4]))
    second = exchange(second)
    second[0], weights[5] = lax.optimization_barrier((second[0], weights[5]))
    quad_1, far_1 = run(*first)
    sums = [chip_sum(far_1, which) for which in range(2)]
    sent_1 = exchange(sums)
    near_rows, near_cots, second[1], far_1[4] = lax.optimization_barrier(
        (rows, cot_rows, second[1], far_1[4])
    )
    quad, near = run(near_rows, near_cots)
    *second, near[4], sent_1[0], sent_1[1] = lax.optimization_barrier((*second, near[4], *sent_1))
    quad_2, far_2 = run(*second)
    sums = [chip_sum(far_2, which) for which in range(2)]
    *sums, far_2[4], far_2[5], far_2[6] = lax.optimization_barrier((*sums, *far_2[4:7]))
    sent_2 = exchange(sums)
    saved = [*quad, *quad_1, *quad_2, *near[4:7], *far_1[4:7], *far_2[4:7]]

    def weight_grads(part, kind):
        return call(
            functools.partial(grads_body, part),
            [(w.shape, kind) for w in weights[:3]],
            [],
            24 * 2 * slots * width * hid // 2,
            14 << 20,
        )(*saved)

    lent = list(weight_grads(1, BF))
    returned = [flip(w, "expert", 2) for w in lent[:2]]
    lent[2], saved[0] = lax.optimization_barrier((lent[2], saved[0]))
    kept = weight_grads(0, F32)
    tied = lax.optimization_barrier((*sent_1, *sent_2, *returned, *kept))
    totals = [jnp.concatenate([tied[which], tied[which + 2]], axis=0) for which in range(2)]
    returned, kept = list(tied[4:6]), list(tied[6:])
    totals = jnp.concatenate([chip_sum(near, which, totals[which]) for which in range(2)], axis=0)
    results = [near, far_1, far_2]

    router_part = sum(r[7] for r in results)
    router_rows = jnp.where(labels[:, None] == me_seq, router_part, 0.0)

    arrived = over_seq(dot(dense, totals, TN).astype(BF))
    block_out, grad_half = call(
        combine_body, [((row_count, width), BF)] * 2, [], 4 * row_count * experts * block * width, 2 << 20
    )(conv_out, cot, place, arrived)
    (taps,) = call(
        taps_body, [((kernel_size, width), F32)], pad_scratch, *conv_cost, smem=2
    )(bounds, anchor, low, mid, high, grad_half)
    taps, grad_half = lax.optimization_barrier((taps, grad_half))
    grad_low, grad_high = halos(grad_half, half)
    peers = lax.axis_size("expert")
    each = kernel_size // peers
    pieces = jnp.concatenate(
        [taps.reshape(peers, each, width), router_rows.reshape(peers, experts // peers, width)], axis=1
    )
    pieces = lax.all_to_all(pieces, "expert", split_axis=0, concat_axis=0, tiled=True)
    pieces, lent[2] = lax.optimization_barrier((pieces, lent[2]))
    returned.append(flip(lent[2], "expert", 2))
    mine = jnp.sum(pieces, axis=0)
    for bit in (2, 4, 8, 16, 1):
        if bit == 16:
            mine, grad_low, grad_high = lax.optimization_barrier((mine, grad_low, grad_high))
        mine = mine + flip(mine, "seq", bit)
    (frame_grad,) = call(
        back_body, [((row_count, width), BF)], pad_scratch, *conv_cost, smem=2
    )(bounds, anchor, grad_low, grad_half, grad_high, conv_weight)
    mine, frame_grad, returned[2] = lax.optimization_barrier((mine, frame_grad, returned[2]))
    gate_grads, up_grads, down_grads = [
        own + far_part.astype(F32) for own, far_part in zip(kept, returned)
    ]
    full = lax.all_to_all(
        jnp.broadcast_to(mine[None], (peers, *mine.shape)), "expert", split_axis=0, concat_axis=0, tiled=True
    )
    conv_grads = full[:, :each].reshape(kernel_size, width)
    router_total = full[:, each:].reshape(experts, width).T

    return (
        block_out[None],
        frame_grad[None],
        conv_grads,
        router_total,
        gate_grads[None],
        up_grads[None],
        down_grads[None],
    )


def solution(mesh):
    in_specs = (
        P("expert", "seq", None),
        P("expert", "seq", None),
        P("expert", "seq", None),
        P("expert", None),
        P(),
        P(),
        P("seq", None, "expert"),
        P("seq", None, "expert"),
        P("seq", "expert", None),
    )
    out_specs = (
        P("expert", "seq", None),
        P("expert", "seq", None),
        P(),
        P(),
        P("seq", None, "expert"),
        P("seq", None, "expert"),
        P("seq", "expert", None),
    )
    return jax.shard_map(shards, mesh=mesh, in_specs=in_specs, out_specs=out_specs, check_vma=False)
```

```python
import jax
import jax.numpy as jnp
from jax import lax
from jax.experimental import pallas as pl
from jax.experimental.pallas import tpu as pltpu
from jax.sharding import PartitionSpec as P

BF = jnp.bfloat16
F32 = jnp.float32
LANES = 128


def flip(value, axis, bit):
    count = lax.axis_size(axis)
    return lax.ppermute(value, axis, [(i, i ^ bit) for i in range(count)])


def ring_up(value):
    count = lax.axis_size("expert")
    return lax.ppermute(value, "expert", [(i, (i + 2) % count) for i in range(count)])


def halos(block, width):
    count = lax.axis_size("seq")
    forward = [(i, i + 1) for i in range(count - 1)]
    backward = [(i + 1, i) for i in range(count - 1)]
    low = lax.ppermute(block[block.shape[0] - width :], "seq", forward)
    high = lax.ppermute(block[:width], "seq", backward)
    return low, high


def dot(a, b, dims=((1,), (0,))):
    return lax.dot_general(a, b, (dims, ((), ())), preferred_element_type=F32)


NT = ((1,), (1,))
TN = ((0,), (0,))


def call(body, outs, scratch, flops, moved, smem=0):
    in_vmem = pl.BlockSpec(memory_space=pltpu.VMEM)

    def run(*args):
        specs = [pl.BlockSpec(memory_space=pltpu.SMEM)] * smem + [in_vmem] * (len(args) - smem)
        return pl.pallas_call(
            body,
            out_shape=[jax.ShapeDtypeStruct(*o) for o in outs],
            in_specs=specs,
            out_specs=[in_vmem] * len(outs),
            scratch_shapes=scratch,
            compiler_params=pltpu.CompilerParams(vmem_limit_bytes=24 * 1024 * 1024),
            cost_estimate=pl.CostEstimate(flops=flops, bytes_accessed=moved, transcendentals=0),
        )(*args)

    return run


def expert_body(
    own, own_c, other, other_c, gate_w, up_w, down_w, wide, column,
    out_own, back_own, out_other, back_other, gate_back, up_back, hidden, router_part,
    gp_ref, up_ref, bb_ref, lg_ref,
):
    slots = own.shape[0]
    hid = gate_w.shape[1]
    repeat = hid // LANES
    for k, (src, cot) in enumerate(((own, own_c), (other, other_c))):
        at = pl.ds(k * slots, slots)
        x = src[...]
        gp_ref[at] = dot(x, gate_w[...])
        up_ref[at] = dot(x, up_w[...])
        bb_ref[at] = dot(cot[...], down_w[...], NT)
        lg_ref[at] = dot(x, wide[...])
    tile = 32

    def step(i, carry):
        at = pl.ds(pl.multiple_of(i * tile, tile), tile)
        gate = jax.nn.sigmoid(lg_ref[at])
        gate_all = jnp.concatenate([gate] * repeat, axis=1)
        gp, up, bb = gp_ref[at], up_ref[at], bb_ref[at]
        sig = jax.nn.sigmoid(gp)
        active = gp * sig
        hid_v = active * up
        terms = hid_v * bb
        row = sum(terms[:, j * LANES : (j + 1) * LANES] for j in range(repeat))
        total = jnp.sum(row, axis=1, keepdims=True)
        lg_ref[at] = total * (gate * (1.0 - gate))
        bh = bb * gate_all
        hidden[at] = (hid_v * gate_all).astype(BF)
        gate_back[at] = (bh * up * (sig * (1.0 + gp * (1.0 - sig)))).astype(BF)
        up_back[at] = (bh * active).astype(BF)
        return carry

    lax.fori_loop(0, 2 * slots // tile, step, 0)
    width = own.shape[1]
    for k, (src, out, back) in enumerate(((own, out_own, back_own), (other, out_other, back_other))):
        at = pl.ds(k * slots, slots)
        out[...] = dot(hidden[at], down_w[...]).astype(BF)
        lg_all = jnp.concatenate([lg_ref[at]] * (width // LANES), axis=1)
        both = dot(gate_back[at], gate_w[...], NT) + dot(up_back[at], up_w[...], NT)
        back[...] = (both + lg_all * column[...]).astype(BF)
    acc = jnp.zeros((8, width), F32)

    def add(i, acc):
        for k, src in enumerate((own, other)):
            at = pl.ds(pl.multiple_of(i * 16, 16), 16)
            here = pl.ds(pl.multiple_of(k * slots + i * 16, 16), 16)
            lg_all = jnp.concatenate([lg_ref[here]] * (width // LANES), axis=1)
            prod = src[at].astype(F32) * lg_all
            acc = acc + prod[:8] + prod[8:]
        return acc

    acc = lax.fori_loop(0, slots // 16, add, acc)
    router_part[...] = jnp.sum(acc, axis=0, keepdims=True)


def grads_body(*refs):
    quads = refs[:16]
    triples = refs[16:28]
    gate_out, up_out, down_out = refs[28:]
    slots = quads[0].shape[0]
    for n in range(4):
        gate_back, up_back, hidden = triples[3 * n : 3 * n + 3]
        for k in range(2):
            x, c = quads[4 * n + 2 * k : 4 * n + 2 * k + 2]
            at = pl.ds(k * slots, slots)
            first = n == 0 and k == 0
            a = dot(x[...], gate_back[at], TN)
            b = dot(x[...], up_back[at], TN)
            d = dot(hidden[at], c[...], TN)
            gate_out[...] = a if first else gate_out[...] + a
            up_out[...] = b if first else up_out[...] + b
            down_out[...] = d if first else down_out[...] + d


def stream_ids(bounds, anchor, half, ids_ref):
    place = anchor[0] - half + lax.broadcasted_iota(jnp.int32, ids_ref.shape, 0)
    total = jnp.zeros(ids_ref.shape, jnp.int32)
    edge = jnp.int32(0)
    for s in range(bounds.shape[0]):
        edge = edge + bounds[s]
        total = total + (place >= edge).astype(jnp.int32)
    ids_ref[...] = total


def same_rows(ids_ref, begin, rows, half, copies):
    same = ids_ref[pl.ds(begin, rows)] == ids_ref[pl.ds(half, rows)]
    return jnp.concatenate([same] * copies, axis=1)


def conv_sum(pad_ref, ids_ref, weight, begin0, rows, half, lanes, order):
    taps = weight.shape[0]
    total = jnp.zeros((rows, lanes.size), F32)
    for i in range(taps):
        begin = begin0 + i
        tap = weight[pl.ds(order(i), 1), lanes]
        same = same_rows(ids_ref, begin, rows, half, lanes.size // LANES)
        total = total + tap * jnp.where(same, pad_ref[pl.ds(begin, rows), lanes], 0.0)
    return total


SPAN = 256


def conv_body(bounds, anchor, low, mid, high, weight, place, conv_out, packed, pad_ref, ids_ref, both_ref):
    rows, width = mid.shape
    part = width // 2
    half = low.shape[0]
    pad_ref[:half] = low[...].astype(F32)
    pad_ref[half : half + rows] = mid[...].astype(F32)
    pad_ref[half + rows :] = high[...].astype(F32)
    stream_ids(bounds, anchor, half, ids_ref)
    for b in range(width // SPAN):
        lanes = pl.ds(b * SPAN, SPAN)
        total = conv_sum(pad_ref, ids_ref, weight, 0, rows, half, lanes, lambda i: i)
        value = (pad_ref[pl.ds(half, rows), lanes] + total).astype(BF)
        conv_out[:, lanes] = value
    both_ref[:rows] = conv_out[:, :part]
    both_ref[rows:] = conv_out[:, part:]
    packed[...] = dot(place[...], both_ref[...]).astype(BF)


def combine_body(cot, place, arrived, grad_half):
    rows, width = cot.shape
    summed = dot(place[...], arrived[...], TN)
    part = width // 2
    for h in range(2):
        lanes = pl.ds(h * part, part)
        grad_half[:, lanes] = (cot[:, lanes].astype(F32) + summed[h * rows : (h + 1) * rows]).astype(BF)


def taps_body(bounds, anchor, low, mid, high, grad_half, taps, pad_ref, ids_ref):
    rows, width = mid.shape
    half = low.shape[0]
    pad_ref[:half] = low[...].astype(F32)
    pad_ref[half : half + rows] = mid[...].astype(F32)
    pad_ref[half + rows :] = high[...].astype(F32)
    stream_ids(bounds, anchor, half, ids_ref)
    for b in range(width // SPAN):
        lanes = pl.ds(b * SPAN, SPAN)
        centre = grad_half[:, lanes].astype(F32)
        for j in range(taps.shape[0]):
            same = same_rows(ids_ref, j, rows, half, SPAN // LANES)
            prod = centre * jnp.where(same, pad_ref[pl.ds(j, rows), lanes], 0.0)
            taps[pl.ds(j, 1), lanes] = jnp.sum(prod, axis=0, keepdims=True)


def back_body(bounds, anchor, low, mid, high, weight, frame_grad, pad_ref, ids_ref):
    rows, width = mid.shape
    half = low.shape[0]
    pad_ref[:half] = low[...].astype(F32)
    pad_ref[half : half + rows] = mid[...].astype(F32)
    pad_ref[half + rows :] = high[...].astype(F32)
    stream_ids(bounds, anchor, half, ids_ref)
    taps = weight.shape[0]
    for b in range(width // SPAN):
        lanes = pl.ds(b * SPAN, SPAN)
        total = conv_sum(pad_ref, ids_ref, weight, 1, rows, half, lanes, lambda i: taps - 1 - i)
        frame_grad[:, lanes] = (pad_ref[pl.ds(half, rows), lanes] + total).astype(BF)


def shards(
    frames,
    cotangent,
    routes,
    stream_lengths,
    conv_weight,
    router_weight,
    gate_weight,
    up_weight,
    down_weight,
):
    row_count = frames.shape[1]
    width = frames.shape[2]
    part = width // 2
    experts = lax.axis_size("seq")
    capacity = 5 * row_count // (2 * experts)
    slots = experts * capacity
    kernel_size = conv_weight.shape[0]
    half = kernel_size // 2
    me_seq = lax.axis_index("seq")
    cot = cotangent[0]
    mid = frames[0]
    low, high = halos(mid, half)
    bounds = stream_lengths[0]
    anchor = (me_seq * row_count)[None].astype(jnp.int32)

    chosen = routes[0]
    labels = jnp.arange(experts, dtype=jnp.int32)
    member = [(chosen[:, k : k + 1] == labels[None, :]) for k in range(2)]
    both = (member[0] | member[1]).astype(BF)
    row_id = jnp.arange(row_count, dtype=jnp.int32)
    earlier = (row_id[:, None] > row_id[None, :]).astype(BF)
    before = dot(earlier, both).astype(jnp.int32)
    slot_of = [
        chosen[:, k] * capacity + jnp.sum(jnp.where(member[k], before, 0), axis=1) for k in range(2)
    ]
    block = -(-2 * capacity // 8) * 8
    packed_id = jnp.arange(experts * block, dtype=jnp.int32)
    inner = packed_id % block
    key = jnp.where(
        inner < 2 * capacity,
        (inner // capacity) * slots + (packed_id // block) * capacity + inner % capacity,
        -1,
    )
    column_key = [jnp.concatenate([s, s + slots]) for s in slot_of]
    place = (
        (key[:, None] == column_key[0][None, :]) | (key[:, None] == column_key[1][None, :])
    ).astype(BF)
    dense = (jnp.arange(2 * slots, dtype=jnp.int32)[:, None] == key[None, :]).astype(BF)

    def over_seq(value):
        cols = value.shape[1]
        return lax.all_to_all(
            value.reshape(experts, block, cols), "seq", split_axis=0, concat_axis=0, tiled=True
        ).reshape(experts * block, cols)

    def halves(value):
        return jnp.concatenate([value[:, :part], value[:, part:]], axis=0)

    def unpack(packed):
        return jnp.concatenate(
            [dot(dense[:slots], packed).astype(BF), dot(dense[slots:], packed).astype(BF)], axis=1
        )

    cot_arrived = over_seq(dot(place, halves(cot)).astype(BF))

    pad_rows = row_count + 2 * half
    pad_scratch = [pltpu.VMEM((pad_rows, width), F32), pltpu.VMEM((pad_rows, LANES), jnp.int32)]
    conv_cost = (6 * kernel_size * row_count * width, 4 << 20)
    conv_out, packed = call(
        conv_body,
        [((row_count, width), BF), ((experts * block, part), BF)],
        pad_scratch + [pltpu.VMEM((2 * row_count, part), BF)],
        *conv_cost,
        smem=2,
    )(bounds, anchor, low, mid, high, conv_weight, place)
    cot_rows, packed = lax.optimization_barrier((unpack(cot_arrived), packed))
    rows = unpack(over_seq(packed))

    gate_block, up_block, down_block = gate_weight[0], up_weight[0], down_weight[0]
    column = lax.dynamic_slice_in_dim(router_weight, me_seq, 1, axis=1)
    wide = jnp.broadcast_to(column, (width, LANES))
    column_row = column.astype(F32).T
    hid = gate_block.shape[1]
    expert = call(
        expert_body,
        [((slots, width), BF)] * 4 + [((2 * slots, hid), BF)] * 3 + [((1, width), F32)],
        [pltpu.VMEM((2 * slots, hid), F32)] * 3 + [pltpu.VMEM((2 * slots, LANES), F32)],
        12 * 2 * slots * width * hid,
        12 << 20,
    )

    steps = lax.axis_size("expert") // 2
    results = []

    def chip_sum(step, which, total):
        own, away = results[step][which], results[step][which + 2]
        value = own.astype(F32) + flip(away, "expert", 1).astype(F32)
        if total is not None:
            value = value + total.astype(F32)
        return value.astype(BF)

    cots = [cot_rows, ring_up(cot_rows)]
    cots.append(ring_up(cots[1]))
    rows, cots[2] = lax.optimization_barrier((rows, cots[2]))
    xs = [rows]
    quads = []

    def run(step):
        quad = [xs[step], cots[step], flip(xs[step], "expert", 1), flip(cots[step], "expert", 1)]
        results.append(list(expert(*quad, gate_block, up_block, down_block, wide, column_row)))
        quads.extend(quad)

    total_back = None
    upcoming = ring_up(rows)
    cots.append(ring_up(cots[2]))
    run(0)
    for step in range(1, steps):
        tied = [upcoming, results[step - 1][1], results[step - 1][3]]
        if step == 2:
            tied.append(cots[3])
        if total_back is not None:
            tied.append(total_back)
        tied = list(lax.optimization_barrier(tied))
        upcoming, results[step - 1][1], results[step - 1][3] = tied[:3]
        if step == 2:
            cots[3] = tied[3]
        if total_back is not None:
            total_back = tied[-1]
        xs.append(upcoming)
        if step < steps - 1:
            upcoming = ring_up(upcoming)
        if step > 1:
            total_back = ring_up(chip_sum(step - 1, 1, total_back))
        run(step)
    total_back = ring_up(chip_sum(steps - 1, 1, total_back))

    weight_grads = call(
        grads_body,
        [((width, hid), F32), ((width, hid), F32), ((hid, width), F32)],
        [],
        6 * 8 * slots * width * hid,
        16 << 20,
    )(*quads, *[r[i] for r in results for i in (4, 5, 6)])
    total_back, results[1][0], *weight_grads = lax.optimization_barrier(
        (total_back, results[1][0], *weight_grads)
    )
    gate_grads, up_grads, down_grads = weight_grads
    total_back = chip_sum(0, 1, total_back)
    router_part = sum(r[7] for r in results)

    def pack_back(total):
        return over_seq(dot(dense, halves(total), TN).astype(BF))

    arrived = pack_back(total_back)
    total_out = ring_up(chip_sum(1, 0, None))
    total_out = ring_up(chip_sum(2, 0, total_out))
    arrived, total_out = lax.optimization_barrier((arrived, total_out))
    total_out = ring_up(chip_sum(3, 0, total_out))
    (grad_half,) = call(
        combine_body, [((row_count, width), BF)], [], 4 * row_count * experts * block * part, 2 << 20
    )(cot, place, arrived)
    (taps,) = call(
        taps_body, [((kernel_size, width), F32)], pad_scratch, *conv_cost, smem=2
    )(bounds, anchor, low, mid, high, grad_half)
    taps, grad_half = lax.optimization_barrier((taps, grad_half))
    grad_low, grad_high = halos(grad_half, half)
    core = lax.axis_index("expert") & 1
    split = kernel_size // 2

    def half_of(which):
        columns = jnp.arange(experts // 2, dtype=jnp.int32)[:, None] + which * (experts // 2)
        return jnp.concatenate(
            [
                lax.dynamic_slice_in_dim(taps, which * split, split, axis=0),
                jnp.where(columns == me_seq, router_part, 0.0),
            ],
            axis=0,
        )

    sums = half_of(core) + flip(half_of(1 - core), "expert", 1)
    (frame_grad,) = call(
        back_body, [((row_count, width), BF)], pad_scratch, *conv_cost, smem=2
    )(bounds, anchor, grad_low, grad_half, grad_high, conv_weight)
    for axis, bit in (("seq", 2), ("seq", 4), ("seq", 8), ("seq", 16), ("expert", 2), ("expert", 4), ("seq", 1)):
        if bit == 8:
            sums, total_out = lax.optimization_barrier((sums, total_out))
            out_arrived = pack_back(chip_sum(0, 0, total_out))
        if bit == 1:
            sums, frame_grad = lax.optimization_barrier((sums, frame_grad))
        sums = sums + flip(sums, axis, bit)
    sums, out_arrived = lax.optimization_barrier((sums, out_arrived))
    got = flip(sums, "expert", 1)
    low_half, high_half = jnp.where(core == 0, sums, got), jnp.where(core == 0, got, sums)
    conv_grads = jnp.concatenate([low_half[:split], high_half[:split]], axis=0)
    router_total = jnp.concatenate([low_half[split:], high_half[split:]], axis=0).T

    summed = dot(place, out_arrived, TN)
    out_sum = jnp.concatenate([summed[:row_count], summed[row_count:]], axis=1)
    block_out = (conv_out.astype(F32) + out_sum).astype(BF)
    return (
        block_out[None],
        frame_grad[None],
        conv_grads,
        router_total,
        gate_grads[None],
        up_grads[None],
        down_grads[None],
    )


def solution(mesh):
    in_specs = (
        P("expert", "seq", None),
        P("expert", "seq", None),
        P("expert", "seq", None),
        P("expert", None),
        P(),
        P(),
        P("seq", None, "expert"),
        P("seq", None, "expert"),
        P("seq", "expert", None),
    )
    out_specs = (
        P("expert", "seq", None),
        P("expert", "seq", None),
        P(),
        P(),
        P("seq", None, "expert"),
        P("seq", None, "expert"),
        P("seq", "expert", None),
    )
    return jax.shard_map(shards, mesh=mesh, in_specs=in_specs, out_specs=out_specs, check_vma=False)
```

```python
import jax
import jax.numpy as jnp
from jax import lax
from jax.experimental import pallas as pl
from jax.experimental.pallas import tpu as pltpu
from jax.sharding import PartitionSpec as P

BF = jnp.bfloat16
F32 = jnp.float32
LANES = 128


def flip(value, axis, bit):
    count = lax.axis_size(axis)
    return lax.ppermute(value, axis, [(i, i ^ bit) for i in range(count)])


def ring_up(value):
    count = lax.axis_size("expert")
    return lax.ppermute(value, "expert", [(i, (i + 2) % count) for i in range(count)])


def halos(block, width):
    count = lax.axis_size("seq")
    forward = [(i, i + 1) for i in range(count - 1)]
    backward = [(i + 1, i) for i in range(count - 1)]
    low = lax.ppermute(block[block.shape[0] - width :], "seq", forward)
    high = lax.ppermute(block[:width], "seq", backward)
    return low, high


def dot(a, b, dims=((1,), (0,))):
    return lax.dot_general(a, b, (dims, ((), ())), preferred_element_type=F32)


NT = ((1,), (1,))
TN = ((0,), (0,))


def call(body, outs, scratch, flops, moved, smem=0):
    in_vmem = pl.BlockSpec(memory_space=pltpu.VMEM)

    def run(*args):
        specs = [pl.BlockSpec(memory_space=pltpu.SMEM)] * smem + [in_vmem] * (len(args) - smem)
        return pl.pallas_call(
            body,
            out_shape=[jax.ShapeDtypeStruct(*o) for o in outs],
            in_specs=specs,
            out_specs=[in_vmem] * len(outs),
            scratch_shapes=scratch,
            compiler_params=pltpu.CompilerParams(vmem_limit_bytes=24 * 1024 * 1024),
            cost_estimate=pl.CostEstimate(flops=flops, bytes_accessed=moved, transcendentals=0),
        )(*args)

    return run


def expert_body(
    own, own_c, other, other_c, gate_w, up_w, down_w, wide, column,
    out_own, back_own, out_other, back_other, gate_back, up_back, hidden, router_part,
    gp_ref, up_ref, bb_ref, lg_ref,
):
    slots = own.shape[0]
    hid = gate_w.shape[1]
    repeat = hid // LANES
    for k, (src, cot) in enumerate(((own, own_c), (other, other_c))):
        at = pl.ds(k * slots, slots)
        x = src[...]
        gp_ref[at] = dot(x, gate_w[...])
        up_ref[at] = dot(x, up_w[...])
        bb_ref[at] = dot(cot[...], down_w[...], NT)
        lg_ref[at] = dot(x, wide[...])
    tile = 32

    def step(i, carry):
        at = pl.ds(pl.multiple_of(i * tile, tile), tile)
        gate = jax.nn.sigmoid(lg_ref[at])
        gate_all = jnp.concatenate([gate] * repeat, axis=1)
        gp, up, bb = gp_ref[at], up_ref[at], bb_ref[at]
        sig = jax.nn.sigmoid(gp)
        active = gp * sig
        hid_v = active * up
        terms = hid_v * bb
        row = sum(terms[:, j * LANES : (j + 1) * LANES] for j in range(repeat))
        total = jnp.sum(row, axis=1, keepdims=True)
        lg_ref[at] = total * (gate * (1.0 - gate))
        bh = bb * gate_all
        hidden[at] = (hid_v * gate_all).astype(BF)
        gate_back[at] = (bh * up * (sig * (1.0 + gp * (1.0 - sig)))).astype(BF)
        up_back[at] = (bh * active).astype(BF)
        return carry

    lax.fori_loop(0, 2 * slots // tile, step, 0)
    width = own.shape[1]
    for k, (src, out, back) in enumerate(((own, out_own, back_own), (other, out_other, back_other))):
        at = pl.ds(k * slots, slots)
        out[...] = dot(hidden[at], down_w[...]).astype(BF)
        lg_all = jnp.concatenate([lg_ref[at]] * (width // LANES), axis=1)
        both = dot(gate_back[at], gate_w[...], NT) + dot(up_back[at], up_w[...], NT)
        back[...] = (both + lg_all * column[...]).astype(BF)
    acc = jnp.zeros((8, width), F32)

    def add(i, acc):
        for k, src in enumerate((own, other)):
            at = pl.ds(pl.multiple_of(i * 16, 16), 16)
            here = pl.ds(pl.multiple_of(k * slots + i * 16, 16), 16)
            lg_all = jnp.concatenate([lg_ref[here]] * (width // LANES), axis=1)
            prod = src[at].astype(F32) * lg_all
            acc = acc + prod[:8] + prod[8:]
        return acc

    acc = lax.fori_loop(0, slots // 16, add, acc)
    router_part[...] = jnp.sum(acc, axis=0, keepdims=True)


def grads_body(*refs):
    quads = refs[:16]
    triples = refs[16:28]
    gate_out, up_out, down_out = refs[28:]
    slots = quads[0].shape[0]
    for n in range(4):
        gate_back, up_back, hidden = triples[3 * n : 3 * n + 3]
        for k in range(2):
            x, c = quads[4 * n + 2 * k : 4 * n + 2 * k + 2]
            at = pl.ds(k * slots, slots)
            first = n == 0 and k == 0
            a = dot(x[...], gate_back[at], TN)
            b = dot(x[...], up_back[at], TN)
            d = dot(hidden[at], c[...], TN)
            gate_out[...] = a if first else gate_out[...] + a
            up_out[...] = b if first else up_out[...] + b
            down_out[...] = d if first else down_out[...] + d


def stream_ids(bounds, anchor, half, ids_ref):
    place = anchor[0] - half + lax.broadcasted_iota(jnp.int32, ids_ref.shape, 0)
    total = jnp.zeros(ids_ref.shape, jnp.int32)
    edge = jnp.int32(0)
    for s in range(bounds.shape[0]):
        edge = edge + bounds[s]
        total = total + (place >= edge).astype(jnp.int32)
    ids_ref[...] = total


def same_rows(ids_ref, begin, rows, half, copies):
    same = ids_ref[pl.ds(begin, rows)] == ids_ref[pl.ds(half, rows)]
    return jnp.concatenate([same] * copies, axis=1)


def conv_sum(pad_ref, ids_ref, weight, begin0, rows, half, lanes, order):
    taps = weight.shape[0]
    total = jnp.zeros((rows, lanes.size), F32)
    for i in range(taps):
        begin = begin0 + i
        tap = weight[pl.ds(order(i), 1), lanes]
        same = same_rows(ids_ref, begin, rows, half, lanes.size // LANES)
        total = total + tap * jnp.where(same, pad_ref[pl.ds(begin, rows), lanes], 0.0)
    return total


SPAN = 256


def conv_body(bounds, anchor, low, mid, high, weight, place, conv_out, packed, pad_ref, ids_ref, both_ref):
    rows, width = mid.shape
    part = width // 2
    half = low.shape[0]
    pad_ref[:half] = low[...].astype(F32)
    pad_ref[half : half + rows] = mid[...].astype(F32)
    pad_ref[half + rows :] = high[...].astype(F32)
    stream_ids(bounds, anchor, half, ids_ref)
    for b in range(width // SPAN):
        lanes = pl.ds(b * SPAN, SPAN)
        total = conv_sum(pad_ref, ids_ref, weight, 0, rows, half, lanes, lambda i: i)
        value = (pad_ref[pl.ds(half, rows), lanes] + total).astype(BF)
        conv_out[:, lanes] = value
    both_ref[:rows] = conv_out[:, :part]
    both_ref[rows:] = conv_out[:, part:]
    packed[...] = dot(place[...], both_ref[...]).astype(BF)


def combine_body(cot, place, arrived, grad_half):
    rows, width = cot.shape
    summed = dot(place[...], arrived[...], TN)
    part = width // 2
    for h in range(2):
        lanes = pl.ds(h * part, part)
        grad_half[:, lanes] = (cot[:, lanes].astype(F32) + summed[h * rows : (h + 1) * rows]).astype(BF)


def taps_body(bounds, anchor, low, mid, high, grad_half, taps, pad_ref, ids_ref):
    rows, width = mid.shape
    half = low.shape[0]
    pad_ref[:half] = low[...].astype(F32)
    pad_ref[half : half + rows] = mid[...].astype(F32)
    pad_ref[half + rows :] = high[...].astype(F32)
    stream_ids(bounds, anchor, half, ids_ref)
    for b in range(width // SPAN):
        lanes = pl.ds(b * SPAN, SPAN)
        centre = grad_half[:, lanes].astype(F32)
        for j in range(taps.shape[0]):
            same = same_rows(ids_ref, j, rows, half, SPAN // LANES)
            prod = centre * jnp.where(same, pad_ref[pl.ds(j, rows), lanes], 0.0)
            taps[pl.ds(j, 1), lanes] = jnp.sum(prod, axis=0, keepdims=True)


def back_body(bounds, anchor, low, mid, high, weight, frame_grad, pad_ref, ids_ref):
    rows, width = mid.shape
    half = low.shape[0]
    pad_ref[:half] = low[...].astype(F32)
    pad_ref[half : half + rows] = mid[...].astype(F32)
    pad_ref[half + rows :] = high[...].astype(F32)
    stream_ids(bounds, anchor, half, ids_ref)
    taps = weight.shape[0]
    for b in range(width // SPAN):
        lanes = pl.ds(b * SPAN, SPAN)
        total = conv_sum(pad_ref, ids_ref, weight, 1, rows, half, lanes, lambda i: taps - 1 - i)
        frame_grad[:, lanes] = (pad_ref[pl.ds(half, rows), lanes] + total).astype(BF)


def shards(
    frames,
    cotangent,
    routes,
    stream_lengths,
    conv_weight,
    router_weight,
    gate_weight,
    up_weight,
    down_weight,
):
    row_count = frames.shape[1]
    width = frames.shape[2]
    part = width // 2
    experts = lax.axis_size("seq")
    capacity = 5 * row_count // (2 * experts)
    slots = experts * capacity
    kernel_size = conv_weight.shape[0]
    half = kernel_size // 2
    me_seq = lax.axis_index("seq")
    cot = cotangent[0]
    mid = frames[0]
    low, high = halos(mid, half)
    bounds = stream_lengths[0]
    anchor = (me_seq * row_count)[None].astype(jnp.int32)

    chosen = routes[0]
    labels = jnp.arange(experts, dtype=jnp.int32)
    member = [(chosen[:, k : k + 1] == labels[None, :]) for k in range(2)]
    both = (member[0] | member[1]).astype(BF)
    row_id = jnp.arange(row_count, dtype=jnp.int32)
    earlier = (row_id[:, None] > row_id[None, :]).astype(BF)
    before = dot(earlier, both).astype(jnp.int32)
    slot_of = [
        chosen[:, k] * capacity + jnp.sum(jnp.where(member[k], before, 0), axis=1) for k in range(2)
    ]
    block = -(-2 * capacity // 8) * 8
    packed_id = jnp.arange(experts * block, dtype=jnp.int32)
    inner = packed_id % block
    key = jnp.where(
        inner < 2 * capacity,
        (inner // capacity) * slots + (packed_id // block) * capacity + inner % capacity,
        -1,
    )
    column_key = [jnp.concatenate([s, s + slots]) for s in slot_of]
    place = (
        (key[:, None] == column_key[0][None, :]) | (key[:, None] == column_key[1][None, :])
    ).astype(BF)
    dense = (jnp.arange(2 * slots, dtype=jnp.int32)[:, None] == key[None, :]).astype(BF)

    def over_seq(value):
        cols = value.shape[1]
        return lax.all_to_all(
            value.reshape(experts, block, cols), "seq", split_axis=0, concat_axis=0, tiled=True
        ).reshape(experts * block, cols)

    def halves(value):
        return jnp.concatenate([value[:, :part], value[:, part:]], axis=0)

    def unpack(packed):
        return jnp.concatenate(
            [dot(dense[:slots], packed).astype(BF), dot(dense[slots:], packed).astype(BF)], axis=1
        )

    cot_arrived = over_seq(dot(place, halves(cot)).astype(BF))

    pad_rows = row_count + 2 * half
    pad_scratch = [pltpu.VMEM((pad_rows, width), F32), pltpu.VMEM((pad_rows, LANES), jnp.int32)]
    conv_cost = (6 * kernel_size * row_count * width, 4 << 20)
    conv_out, packed = call(
        conv_body,
        [((row_count, width), BF), ((experts * block, part), BF)],
        pad_scratch + [pltpu.VMEM((2 * row_count, part), BF)],
        *conv_cost,
        smem=2,
    )(bounds, anchor, low, mid, high, conv_weight, place)
    cot_rows, packed = lax.optimization_barrier((unpack(cot_arrived), packed))
    rows = unpack(over_seq(packed))

    gate_block, up_block, down_block = gate_weight[0], up_weight[0], down_weight[0]
    column = lax.dynamic_slice_in_dim(router_weight, me_seq, 1, axis=1)
    wide = jnp.broadcast_to(column, (width, LANES))
    column_row = column.astype(F32).T
    hid = gate_block.shape[1]
    expert = call(
        expert_body,
        [((slots, width), BF)] * 4 + [((2 * slots, hid), BF)] * 3 + [((1, width), F32)],
        [pltpu.VMEM((2 * slots, hid), F32)] * 3 + [pltpu.VMEM((2 * slots, LANES), F32)],
        12 * 2 * slots * width * hid,
        12 << 20,
    )

    steps = lax.axis_size("expert") // 2
    results = []

    def chip_sum(step, which, total):
        own, away = results[step][which], results[step][which + 2]
        value = own.astype(F32) + flip(away, "expert", 1).astype(F32)
        if total is not None:
            value = value + total.astype(F32)
        return value.astype(BF)

    cots = [cot_rows, ring_up(cot_rows)]
    cots.append(ring_up(cots[1]))
    rows, cots[2] = lax.optimization_barrier((rows, cots[2]))
    xs = [rows]
    quads = []

    def run(step):
        quad = [xs[step], cots[step], flip(xs[step], "expert", 1), flip(cots[step], "expert", 1)]
        results.append(list(expert(*quad, gate_block, up_block, down_block, wide, column_row)))
        quads.extend(quad)

    total_back = None
    upcoming = ring_up(rows)
    cots.append(ring_up(cots[2]))
    run(0)
    for step in range(1, steps):
        tied = [upcoming, results[step - 1][1], results[step - 1][3]]
        if step == 2:
            tied.append(cots[3])
        if total_back is not None:
            tied.append(total_back)
        tied = list(lax.optimization_barrier(tied))
        upcoming, results[step - 1][1], results[step - 1][3] = tied[:3]
        if step == 2:
            cots[3] = tied[3]
        if total_back is not None:
            total_back = tied[-1]
        xs.append(upcoming)
        if step < steps - 1:
            upcoming = ring_up(upcoming)
        if step > 1:
            total_back = ring_up(chip_sum(step - 1, 1, total_back))
        run(step)
    total_back = ring_up(chip_sum(steps - 1, 1, total_back))

    weight_grads = call(
        grads_body,
        [((width, hid), F32), ((width, hid), F32), ((hid, width), F32)],
        [],
        6 * 8 * slots * width * hid,
        16 << 20,
    )(*quads, *[r[i] for r in results for i in (4, 5, 6)])
    total_back, results[1][0], *weight_grads = lax.optimization_barrier(
        (total_back, results[1][0], *weight_grads)
    )
    gate_grads, up_grads, down_grads = weight_grads
    total_back = chip_sum(0, 1, total_back)
    router_part = sum(r[7] for r in results)
    router_rows = jnp.where(labels[:, None] == me_seq, router_part, 0.0)

    def pack_back(total):
        return over_seq(dot(dense, halves(total), TN).astype(BF))

    arrived = pack_back(total_back)
    total_out = ring_up(chip_sum(1, 0, None))
    arrived, total_out = lax.optimization_barrier((arrived, total_out))
    total_out = ring_up(chip_sum(2, 0, total_out))
    total_out = ring_up(chip_sum(3, 0, total_out))
    (grad_half,) = call(
        combine_body, [((row_count, width), BF)], [], 4 * row_count * experts * block * part, 2 << 20
    )(cot, place, arrived)
    (taps,) = call(
        taps_body, [((kernel_size, width), F32)], pad_scratch, *conv_cost, smem=2
    )(bounds, anchor, low, mid, high, grad_half)
    taps, grad_half = lax.optimization_barrier((taps, grad_half))
    grad_low, grad_high = halos(grad_half, half)
    peers = lax.axis_size("expert")
    each = kernel_size // peers
    pieces = jnp.concatenate(
        [taps.reshape(peers, each, width), router_rows.reshape(peers, experts // peers, width)], axis=1
    )
    pieces = lax.all_to_all(pieces, "expert", split_axis=0, concat_axis=0, tiled=True)
    pieces, grad_low, grad_high, total_out = lax.optimization_barrier(
        (pieces, grad_low, grad_high, total_out)
    )
    out_arrived = pack_back(chip_sum(0, 0, total_out))
    (frame_grad,) = call(
        back_body, [((row_count, width), BF)], pad_scratch, *conv_cost, smem=2
    )(bounds, anchor, grad_low, grad_half, grad_high, conv_weight)
    mine = jnp.sum(pieces, axis=0)
    for bit in (2, 4, 8, 16, 1):
        mine = mine + flip(mine, "seq", bit)
    mine, out_arrived, frame_grad = lax.optimization_barrier((mine, out_arrived, frame_grad))
    full = lax.all_to_all(
        jnp.broadcast_to(mine[None], (peers, *mine.shape)), "expert", split_axis=0, concat_axis=0, tiled=True
    )
    conv_grads = full[:, :each].reshape(kernel_size, width)
    router_total = full[:, each:].reshape(experts, width).T

    summed = dot(place, out_arrived, TN)
    out_sum = jnp.concatenate([summed[:row_count], summed[row_count:]], axis=1)
    block_out = (conv_out.astype(F32) + out_sum).astype(BF)
    return (
        block_out[None],
        frame_grad[None],
        conv_grads,
        router_total,
        gate_grads[None],
        up_grads[None],
        down_grads[None],
    )


def solution(mesh):
    in_specs = (
        P("expert", "seq", None),
        P("expert", "seq", None),
        P("expert", "seq", None),
        P("expert", None),
        P(),
        P(),
        P("seq", None, "expert"),
        P("seq", None, "expert"),
        P("seq", "expert", None),
    )
    out_specs = (
        P("expert", "seq", None),
        P("expert", "seq", None),
        P(),
        P(),
        P("seq", None, "expert"),
        P("seq", None, "expert"),
        P("seq", "expert", None),
    )
    return jax.shard_map(shards, mesh=mesh, in_specs=in_specs, out_specs=out_specs, check_vma=False)
```
